128 devices in a mesh: section: 2 (over y_hi), dp: 16 (over x, y_lo, core), expert: 4 (over z).
Axes of the slice: x: 4, y: 4 (y_hi: 2, y_lo: 2; y = y_hi * 2 + y_lo), z: 4, core: 2. Of those that a mesh axis runs over, the one named last changes fastest.
Arguments:
- block_input: bfloat16 [2, 4096, 1536], P(None, ('dp', 'expert')), may hold values from -6 to 6
- segments: int32 [2, 4096], P(None, ('dp', 'expert')), may hold values from 0 to 47, as said below
- expert_ids: int32 [2, 2, 4096, 8], P('section', None, ('dp', 'expert')), may hold values from 0 to 15, all different within a row; in each aligned block of 64 rows (0 to 63, 64 to 127, ..., all dimensions but the last counted through in order) at most 36 rows name the same one
- route_weights: float32 [2, 2, 4096, 8], P('section', None, ('dp', 'expert')), may hold values from 0.06 to 0.2
- attn_gain: float32 [2, 1536], P('section'), may hold values from 0.5 to 1.5
- w_query: bfloat16 [2, 1536, 1536], P('section'), may hold values from -0.15625 to 0.15625
- key_projection_weight: bfloat16 [2, 1536, 512], P('section'), may hold values from -0.15625 to 0.15625
- value_projection_weight: bfloat16 [2, 1536, 512], P('section'), may hold values from -0.15625 to 0.15625
- w_out: bfloat16 [2, 1536, 1536], P('section'), may hold values from -0.625 to 0.625
- ffn_gain: float32 [2, 1536], P('section'), may hold values from 0.5 to 1.5
- w_gate: bfloat16 [2, 16, 1536, 512], P('section', 'expert', 'dp'), may hold values from -0.15625 to 0.15625
- w_up: bfloat16 [2, 16, 1536, 512], P('section', 'expert', 'dp'), may hold values from -0.15625 to 0.15625
- w_down: bfloat16 [2, 16, 512, 1536], P('section', 'expert', 'dp'), may hold values from -1 to 1
- out_grad: bfloat16 [2, 4096, 1536], P(None, ('dp', 'expert')), may hold values from -6 to 6
Outputs:
- layer_outputs: bfloat16 [2, 2, 4096, 1536], P('section', None, ('dp', 'expert'))
- input_grads: float32 [2, 2, 4096, 1536], P('section', None, ('dp', 'expert'))
- attn_gain_grad: float32 [2, 1536], P('section')
- w_query_grad: float32 [2, 1536, 1536], P('section')
- w_key_grad: float32 [2, 1536, 512], P('section')
- w_value_grad: float32 [2, 1536, 512], P('section')
- w_out_grad: float32 [2, 1536, 1536], P('section')
- ffn_gain_grad: float32 [2, 1536], P('section')
- w_gate_grad: float32 [2, 16, 1536, 512], P('section', 'expert', 'dp')
- w_up_grad: float32 [2, 16, 1536, 512], P('section', 'expert', 'dp')
- w_down_grad: float32 [2, 16, 512, 1536], P('section', 'expert', 'dp')
The draws below stay inside these ranges and needn't reach their ends.
Inputs may be any that keep to these rules, and one draw needn't show every extreme that they name: `segments`: each sequence of 256 consecutive tokens holds three documents numbered 3 j, 3 j + 1, 3 j + 2 for the j-th sequence of a micro-batch, in that order; the first and last hold 1 to 32 tokens each. `expert_ids`: each row names 8 different experts; within the rows of one device of one layer and micro-batch no expert is named more than 36 times, a bound that some block reaches.
All inputs are finite; a program needn't handle non-finite values.
Results may differ from the reference program's by a relative error of at most 0.028.
Values may be sent and summed in bfloat16 or wider, within the bound.
No kernel may reach another device: no remote copies, remote signals or barrier semaphores. Data moves between devices by JAX's collectives and lax.ppermute only.
A program may use at most 256 MiB of HBM per device.

```python
import math
import jax
import jax.numpy as jnp
import numpy as np
from jax import lax

MODEL_WIDTH = 1536
QUERY_HEADS = 24
KEY_VALUE_HEADS = 8
HEAD_SIZE = 64
FFE = 512
TOP = 8
MB = 2
TOK_DEV = 64
SECTION_LAYERS = 2
EXPERTS = 16
CAP = 36
PACKED_TOKENS = 256
TOKENS = 4096


def draw_segments(key, part):
    key = jax.random.fold_in(key, 11)
    key_start, key_end = jax.random.split(key)
    sequences = MB * TOKENS // PACKED_TOKENS
    starts = jax.random.randint(key_start, (sequences, 1), 1, TOK_DEV // 2 + 1)
    ends = PACKED_TOKENS - jax.random.randint(key_end, (sequences, 1), 1, TOK_DEV // 2 + 1)
    place = jnp.arange(PACKED_TOKENS, dtype=jnp.int32)[None, :]
    local = (place >= starts).astype(jnp.int32) + (place >= ends).astype(jnp.int32)
    numbers = local + 3 * (jnp.arange(sequences, dtype=jnp.int32)[:, None] % (TOKENS // PACKED_TOKENS))
    return numbers.reshape(MB, TOKENS).astype(jnp.int32)


def block_scale(rng, dims, shards, smallest, high):
    def one(axis_at, blocks):
        heights = jax.random.uniform(jax.random.fold_in(jax.random.fold_in(rng, 6), axis_at), (blocks,), jnp.float32, smallest / len(shards), high / len(shards))
        return jnp.repeat(jnp.exp(heights), dims[axis_at] // blocks).reshape((-1,) + (1,) * (len(dims) - axis_at - 1))

    level = one(*shards[0])
    for cut in shards[1:]:
        level = level * one(*cut)
    return level


def shared_out(key, own, number, rows, number_of, top, reach, slope):
    ranking = jax.random.permutation(key, number_of)
    crowded, ordinary = load_shares(number_of, rows * top, reach, slope, True), load_shares(number_of, rows * top, reach, slope, False)
    places = jnp.arange(number_of)

    def named(sizes, rotation):
        used = int((sizes > 0).sum())
        fixed = max(1, used // 4)
        passed = fixed + (places - fixed + rotation * (used - fixed)) % max(1, number_of - fixed)
        return jnp.zeros((number_of,), jnp.int32).at[ranking[jnp.where(places < fixed, places, passed)]].set(jnp.asarray(sizes, jnp.int32))

    sizes = jnp.where(number % 4 == 0, named(crowded, number // 4), named(ordinary, number - number // 4 - 1))
    mixed = jax.random.permutation(jax.random.fold_in(own, 3), number_of)
    source_of, sink = mixed[0:number_of // 2 * 2:2], mixed[1:number_of // 2 * 2:2]
    slack = jnp.minimum(sizes[source_of] - 1, reach - sizes[sink]) // 2
    slack = jnp.where((source_of == ranking[0]) | (sink == ranking[0]) | (sizes[sink] == 0), 0, jnp.maximum(slack, 0))
    passed = jax.random.randint(jax.random.fold_in(own, 4), (number_of // 2,), 0, 1 << 20) % (slack + 1)
    sizes = sizes.at[source_of].add(-passed).at[sink].add(passed)
    labels = jnp.searchsorted(jnp.cumsum(sizes), jnp.arange(rows * top), side="right").astype(jnp.int32)
    grid = labels.reshape(top, rows).T
    grid = grid[jax.random.permutation(jax.random.fold_in(own, 1), rows)]
    rotation = jax.random.randint(jax.random.fold_in(own, 2), (rows, 1), 0, top)
    return jnp.take_along_axis(grid, (jnp.arange(top)[None, :] + rotation) % top, axis=1)


def load_shares(amount, total, limit, lean, full):
    loads = [(1 << 20) // math.isqrt(grade ** lean) + 1 for grade in range(1, amount + 1)]
    largest = limit if full else min(limit, max(-(-total // amount), total * loads[0] // sum(loads)))
    least = 1 if total - largest >= amount - 1 else 0
    given, spare = [largest] + [least] * (amount - 1), total - largest - least * (amount - 1)
    while spare > 0:
        movable = [i for i in range(1, amount) if given[i] < largest] or [i for i in range(1, amount) if given[i] < limit]
        mass, remaining = sum([loads[i] for i in movable]), spare
        for i in movable:
            addition = min(limit - given[i], max(1, remaining * loads[i] // mass), spare)
            given[i] = given[i] + addition
            spare = spare - addition
    return np.array(given)


def scatter_about(key, shape, deviation, bound, cuts=(), kind=jnp.bfloat16):
    entries = jax.random.normal(key, shape, jnp.float32) * deviation
    if len(cuts) > 0:
        entries = block_scale(key, shape, cuts, -0.22, 0.18) * entries
    return jnp.clip(entries, min=-bound, max=bound).astype(kind)


def setup_inputs(seed: int = 0) -> dict:
    splits = jax.random.split(jax.random.key(seed), 15)
    block_input = scatter_about(splits[0], (MB, TOKENS, MODEL_WIDTH), 1.0, 6.0, ((1, 64),))
    segments = draw_segments(jax.random.fold_in(splits[14], 71), 0)
    expert_ids_keys = jax.random.split(jax.random.fold_in(splits[2], 1), SECTION_LAYERS * MB * TOKENS // TOK_DEV)
    expert_ids_turns = jax.random.permutation(jax.random.fold_in(splits[2], 3), SECTION_LAYERS * MB * TOKENS // TOK_DEV)
    expert_ids = jax.vmap(lambda own, number: shared_out(jax.random.fold_in(splits[2], 2), own, number, TOK_DEV, EXPERTS, TOP, CAP, 1))(expert_ids_keys, expert_ids_turns).reshape((SECTION_LAYERS, MB, TOKENS, TOP))
    route_weights = jnp.clip(jnp.exp(math.log(0.2) - 1.2039728 * jax.random.uniform(splits[3], (SECTION_LAYERS, MB, TOKENS, TOP), jnp.float32) ** block_scale(splits[3], (SECTION_LAYERS, MB, TOKENS, TOP), ((0, 2), (2, 64)), -0.2, 0.2)), 0.06, 0.2)
    attn_gain = jnp.clip(1.0 + 0.1 * jax.random.normal(splits[4], (SECTION_LAYERS, MODEL_WIDTH), jnp.float32), 0.5, 1.5)
    w_query = scatter_about(splits[5], (SECTION_LAYERS, MODEL_WIDTH, QUERY_HEADS * HEAD_SIZE), MODEL_WIDTH ** -0.5, 0.15625, ((0, 2),))
    key_projection_weight = scatter_about(splits[6], (SECTION_LAYERS, MODEL_WIDTH, KEY_VALUE_HEADS * HEAD_SIZE), MODEL_WIDTH ** -0.5, 0.15625, ((0, 2),))
    value_projection_weight = scatter_about(splits[7], (SECTION_LAYERS, MODEL_WIDTH, KEY_VALUE_HEADS * HEAD_SIZE), MODEL_WIDTH ** -0.5, 0.15625, ((0, 2),))
    w_out = scatter_about(splits[8], (SECTION_LAYERS, QUERY_HEADS * HEAD_SIZE, MODEL_WIDTH), (QUERY_HEADS * HEAD_SIZE // 16) ** -0.5, 0.625, ((0, 2),))
    ffn_gain = jnp.clip(1.0 + 0.1 * jax.random.normal(splits[9], (SECTION_LAYERS, MODEL_WIDTH), jnp.float32), 0.5, 1.5)
    w_gate = scatter_about(splits[10], (SECTION_LAYERS, EXPERTS, MODEL_WIDTH, FFE), MODEL_WIDTH ** -0.5, 0.15625, ((0, 2), (1, 4), (2, 16)))
    w_up = scatter_about(splits[11], (SECTION_LAYERS, EXPERTS, MODEL_WIDTH, FFE), MODEL_WIDTH ** -0.5, 0.15625, ((0, 2), (1, 4), (2, 16)))
    w_down = scatter_about(splits[12], (SECTION_LAYERS, EXPERTS, FFE, MODEL_WIDTH), (FFE // 16) ** -0.5, 1.0, ((0, 2), (1, 4), (2, 16)))
    out_grad = scatter_about(splits[13], (MB, TOKENS, MODEL_WIDTH), 1.0, 6.0, ((1, 64),))
    return {"block_input": block_input, "segments": segments, "expert_ids": expert_ids, "route_weights": route_weights, "attn_gain": attn_gain, "w_query": w_query, "key_projection_weight": key_projection_weight, "value_projection_weight": value_projection_weight, "w_out": w_out, "ffn_gain": ffn_gain, "w_gate": w_gate, "w_up": w_up, "w_down": w_down, "out_grad": out_grad}


@jax.custom_vjp
def lower_precision(v):
    return lax.optimization_barrier(v.astype(jnp.bfloat16)).astype(jnp.float32)

@jax.custom_vjp
def lower_precision_backward(v):
    return v

def low_keep(v):
    return (lower_precision(v), None)

def low_pass(kept, grad):
    return (grad,)

def back_keep(v):
    return (v, None)

def back_low(kept, grad):
    return (lower_precision(grad),)
lower_precision.defvjp(low_keep, low_pass)
lower_precision_backward.defvjp(back_keep, back_low)

def product_highest(left, right):
    return jnp.dot(left, right, precision=lax.Precision.HIGHEST, preferred_element_type=jnp.float32)

def normalize(values, gain):
    return values * lax.rsqrt(lax.optimization_barrier(jnp.mean(values * values, -1, keepdims=True)) + 1e-06) * gain

def rotary_tables(token_count):
    half_size = HEAD_SIZE // 2
    frequency = 10000.0 ** (-jnp.arange(half_size, dtype=jnp.float32) * 2.0 / HEAD_SIZE)
    position = (jnp.arange(token_count) % PACKED_TOKENS).astype(jnp.float32)
    angles = position[:, None] * frequency[None, :]
    angles = jnp.concatenate([angles, angles], -1)
    return (jnp.cos(angles), jnp.sin(angles))

def rotary_apply(values, cosine_table, sine_table):
    half_size = values.shape[-1] // 2
    turned = jnp.concatenate([-values[..., half_size:], values[..., :half_size]], -1)
    return values * cosine_table[:, None, :] + turned * sine_table[:, None, :]

def attend_heads(operands):
    query_rows, every_key, every_value, document_labels = operands
    sequence_length = query_rows.shape[0]
    grouped_heads = query_rows.reshape(sequence_length, KEY_VALUE_HEADS, QUERY_HEADS // KEY_VALUE_HEADS, HEAD_SIZE)
    raw_scores = lower_precision_backward(jnp.einsum('tkgd,skd->kgts', grouped_heads, every_key, precision=lax.Precision.HIGHEST))
    place = jnp.arange(sequence_length)
    allowed = (place[None, :] <= place[:, None]) & (document_labels[None, :] == document_labels[:, None])
    scores = jnp.where(allowed, raw_scores * 0.125, -1e+30)
    peak = lax.optimization_barrier(jnp.max(scores, -1, keepdims=True))
    log_total = peak + jnp.log(lax.optimization_barrier(jnp.sum(jnp.exp(scores - peak), -1, keepdims=True)))
    weights_low = lower_precision(jnp.exp(scores - log_total))
    mixed_heads = jnp.einsum('kgts,skd->tkgd', weights_low, every_value, precision=lax.Precision.HIGHEST)
    return mixed_heads.reshape(sequence_length, QUERY_HEADS * HEAD_SIZE)

def block_layer(hidden, document_labels, routes, gates, attn_g, w_q, key_weight, value_weight, w_o, ffn_g, gate_all, up_all, down_all):
    token_count = hidden.shape[0]
    normed_input = lower_precision(normalize(hidden, attn_g))
    cosine_table, sine_table = rotary_tables(token_count)
    query_rows = lower_precision(rotary_apply(lower_precision_backward(product_highest(normed_input, w_q)).reshape(token_count, QUERY_HEADS, HEAD_SIZE), cosine_table, sine_table))
    every_key = lower_precision(rotary_apply(lower_precision_backward(product_highest(normed_input, key_weight)).reshape(token_count, KEY_VALUE_HEADS, HEAD_SIZE), cosine_table, sine_table))
    every_value = lower_precision_backward(lower_precision(product_highest(normed_input, value_weight))).reshape(token_count, KEY_VALUE_HEADS, HEAD_SIZE)
    query_groups = token_count // PACKED_TOKENS
    mixed_heads = lax.map(jax.checkpoint(attend_heads), (query_rows.reshape(query_groups, PACKED_TOKENS, QUERY_HEADS, HEAD_SIZE), every_key.reshape(query_groups, PACKED_TOKENS, KEY_VALUE_HEADS, HEAD_SIZE), every_value.reshape(query_groups, PACKED_TOKENS, KEY_VALUE_HEADS, HEAD_SIZE), document_labels.reshape(query_groups, PACKED_TOKENS)))
    mixed_heads = lower_precision_backward(lower_precision(mixed_heads.reshape(token_count, QUERY_HEADS * HEAD_SIZE)))
    after_attn = hidden + lower_precision_backward(product_highest(mixed_heads, w_o))
    normed_ffn = lower_precision(normalize(after_attn, ffn_g))
    shares = lax.optimization_barrier(jnp.sum(gates[:, :, None] * (routes[:, :, None] == jnp.arange(EXPERTS)[None, None, :]).astype(jnp.float32), 1))

    def expert_step(total, operands):
        gate_w, up_w, down_w, weight = operands
        routed = lower_precision_backward(normed_ffn)
        gate_pre = lower_precision_backward(product_highest(routed, gate_w))
        up_pre = lower_precision_backward(product_highest(routed, up_w))
        hidden_units = lower_precision(jax.nn.silu(gate_pre) * up_pre)
        result = lower_precision_backward(lower_precision(product_highest(hidden_units, down_w)))
        return (total + weight[:, None] * result, None)
    mixture, unused = lax.scan(jax.checkpoint(expert_step), jnp.zeros_like(after_attn), (gate_all, up_all, down_all, shares.T))
    return after_attn + mixture

def reference(block_input, segments, expert_ids, route_weights, attn_gain, w_query, key_projection_weight, value_projection_weight, w_out, ffn_gain, w_gate, w_up, w_down, out_grad):
    token_count = MB * TOKENS
    start = block_input.astype(jnp.float32).reshape(token_count, MODEL_WIDTH)
    document_labels = segments.reshape(token_count)
    routes = expert_ids.reshape(SECTION_LAYERS, token_count, TOP)
    gates = route_weights.astype(jnp.float32).reshape(SECTION_LAYERS, token_count, TOP)
    params = tuple((item.astype(jnp.float32) for item in (attn_gain, w_query, key_projection_weight, value_projection_weight, w_out, ffn_gain, w_gate, w_up, w_down)))

    def forward(first_in, offset, weights):
        first = block_layer(first_in, document_labels, routes[0], gates[0], *[item[0] for item in weights])
        first_low = lower_precision(first)
        second_in = lower_precision_backward(first_low) + offset
        second = block_layer(second_in, document_labels, routes[1], gates[1], *[item[1] for item in weights])
        return (first_low, second)
    outputs, pullback = jax.vjp(forward, start, jnp.zeros_like(start), params)
    first_low, second = outputs
    cotangent = out_grad.astype(jnp.float32).reshape(token_count, MODEL_WIDTH)
    start_grad, middle_grad, grads = pullback((jnp.zeros_like(first_low), cotangent))
    layer_outputs = jnp.stack([first_low, second]).reshape(SECTION_LAYERS, MB, TOKENS, MODEL_WIDTH).astype(jnp.bfloat16)
    input_grads = jnp.stack([start_grad, middle_grad]).reshape(SECTION_LAYERS, MB, TOKENS, MODEL_WIDTH)
    return (layer_outputs, input_grads, grads[0], grads[1], grads[2], grads[3], grads[4], grads[5], grads[6], grads[7], grads[8])
```

```python
import functools

import jax
import jax.numpy as jnp
from jax import lax
from jax.experimental import pallas as pl
from jax.experimental.pallas import tpu as pltpu
from jax.sharding import PartitionSpec as P

QUERY_HEADS = 24
KEY_VALUE_HEADS = 8
HEAD_SIZE = 64
GROUP = QUERY_HEADS // KEY_VALUE_HEADS
EPS = 1e-06
LOW = jnp.bfloat16
F32 = jnp.float32
VMEM_BYTES = 56 * 1024 * 1024


def params(*semantics):
    return pltpu.CompilerParams(dimension_semantics=semantics, vmem_limit_bytes=VMEM_BYTES)


def dot(left, right):
    return jnp.dot(left, right, preferred_element_type=F32)


def dot_nt(left, right):
    return lax.dot_general(left, right, (((1,), (1,)), ((), ())), preferred_element_type=F32)


def dot_tn(left, right):
    return lax.dot_general(left, right, (((0,), (0,)), ((), ())), preferred_element_type=F32)


def shifted(block, by):
    size = lax.axis_size("expert")
    return lax.ppermute(block, "expert", [(i, (i + by) % size) for i in range(size)])


def gather_group(block):
    size = lax.axis_size("expert")
    return jnp.concatenate([block] + [shifted(block, j) for j in range(1, size)], 1)


def sum_to_owners(partial, tokens):
    size = lax.axis_size("expert")
    total = partial[:, :tokens].astype(F32)
    for j in range(1, size):
        total = total + shifted(partial[:, j * tokens : (j + 1) * tokens], size - j).astype(F32)
    return total


def to_section(block, target):
    return lax.ppermute(block, "section", [(1 - target, target)])


RING, PAIR, CORES = 4, 2, 2


def moved(block, x=0, y=0, core=0):
    route = []
    for i in range(RING):
        for j in range(PAIR):
            for k in range(CORES):
                target = ((i + x) % RING * PAIR + (j + y) % PAIR) * CORES + (k + core) % CORES
                route.append(((i * PAIR + j) * CORES + k, target))
    return lax.ppermute(block, "dp", route)


def added(*terms):
    total = terms[0].astype(F32)
    for term in terms[1:]:
        total = total + term.astype(F32)
    return total


def ring_sum(blocks):
    flat = blocks.reshape((2 * RING,) + blocks.shape[2:])
    from_below = moved(flat[3:5], x=1)
    from_above = moved(flat[5:7], x=-1)
    below = moved(added(flat[2], from_below[1]).astype(LOW), x=1)
    above = moved(added(flat[7], from_above[0]).astype(LOW), x=-1)
    return added(flat[0], from_above[1], below), added(flat[1], from_below[0], above)


def ring_first_sum(blocks):
    first, second = ring_sum(blocks)
    away = jnp.stack([first[1], second[1]]).astype(LOW)
    return added(jnp.stack([first[0], second[0]]), moved(away, y=1))


def pair_first_sum(blocks):
    return jnp.stack(ring_sum(added(blocks[0], moved(blocks[1], y=1)).astype(LOW)))


def ring_gather(block):
    below, above = moved(block, x=1), moved(block, x=-1)
    across = jnp.stack([moved(below[0], x=1), moved(above[1], x=-1)])
    return jnp.stack([block, below, across, above])


def pair_gather(block):
    return jnp.stack([block, moved(block, y=1)])


def group_stack(block):
    return jnp.stack([block] + [shifted(block, j) for j in range(1, lax.axis_size("expert"))])


def sum_everywhere(values):
    for axis in ("dp", "expert"):
        size, bit = lax.axis_size(axis), 1
        while bit < size:
            values = values + lax.ppermute(values, axis, [(i, i ^ bit) for i in range(size)])
            bit *= 2
    return values


def swap_halves(values):
    half = HEAD_SIZE // 2
    lanes = values.shape[-1]
    lane = lax.broadcasted_iota(jnp.int32, values.shape, values.ndim - 1)
    ahead = pltpu.roll(values, lanes - half, values.ndim - 1)
    behind = pltpu.roll(values, half, values.ndim - 1)
    return jnp.where(lane % HEAD_SIZE < half, ahead, behind)


def widen_table(table, lanes):
    return jnp.concatenate([table] * (lanes // table.shape[-1]), -1)


def project_kernel(query_steps, x_ref, gain_ref, wq_ref, wk_ref, wv_ref, cos_ref, sin_ref, out_ref, xn_ref):
    step = pl.program_id(0)

    @pl.when(step == 0)
    def _():
        wide = x_ref[...].astype(F32)
        scale = lax.rsqrt(jnp.mean(wide * wide, -1, keepdims=True) + EPS)
        xn_ref[...] = (wide * scale * gain_ref[...]).astype(LOW)

    def turned(weight):
        product = dot(xn_ref[...], weight)
        lanes = product.shape[-1]
        cos, sin = widen_table(cos_ref[...], lanes), widen_table(sin_ref[...], lanes)
        return (product * cos + swap_halves(product) * sin).astype(LOW)

    @pl.when(step < query_steps)
    def _():
        out_ref[...] = turned(wq_ref[...])

    @pl.when(step == query_steps)
    def _():
        out_ref[...] = turned(wk_ref[...])

    @pl.when(step == query_steps + 1)
    def _():
        out_ref[...] = dot(xn_ref[...], wv_ref[...]).astype(LOW)


def project(x, gain, wq, wk, wv, cos, sin):
    rows, width = x.shape
    lanes = wk.shape[1]
    query_steps = wq.shape[1] // lanes
    whole = lambda *shape: pl.BlockSpec(shape, lambda i: (0,) * len(shape))
    return pl.pallas_call(
        functools.partial(project_kernel, query_steps),
        grid=(query_steps + 2,),
        in_specs=[
            whole(rows, width),
            whole(1, width),
            pl.BlockSpec((width, lanes), lambda i: (0, jnp.minimum(i, query_steps - 1))),
            whole(width, lanes),
            whole(width, lanes),
            whole(rows, cos.shape[1]),
            whole(rows, cos.shape[1]),
        ],
        out_specs=[pl.BlockSpec((rows, lanes), lambda i: (0, i)), whole(rows, width)],
        out_shape=[
            jax.ShapeDtypeStruct((rows, lanes * (query_steps + 2)), LOW),
            jax.ShapeDtypeStruct((rows, width), LOW),
        ],
        compiler_params=params("arbitrary"),
        cost_estimate=pl.CostEstimate(
            flops=2 * rows * width * lanes * (query_steps + 2),
            bytes_accessed=2 * width * lanes * (query_steps + 2) + 8 * rows * width,
            transcendentals=0,
        ),
        name="project",
    )(x, gain, wq, wk, wv, cos, sin)


def head(values, index):
    return values[:, index * HEAD_SIZE : (index + 1) * HEAD_SIZE]


def softmax_parts(stacked_q, key, allowed):
    scores = jnp.where(allowed, dot_nt(stacked_q, key) * 0.125, -1e30)
    raised = jnp.exp(scores - jnp.max(scores, -1, keepdims=True))
    return raised / jnp.sum(raised, -1, keepdims=True)


def allowed_mask(place_col, place_row, label_col, label_row):
    one = (place_row <= place_col) & (label_row == label_col)
    return jnp.concatenate([one] * GROUP, 0)


def attend_kernel(
    q_ref, k_ref, v_ref, pc_ref, pr_ref, lc_ref, lr_ref, x_ref, wo_ref, gain_ref,
    o_ref, h1_ref, xn2_ref, total_ref,
):
    chunk = pl.program_id(1)
    allowed = allowed_mask(pc_ref[...], pr_ref[...], lc_ref[0], lr_ref[0])
    q, k, v = q_ref[0], k_ref[0], v_ref[0]
    rows = q.shape[0]
    mixed = []
    for pair in range(k.shape[1] // HEAD_SIZE):
        stacked = jnp.concatenate([head(q, pair * GROUP + j) for j in range(GROUP)], 0)
        probs = softmax_parts(stacked, head(k, pair), allowed).astype(LOW)
        out = dot(probs, head(v, pair))
        mixed += [out[j * rows : (j + 1) * rows] for j in range(GROUP)]
    mixed = jnp.concatenate(mixed, -1).astype(LOW)
    o_ref[0] = mixed
    part = dot(mixed, wo_ref[...])

    @pl.when(chunk == 0)
    def _():
        total_ref[...] = x_ref[0].astype(F32) + part

    @pl.when(chunk > 0)
    def _():
        total_ref[...] += part

    @pl.when(chunk == pl.num_programs(1) - 1)
    def _():
        total = total_ref[...]
        scale = lax.rsqrt(jnp.mean(total * total, -1, keepdims=True) + EPS)
        h1_ref[0] = total[: h1_ref.shape[1]]
        xn2_ref[0] = (total * scale * gain_ref[...]).astype(LOW)


def attend(qkv, x, wo, gain, marks, parts, own):
    batches, rows, width = x.shape
    place_col, place_row, label_col, label_row = marks
    q_lanes, k_lanes = wo.shape[0] // parts, KEY_VALUE_HEADS * HEAD_SIZE // parts
    k_at = wo.shape[0] // k_lanes
    full = lambda *shape: pl.BlockSpec(shape, lambda b, c: (0,) * len(shape))
    batch = lambda *shape: pl.BlockSpec((1,) + shape, lambda b, c: (b, 0, 0))
    return pl.pallas_call(
        attend_kernel,
        grid=(batches, parts),
        in_specs=[
            pl.BlockSpec((1, rows, q_lanes), lambda b, c: (b, 0, c)),
            pl.BlockSpec((1, rows, k_lanes), lambda b, c: (b, 0, k_at + c)),
            pl.BlockSpec((1, rows, k_lanes), lambda b, c: (b, 0, k_at + parts + c)),
            full(rows, 1),
            full(1, rows),
            batch(rows, 1),
            batch(1, rows),
            batch(rows, width),
            pl.BlockSpec((q_lanes, width), lambda b, c: (c, 0)),
            full(1, width),
        ],
        out_specs=[
            pl.BlockSpec((1, rows, q_lanes), lambda b, c: (b, 0, c)),
            batch(own, width),
            batch(rows, width),
        ],
        out_shape=[
            jax.ShapeDtypeStruct((batches, rows, wo.shape[0]), LOW),
            jax.ShapeDtypeStruct((batches, own, width), F32),
            jax.ShapeDtypeStruct((batches, rows, width), LOW),
        ],
        scratch_shapes=[pltpu.VMEM((rows, width), F32)],
        compiler_params=params("arbitrary", "arbitrary"),
        cost_estimate=pl.CostEstimate(
            flops=2 * batches * rows * width * wo.shape[0] + 16 * batches * rows * rows * wo.shape[0],
            bytes_accessed=4 * width * wo.shape[0] + 12 * batches * rows * width,
            transcendentals=batches * rows * rows * QUERY_HEADS,
        ),
        name="attend",
    )(qkv, qkv, qkv, place_col, place_row, label_col, label_row, x, wo, gain)


def expert_hidden(xn_ref, share_ref, wg_ref, wu_ref):
    gate, up = dot(xn_ref[...], wg_ref[0]), dot(xn_ref[...], wu_ref[0])
    share = share_ref[0]
    sigma = jax.nn.sigmoid(gate)
    silu = gate * sigma
    return gate, up, share, sigma, silu


def experts_forward_kernel(xn_ref, share_ref, wg_ref, wu_ref, wd_ref, out_ref, total_ref):
    step = pl.program_id(0)
    _, up, share, _, silu = expert_hidden(xn_ref, share_ref, wg_ref, wu_ref)
    part = dot((silu * up * share).astype(LOW), wd_ref[0])

    @pl.when(step == 0)
    def _():
        total_ref[...] = part

    @pl.when(step > 0)
    def _():
        total_ref[...] += part

    @pl.when(step == pl.num_programs(0) - 1)
    def _():
        out_ref[...] = total_ref[...].astype(LOW)


def experts_keep_kernel(xn_ref, share_ref, wg_ref, wu_ref, hidden_ref, to_up_ref, to_gate_ref):
    gate, up, share, sigma, silu = expert_hidden(xn_ref, share_ref, wg_ref, wu_ref)
    shared = silu * share
    hidden_ref[...] = (shared * up).astype(LOW)
    to_up_ref[...] = shared.astype(LOW)
    to_gate_ref[...] = (share * up * sigma * (1.0 + gate * (1.0 - sigma))).astype(LOW)


def expert_specs(rows, width, units):
    return [
        pl.BlockSpec((rows, width), lambda e: (0, 0)),
        pl.BlockSpec((1, rows, 1), lambda e: (e, 0, 0)),
        pl.BlockSpec((1, width, units), lambda e: (e, 0, 0)),
        pl.BlockSpec((1, width, units), lambda e: (e, 0, 0)),
    ]


def experts_forward(xn, share, wg, wu, wd):
    rows, width = xn.shape
    count, _, units = wg.shape
    return pl.pallas_call(
        experts_forward_kernel,
        grid=(count,),
        in_specs=expert_specs(rows, width, units)
        + [pl.BlockSpec((1, units, width), lambda e: (e, 0, 0))],
        out_specs=pl.BlockSpec((rows, width), lambda e: (0, 0)),
        out_shape=jax.ShapeDtypeStruct((rows, width), LOW),
        scratch_shapes=[pltpu.VMEM((rows, width), F32)],
        compiler_params=params("arbitrary"),
        cost_estimate=pl.CostEstimate(
            flops=6 * rows * width * units * count,
            bytes_accessed=6 * width * units * count,
            transcendentals=rows * units * count,
        ),
        name="experts_forward",
    )(xn, share, wg, wu, wd)


def experts_keep(xn, share, wg, wu):
    rows, width = xn.shape
    count, _, units = wg.shape
    kept = pl.BlockSpec((rows, units), lambda e: (0, e))
    return pl.pallas_call(
        experts_keep_kernel,
        grid=(count,),
        in_specs=expert_specs(rows, width, units),
        out_specs=[kept] * 3,
        out_shape=[jax.ShapeDtypeStruct((rows, units * count), LOW)] * 3,
        compiler_params=params("arbitrary"),
        cost_estimate=pl.CostEstimate(
            flops=4 * rows * width * units * count,
            bytes_accessed=4 * width * units * count,
            transcendentals=rows * units * count,
        ),
        name="experts_keep",
    )(xn, share, wg, wu)


def experts_backward_kernel(c_ref, up_ref, gate_ref, wg_ref, wu_ref, wd_ref, *refs):
    out_ref, total_ref = refs[0], refs[-1]
    step = pl.program_id(0)
    hidden = dot_nt(c_ref[...], wd_ref[0])
    gate_grad = (hidden * gate_ref[...].astype(F32)).astype(LOW)
    up_grad = (hidden * up_ref[...].astype(F32)).astype(LOW)
    if len(refs) == 4:
        refs[1][...] = gate_grad
        refs[2][...] = up_grad
    part = dot_nt(gate_grad, wg_ref[0]) + dot_nt(up_grad, wu_ref[0])

    @pl.when(step == 0)
    def _():
        total_ref[...] = part

    @pl.when(step > 0)
    def _():
        total_ref[...] += part

    @pl.when(step == pl.num_programs(0) - 1)
    def _():
        out_ref[...] = total_ref[...].astype(LOW)


def experts_backward(c, to_up, to_gate, wg, wu, wd, keep):
    rows, width = c.shape
    count, _, units = wg.shape
    kept = pl.BlockSpec((rows, units), lambda e: (0, e))
    kept_shape = jax.ShapeDtypeStruct((rows, units * count), LOW)
    return pl.pallas_call(
        experts_backward_kernel,
        grid=(count,),
        in_specs=[
            pl.BlockSpec((rows, width), lambda e: (0, 0)),
            kept,
            kept,
            pl.BlockSpec((1, width, units), lambda e: (e, 0, 0)),
            pl.BlockSpec((1, width, units), lambda e: (e, 0, 0)),
            pl.BlockSpec((1, units, width), lambda e: (e, 0, 0)),
        ],
        out_specs=[pl.BlockSpec((rows, width), lambda e: (0, 0))] + [kept, kept] * keep,
        out_shape=[jax.ShapeDtypeStruct((rows, width), LOW)] + [kept_shape, kept_shape] * keep,
        scratch_shapes=[pltpu.VMEM((rows, width), F32)],
        compiler_params=params("arbitrary"),
        cost_estimate=pl.CostEstimate(
            flops=6 * rows * width * units * count,
            bytes_accessed=6 * width * units * count,
            transcendentals=0,
        ),
        name="experts_backward",
    )(c, to_up, to_gate, wg, wu, wd)


def attend_backward_kernel(
    z_ref, q_ref, k_ref, v_ref, da_ref, wo_ref, wq_ref, wk_ref, wv_ref,
    pc_ref, pr_ref, lc_ref, lr_ref, cos_ref, sin_ref,
    dqkv_ref, dn_ref,
):
    del z_ref
    allowed = allowed_mask(pc_ref[...], pr_ref[...], lc_ref[0], lr_ref[0])
    q, k, v = q_ref[0], k_ref[0], v_ref[0]
    rows = q.shape[0]
    dout = dot_nt(da_ref[0], wo_ref[...]).astype(LOW)
    dqs, dks, dvs = [], [], []
    for pair in range(k.shape[1] // HEAD_SIZE):
        key, value = head(k, pair), head(v, pair)
        queries = jnp.concatenate([head(q, pair * GROUP + j) for j in range(GROUP)], 0)
        douts = jnp.concatenate([head(dout, pair * GROUP + j) for j in range(GROUP)], 0)
        probs = softmax_parts(queries, key, allowed)
        dprobs = dot_nt(douts, value)
        centre = jnp.sum(probs * dprobs, -1, keepdims=True)
        dscores = (probs * (dprobs - centre) * 0.125).astype(LOW)
        dquery = dot(dscores, key)
        dqs += [dquery[j * rows : (j + 1) * rows] for j in range(GROUP)]
        dks.append(dot_tn(dscores, queries))
        dvs.append(dot_tn(probs.astype(LOW), douts))

    def turned_back(grads):
        lanes = grads.shape[-1]
        cos, sin = widen_table(cos_ref[...], lanes), widen_table(sin_ref[...], lanes)
        return (grads * cos + swap_halves(grads * sin)).astype(LOW)

    dq = turned_back(jnp.concatenate(dqs, -1))
    dk = turned_back(jnp.concatenate(dks, -1))
    dv = jnp.concatenate(dvs, -1).astype(LOW)
    dqkv_ref[0] = jnp.concatenate([dq, dk, dv], -1)
    dn = dot_nt(dq, wq_ref[...]) + dot_nt(dk, wk_ref[...]) + dot_nt(dv, wv_ref[...])
    dn_ref[0] = dn.astype(LOW)


def attend_backward(z, qkv, da, wo, wq, wk, wv, marks, cos, sin, parts):
    batches, rows, width = da.shape
    place_col, place_row, label_col, label_row = marks
    q_lanes, k_lanes = wo.shape[0] // parts, KEY_VALUE_HEADS * HEAD_SIZE // parts
    k_at = wo.shape[0] // k_lanes
    full = lambda *shape: pl.BlockSpec(shape, lambda b, z: (0,) * len(shape))
    batch = lambda *shape: pl.BlockSpec((1,) + shape, lambda b, z: (b, 0, 0))
    columns = lambda lanes: pl.BlockSpec((width, lanes), lambda b, z: (0, z[0]))
    return pl.pallas_call(
        attend_backward_kernel,
        grid_spec=pltpu.PrefetchScalarGridSpec(
            num_scalar_prefetch=1,
            grid=(batches,),
            in_specs=[
                pl.BlockSpec((1, rows, q_lanes), lambda b, z: (b, 0, z[0])),
                pl.BlockSpec((1, rows, k_lanes), lambda b, z: (b, 0, k_at + z[0])),
                pl.BlockSpec((1, rows, k_lanes), lambda b, z: (b, 0, k_at + parts + z[0])),
                batch(rows, width),
                pl.BlockSpec((q_lanes, width), lambda b, z: (z[0], 0)),
                columns(q_lanes),
                columns(k_lanes),
                columns(k_lanes),
                full(rows, 1),
                full(1, rows),
                batch(rows, 1),
                batch(1, rows),
                full(rows, cos.shape[1]),
                full(rows, cos.shape[1]),
            ],
            out_specs=[batch(rows, q_lanes + 2 * k_lanes), batch(rows, width)],
        ),
        out_shape=[
            jax.ShapeDtypeStruct((batches, rows, q_lanes + 2 * k_lanes), LOW),
            jax.ShapeDtypeStruct((batches, rows, width), LOW),
        ],
        compiler_params=params("arbitrary"),
        cost_estimate=pl.CostEstimate(
            flops=2 * batches * rows * width * 2 * (q_lanes + k_lanes) + 40 * batches * rows * rows * q_lanes,
            bytes_accessed=4 * width * (q_lanes + k_lanes) + 6 * batches * rows * width,
            transcendentals=batches * rows * rows * q_lanes // HEAD_SIZE,
        ),
        name="attend_backward",
    )(z, qkv, qkv, qkv, da, wo, wq, wk, wv, place_col, place_row, label_col, label_row, cos, sin)


def chip_block(place_ref, x, y, core):
    ring = lax.rem(place_ref[0] + x, RING)
    pair = lax.rem(place_ref[1] + y, PAIR)
    return (ring * PAIR + pair) * CORES + lax.rem(place_ref[2] + core, CORES)


def expert_grad_kernel(cut, place_ref, left_ref, right_ref, *refs):
    product_ref = refs[-1]
    rows = product_ref.shape[1]
    product = dot_tn(left_ref[...], right_ref[...]).astype(LOW)
    for i in range(RING * PAIR * CORES):
        product_ref[i] = product[i * rows : (i + 1) * rows]
    step = pl.program_id(0)
    lanes = refs[0].shape[-1]

    def place(refs, ring_first):
        for core in range(CORES):
            for x in range(RING):
                for y in range(PAIR):
                    block = product_ref[chip_block(place_ref, x, y, core)]
                    for part in range(cut):
                        at = slice(part * rows, (part + 1) * rows)
                        value = block[:, part * lanes : (part + 1) * lanes]
                        if ring_first:
                            refs[core][x, 0, y, at] = value
                        else:
                            refs[core][y, x, 0, at] = value

    @pl.when(step < pl.num_programs(0) // 2)
    def _():
        place(refs[0:2], True)

    @pl.when(step >= pl.num_programs(0) // 2)
    def _():
        place(refs[2:4], False)


def expert_grad(place, left, right, count, cut):
    rows = left.shape[0]
    left_lanes = left.shape[1] // count if cut > 1 else left.shape[1]
    right_lanes = right.shape[1] if cut > 1 else right.shape[1] // count
    owners = RING * PAIR * CORES
    high, lanes, half = left_lanes // owners, right_lanes // cut, count // 2
    ring_first = (RING, half, PAIR, high * cut, lanes)
    pair_first = (PAIR, RING, half, high * cut, lanes)
    ring_spec = pl.BlockSpec((RING, 1, PAIR, high * cut, lanes), lambda e, p: (0, jnp.minimum(e, half - 1), 0, 0, 0))
    pair_spec = pl.BlockSpec((PAIR, RING, 1, high * cut, lanes), lambda e, p: (0, 0, jnp.maximum(e - half, 0), 0, 0))
    split = lambda wide, by: pl.BlockSpec((rows, wide), (lambda e, p: (0, e)) if by else (lambda e, p: (0, 0)))
    return pl.pallas_call(
        functools.partial(expert_grad_kernel, cut),
        grid_spec=pltpu.PrefetchScalarGridSpec(
            num_scalar_prefetch=1,
            grid=(count,),
            in_specs=[split(left_lanes, cut > 1), split(right_lanes, cut == 1)],
            out_specs=[ring_spec, ring_spec, pair_spec, pair_spec],
            scratch_shapes=[pltpu.VMEM((owners, high, right_lanes), LOW)],
        ),
        out_shape=[jax.ShapeDtypeStruct(shape, LOW) for shape in (ring_first, ring_first, pair_first, pair_first)],
        compiler_params=params("arbitrary"),
        cost_estimate=pl.CostEstimate(
            flops=2 * rows * left_lanes * right_lanes * count,
            bytes_accessed=2 * left_lanes * right_lanes * count + 4 * rows * (left_lanes + right_lanes),
            transcendentals=0,
        ),
        name="expert_grad",
    )(place, left, right)


def into_grad_kernel(place_ref, left_ref, right_ref, mine_ref, other_ref, product_ref):
    half = product_ref.shape[1] // 2
    product = dot_tn(left_ref[...], right_ref[...]).astype(LOW)
    for i in range(RING * PAIR * CORES):
        product_ref[i] = product[i * 2 * half : (i + 1) * 2 * half]
    for core, ref in enumerate((mine_ref, other_ref)):
        for x in range(RING):
            for y in range(PAIR):
                block = product_ref[chip_block(place_ref, x, y, core)]
                ref[x, 0, y] = block[:half]
                ref[x, 1, y] = block[half:]


def out_of_grad_kernel(place_ref, z_ref, left_ref, right_ref, mine_ref, other_ref, product_ref):
    del z_ref
    high, lanes = mine_ref.shape[-2:]
    product = dot_tn(left_ref[...], right_ref[...]).astype(LOW)
    for i in range(RING * PAIR):
        for core in range(CORES):
            product_ref[i * CORES + core] = product[i * high : (i + 1) * high, core * 2 * lanes : (core + 1) * 2 * lanes]
    for core, ref in enumerate((mine_ref, other_ref)):
        for x in range(RING):
            for y in range(PAIR):
                block = product_ref[chip_block(place_ref, x, y, core)]
                ref[x, 0, y] = block[:, :lanes]
                ref[x, 1, y] = block[:, lanes:]


def dense_grad(place, z, left, right, parts, outward):
    rows = left.shape[0]
    owners = RING * PAIR * CORES
    if outward:
        left_lanes = left.shape[1] // parts
        high, lanes = left_lanes // (RING * PAIR), right.shape[1] // CORES // 2
        scratch = (owners, high, 2 * lanes)
    else:
        left_lanes = left.shape[1]
        high, lanes = left_lanes // owners // 2, right.shape[1]
        scratch = (owners, 2 * high, lanes)
    shape = (RING, 2, PAIR, high, lanes)
    scalars = (place, z) if outward else (place,)
    return pl.pallas_call(
        out_of_grad_kernel if outward else into_grad_kernel,
        grid_spec=pltpu.PrefetchScalarGridSpec(
            num_scalar_prefetch=len(scalars),
            grid=(1,),
            in_specs=[
                pl.BlockSpec((rows, left_lanes), lambda i, *s: (0, s[1][0] if outward else 0)),
                pl.BlockSpec((rows, right.shape[1]), lambda i, *s: (0, 0)),
            ],
            out_specs=[pl.BlockSpec(shape, lambda i, *s: (0,) * 5)] * 2,
            scratch_shapes=[pltpu.VMEM(scratch, LOW)],
        ),
        out_shape=[jax.ShapeDtypeStruct(shape, LOW)] * 2,
        compiler_params=params("arbitrary"),
        cost_estimate=pl.CostEstimate(
            flops=2 * rows * left_lanes * right.shape[1],
            bytes_accessed=2 * left_lanes * right.shape[1] + 2 * rows * (left_lanes + right.shape[1]),
            transcendentals=0,
        ),
        name="dense_grad",
    )(*scalars, left, right)


def into_layout_kernel(place_ref, z_ref, mine_ref, other_ref, wq_ref, wk_ref, wv_ref):
    parts = mine_ref.shape[0]
    half = mine_ref.shape[-2]

    def place(ref):
        for k in range(parts):
            at = lax.rem(z_ref[0] + parts - k, parts)
            start = 0
            for out in (wq_ref, wk_ref, wv_ref):
                lanes = out.shape[1] // parts
                for h in range(2):
                    columns = pl.ds(pl.multiple_of(at * lanes, 128), lanes)
                    value = ref[k, 0, 0, h, :, start : start + lanes]
                    out[h * half : (h + 1) * half, columns] = value.astype(F32)
                start += lanes

    @pl.when(pl.program_id(0) == 0)
    def _():
        place(mine_ref)

    @pl.when(pl.program_id(0) == 1)
    def _():
        place(other_ref)


def into_layout(place, z, mine, other, shapes):
    parts, _, _, _, half, lanes = mine.shape

    def row_block(core, x, y, place, z):
        ring = lax.rem(place[0] + RING - x, RING)
        pair = lax.rem(place[1] + y, PAIR)
        return ((ring * PAIR + pair) * CORES + lax.rem(place[2] + core, CORES), 0)

    block = (parts, 1, 1, 2, half, lanes)
    return pl.pallas_call(
        into_layout_kernel,
        grid_spec=pltpu.PrefetchScalarGridSpec(
            num_scalar_prefetch=2,
            grid=(CORES, RING, PAIR),
            in_specs=[
                pl.BlockSpec(block, lambda c, x, y, p, z: (0, jnp.where(c == 0, y, PAIR - 1), jnp.where(c == 0, x, RING - 1), 0, 0, 0)),
                pl.BlockSpec(block, lambda c, x, y, p, z: (0, jnp.where(c == 1, y, 0), jnp.where(c == 1, x, 0), 0, 0, 0)),
            ],
            out_specs=[pl.BlockSpec((2 * half, shape[1]), row_block) for shape in shapes],
        ),
        out_shape=[jax.ShapeDtypeStruct(shape, F32) for shape in shapes],
        compiler_params=params("arbitrary", "arbitrary", "arbitrary"),
        cost_estimate=pl.CostEstimate(flops=0, bytes_accessed=12 * mine.size, transcendentals=0),
        name="into_layout",
    )(place, z, mine, other)


def out_of_layout_kernel(place_ref, z_ref, mine_ref, other_ref, out_ref):
    parts = mine_ref.shape[0]
    lanes = mine_ref.shape[-1]
    for core, ref in enumerate((mine_ref, other_ref)):
        first = lax.rem(place_ref[2] + core, CORES) * 2 * lanes
        for k in range(parts):
            at = lax.rem(z_ref[0] + parts - k, parts)
            for h in range(2):
                columns = pl.ds(pl.multiple_of(first + h * lanes, 128), lanes)
                out_ref[at, 0, :, columns] = ref[k, 0, 0, h].astype(F32)


def out_of_layout(place, z, mine, other):
    parts, _, _, _, high, lanes = mine.shape
    width = 2 * CORES * lanes
    block = pl.BlockSpec((parts, 1, 1, 2, high, lanes), lambda x, y, p, z: (0, y, x, 0, 0, 0))

    def row_block(x, y, place, z):
        return (0, lax.rem(place[0] + RING - x, RING) * PAIR + lax.rem(place[1] + y, PAIR), 0, 0)

    out = pl.pallas_call(
        out_of_layout_kernel,
        grid_spec=pltpu.PrefetchScalarGridSpec(
            num_scalar_prefetch=2,
            grid=(RING, PAIR),
            in_specs=[block, block],
            out_specs=pl.BlockSpec((parts, 1, high, width), row_block),
        ),
        out_shape=jax.ShapeDtypeStruct((parts, RING * PAIR, high, width), F32),
        compiler_params=params("arbitrary", "arbitrary"),
        cost_estimate=pl.CostEstimate(flops=0, bytes_accessed=12 * mine.size, transcendentals=0),
        name="out_of_layout",
    )(place, z, mine, other)
    return out.reshape(-1, width)


def norm_back(grad_normed, values, gain):
    scale = lax.rsqrt(jnp.mean(values * values, -1, keepdims=True) + EPS)
    scaled = grad_normed * gain
    gain_grad = jnp.sum(grad_normed * values * scale, (0, 1))
    inner = jnp.mean(scaled * values, -1, keepdims=True)
    return (scale * scaled - values * scale * scale * scale * inner, gain_grad)


def local(
    block_input, segments, expert_ids, route_weights, attn_gain, w_query, key_projection_weight,
    value_projection_weight, w_out, ffn_gain, w_gate, w_up, w_down, out_grad,
):
    parts = lax.axis_size("expert")
    section = lax.axis_index("section")
    z = lax.axis_index("expert")
    z_at = z.reshape(1)
    dp = lax.axis_index("dp")
    dp_place = jnp.stack([dp // (PAIR * CORES), dp // CORES % PAIR, dp % CORES])
    batches, own, width = block_input.shape
    rows = parts * own
    wq, wk, wv, wo = w_query[0], key_projection_weight[0], value_projection_weight[0], w_out[0]
    local_experts, units = w_gate.shape[1], w_gate.shape[3]

    wg = lax.all_gather(w_gate[0], "dp", axis=1, tiled=True)
    wu = lax.all_gather(w_up[0], "dp", axis=1, tiled=True)
    wd = lax.all_gather(w_down[0], "dp", axis=1, tiled=True)

    start = gather_group(block_input)
    labels = gather_group(segments)
    numbers = jnp.arange(parts * local_experts, dtype=jnp.int32)
    hits = expert_ids[0][..., None] == numbers
    shares_own = jnp.sum(jnp.where(hits, route_weights[0][..., None], 0.0), 2)
    shares = gather_group(shares_own).reshape(batches * rows, parts, local_experts)
    share = lax.dynamic_index_in_dim(shares, z, 1, keepdims=False).T[..., None]
    block = jnp.arange(parts, dtype=jnp.int32)[:, None]
    place = ((z - block) % parts * own + jnp.arange(own, dtype=jnp.int32)[None, :]).reshape(rows)
    marks = (place[:, None], place[None, :], labels[:, :, None], labels[:, None, :])
    half = HEAD_SIZE // 2
    frequency = 10000.0 ** (-jnp.arange(half, dtype=F32) * 2.0 / HEAD_SIZE)
    angles = place.astype(F32)[:, None] * frequency[None, :]
    cos_half, sin_half = jnp.cos(angles), jnp.sin(angles)
    cos = jnp.concatenate([cos_half] * 4, -1)
    sin = jnp.concatenate([-sin_half, sin_half] * 2, -1)
    cos_all, sin_all = jnp.concatenate([cos] * batches, 0), jnp.concatenate([sin] * batches, 0)

    def attention(x):
        qkv, xn = project(x.reshape(batches * rows, width), attn_gain, wq, wk, wv, cos_all, sin_all)
        qkv = qkv.reshape(batches, rows, -1)
        mixed, h1, xn2 = attend(qkv, x, wo, ffn_gain, marks, parts, own)
        return qkv, xn, mixed, h1, xn2.reshape(batches * rows, width)

    _, _, _, h1, xn2 = attention(start)
    partial = experts_forward(xn2, share, wg, wu, wd).reshape(batches, rows, width)
    result = (h1 + sum_to_owners(partial, own)).astype(LOW)
    received = gather_group(to_section(result, 1))

    x = jnp.where(section == 0, start, received)
    qkv, xn, mixed, h1, xn2 = attention(x)
    hidden, to_up, to_gate = experts_keep(xn2, share, wg, wu)

    def backward(c, c_own, keep):
        partial, *kept = experts_backward(c.reshape(batches * rows, width), to_up, to_gate, wg, wu, wd, keep)
        normed_grad = sum_to_owners(partial.reshape(batches, rows, width), own)
        norm_part, ffn_grad = norm_back(normed_grad, h1, ffn_gain)
        after = c_own.astype(F32) + norm_part
        da = gather_group(after.astype(LOW))
        dqkv, dn = attend_backward(z_at, qkv, da, wo, wq, wk, wv, marks, cos, sin, parts)
        dn_own = sum_to_owners(dn, own)
        norm_part, attn_grad = norm_back(dn_own, x[:, :own].astype(F32), attn_gain)
        return after + norm_part, da, dqkv, ffn_grad, attn_grad, kept

    c_second = gather_group(out_grad)
    input_grad = backward(c_second, out_grad, False)[0]
    received_own = to_section(input_grad.astype(LOW), 0)

    partial = dot(hidden, wd.reshape(local_experts * units, width)).astype(LOW).reshape(batches, rows, width)
    layer_outputs = (h1 + sum_to_owners(partial, own)).astype(LOW)

    c_own = jnp.where(section == 1, out_grad, received_own)
    c = jnp.where(section == 1, c_second, gather_group(received_own))
    input_grad, da, dqkv, ffn_grad, attn_grad, (gate_grad, up_grad) = backward(c, c_own, True)

    flat_c = c.reshape(batches * rows, width)

    def to_owners(left, right, cut):
        mine_ring, other_ring, mine_pair, other_pair = expert_grad(dp_place, left, right, local_experts, cut)
        ring = added(mine_ring, moved(other_ring, core=1)).astype(LOW)
        pair = added(mine_pair, moved(other_pair, core=1)).astype(LOW)
        return jnp.concatenate([ring_first_sum(ring), pair_first_sum(pair)], 0)

    w_down_grad = to_owners(hidden, flat_c, width // units)
    w_gate_grad = to_owners(xn2, gate_grad, 1)
    w_up_grad = to_owners(xn2, up_grad, 1)
    w_down_grad = w_down_grad.reshape(local_experts, width // units, -1, units)
    w_down_grad = jnp.swapaxes(w_down_grad, 1, 2).reshape(local_experts, -1, width)

    mine, other = dense_grad(dp_place, z_at, mixed.reshape(batches * rows, -1), da.reshape(batches * rows, width), parts, True)
    share_out = ring_first_sum(added(mine, moved(other, core=1)).astype(LOW)).astype(LOW)
    mine = group_stack(pair_gather(ring_gather(share_out)))
    mine = jnp.reshape(mine, (parts, PAIR, RING) + share_out.shape)
    w_out_grad = out_of_layout(dp_place, z_at, mine, moved(mine, core=1))

    mine, other = dense_grad(dp_place, z_at, xn, dqkv.reshape(batches * rows, -1), parts, False)
    share_in = ring_first_sum(added(mine, moved(other, core=1)).astype(LOW)).astype(LOW)
    mine = pair_gather(group_stack(share_in))
    mine = ring_gather(jnp.moveaxis(mine, 2, 0))
    mine = jnp.transpose(mine, (3, 2, 0, 1, 4, 5))
    w_query_grad, w_key_grad, w_value_grad = into_layout(
        dp_place, z_at, mine, moved(mine, core=1), (wq.shape, wk.shape, wv.shape)
    )
    gains = sum_everywhere(jnp.stack([attn_grad, ffn_grad]))
    return (
        layer_outputs[None],
        input_grad[None],
        gains[0:1],
        w_query_grad[None],
        w_key_grad[None],
        w_value_grad[None],
        w_out_grad[None],
        gains[1:2],
        w_gate_grad[None],
        w_up_grad[None],
        w_down_grad[None],
    )


def solution(mesh):
    tokens = P(None, ("dp", "expert"), None)
    layered = P("section", None, ("dp", "expert"), None)
    vector = P("section", None)
    matrix = P("section", None, None)
    expert = P("section", "expert", "dp", None)
    return jax.shard_map(
        local,
        mesh=mesh,
        in_specs=(
            tokens, P(None, ("dp", "expert")), layered, layered, vector, matrix, matrix, matrix, matrix,
            vector, expert, expert, expert, tokens,
        ),
        out_specs=(layered, layered, vector, matrix, matrix, matrix, matrix, vector, expert, expert, expert),
        check_vma=False,
    )
```

```python
import functools

import jax
import jax.numpy as jnp
from jax import lax
from jax.experimental import pallas as pl
from jax.experimental.pallas import tpu as pltpu
from jax.sharding import PartitionSpec as P

QUERY_HEADS = 24
KEY_VALUE_HEADS = 8
HEAD_SIZE = 64
GROUP = QUERY_HEADS // KEY_VALUE_HEADS
EPS = 1e-06
LOW = jnp.bfloat16
F32 = jnp.float32
MIB = 1024 * 1024
TINY = pl.CostEstimate(flops=1, bytes_accessed=1, transcendentals=0)


def params(*semantics, mib=30):
    return pltpu.CompilerParams(dimension_semantics=semantics, vmem_limit_bytes=mib * MIB)


def dot(left, right):
    return jnp.dot(left, right, preferred_element_type=F32)


def dot_nt(left, right):
    return lax.dot_general(left, right, (((1,), (1,)), ((), ())), preferred_element_type=F32)


def dot_tn(left, right):
    return lax.dot_general(left, right, (((0,), (0,)), ((), ())), preferred_element_type=F32)


def shifted(block, by):
    size = lax.axis_size("expert")
    return lax.ppermute(block, "expert", [(i, (i + by) % size) for i in range(size)])


def spread_group(block):
    return [block] + [shifted(block, j) for j in range(1, lax.axis_size("expert"))]


def gather_group(block):
    return jnp.concatenate(spread_group(block), 1)


def sum_to_owners(blocks):
    size = len(blocks)
    return added(blocks[0], *[shifted(blocks[j], size - j) for j in range(1, size)])


def to_section(block, target):
    return lax.ppermute(block, "section", [(1 - target, target)])


RING, PAIR, CORES = 4, 2, 2


def moved(block, x=0, y=0, core=0):
    route = []
    for i in range(RING):
        for j in range(PAIR):
            for k in range(CORES):
                target = ((i + x) % RING * PAIR + (j + y) % PAIR) * CORES + (k + core) % CORES
                route.append(((i * PAIR + j) * CORES + k, target))
    return lax.ppermute(block, "dp", route)


def added(*terms):
    total = terms[0].astype(F32)
    for term in terms[1:]:
        total = total + term.astype(F32)
    return total


def ring_step(blocks):
    return moved(blocks[:, 3:5], x=1), moved(blocks[:, 5:7], x=-1)


def ring_next(blocks, step):
    from_below, from_above = step
    below = moved(added(blocks[:, 2], from_below[:, 1]).astype(LOW), x=1)
    above = moved(added(blocks[:, 7], from_above[:, 0]).astype(LOW), x=-1)
    return below, above


def ring_end(blocks, step, last):
    first = added(blocks[:, 0], step[1][:, 1], last[0])
    return jnp.stack([first, added(blocks[:, 1], step[0][:, 0], last[1])])


def ring_gather_step(block):
    return moved(block, x=1), moved(block, x=-1)


def ring_gather_next(step):
    return moved(step[0][0], x=1), moved(step[1][1], x=-1)


def group_gather_step(block):
    return shifted(block, 1), shifted(block, 3)


def group_gather_next(step):
    return shifted(step[0][0], 1), shifted(step[1][1], 3)


def ring_stack(block, step, last):
    return jnp.stack([block, step[0], jnp.stack(last), step[1]])


def by_lanes(block):
    lanes = block.shape[-1] // 2
    return jnp.stack([block[..., :lanes], block[..., lanes:]])


def exchanged(values, axis, bit):
    return lax.ppermute(values, axis, [(i, i ^ bit) for i in range(lax.axis_size(axis))])


def hold(*values):
    return lax.optimization_barrier(values)


def swap_halves(values):
    half = HEAD_SIZE // 2
    lanes = values.shape[-1]
    lane = lax.broadcasted_iota(jnp.int32, values.shape, values.ndim - 1)
    ahead = pltpu.roll(values, lanes - half, values.ndim - 1)
    behind = pltpu.roll(values, half, values.ndim - 1)
    return jnp.where(lane % HEAD_SIZE < half, ahead, behind)


def widen_table(table, lanes):
    return jnp.concatenate([table] * (lanes // table.shape[-1]), -1)


def project_kernel(query_steps, x_ref, gain_ref, wq_ref, wk_ref, wv_ref, cos_ref, sin_ref, out_ref, xn_ref):
    step = pl.program_id(0)

    @pl.when(step == 0)
    def _():
        wide = x_ref[...].astype(F32)
        scale = lax.rsqrt(jnp.mean(wide * wide, -1, keepdims=True) + EPS)
        xn_ref[...] = (wide * scale * gain_ref[...]).astype(LOW)

    def turned(weight):
        product = dot(xn_ref[...], weight)
        lanes = product.shape[-1]
        cos, sin = widen_table(cos_ref[...], lanes), widen_table(sin_ref[...], lanes)
        return (product * cos + swap_halves(product) * sin).astype(LOW)

    @pl.when(step < query_steps)
    def _():
        out_ref[...] = turned(wq_ref[...])

    @pl.when(step == query_steps)
    def _():
        out_ref[...] = turned(wk_ref[...])

    @pl.when(step == query_steps + 1)
    def _():
        out_ref[...] = dot(xn_ref[...], wv_ref[...]).astype(LOW)


def project(x, gain, wq, wk, wv, cos, sin):
    rows, width = x.shape
    lanes = wk.shape[1]
    query_steps = wq.shape[1] // lanes
    whole = lambda *shape: pl.BlockSpec(shape, lambda i: (0,) * len(shape))
    return pl.pallas_call(
        functools.partial(project_kernel, query_steps),
        grid=(query_steps + 2,),
        in_specs=[
            whole(rows, width),
            whole(1, width),
            pl.BlockSpec((width, lanes), lambda i: (0, jnp.minimum(i, query_steps - 1))),
            whole(width, lanes),
            whole(width, lanes),
            whole(rows, cos.shape[1]),
            whole(rows, cos.shape[1]),
        ],
        out_specs=[pl.BlockSpec((rows, lanes), lambda i: (0, i)), whole(rows, width)],
        out_shape=[
            jax.ShapeDtypeStruct((rows, lanes * (query_steps + 2)), LOW),
            jax.ShapeDtypeStruct((rows, width), LOW),
        ],
        compiler_params=params("arbitrary"),
        cost_estimate=TINY,
        name="project",
    )(x, gain, wq, wk, wv, cos, sin)


def head(values, index):
    return values[:, index * HEAD_SIZE : (index + 1) * HEAD_SIZE]


def softmax_parts(stacked_q, key, bias):
    scores = dot_nt(stacked_q, key) * 0.125 + bias
    raised = jnp.exp(scores - jnp.max(scores, -1, keepdims=True))
    return raised * (1.0 / jnp.sum(raised, -1, keepdims=True))


def attend_kernel(q_ref, k_ref, v_ref, bias_ref, o_ref):
    bias = bias_ref[0]
    q, k, v = q_ref[0] * jnp.asarray(0.125, LOW), k_ref[0], v_ref[0]
    mixed = []
    for pair in range(k.shape[1] // HEAD_SIZE):
        key, value = head(k, pair), head(v, pair)
        for j in range(GROUP):
            scores = dot_nt(head(q, pair * GROUP + j), key) + bias
            raised = jnp.exp(scores - jnp.max(scores, -1, keepdims=True))
            total = jnp.sum(raised, -1, keepdims=True)
            mixed.append(dot(raised.astype(LOW), value) * (1.0 / total))
    o_ref[0] = jnp.concatenate(mixed, -1).astype(LOW)


def attend(qkv, bias, parts):
    batches, rows, lanes = qkv.shape
    k_lanes = KEY_VALUE_HEADS * HEAD_SIZE // parts
    q_lanes = k_lanes * GROUP
    k_at = parts * GROUP
    return pl.pallas_call(
        attend_kernel,
        grid=(batches, parts),
        in_specs=[
            pl.BlockSpec((1, rows, q_lanes), lambda b, c: (b, 0, c)),
            pl.BlockSpec((1, rows, k_lanes), lambda b, c: (b, 0, k_at + c)),
            pl.BlockSpec((1, rows, k_lanes), lambda b, c: (b, 0, k_at + parts + c)),
            pl.BlockSpec((1, rows, rows), lambda b, c: (b, 0, 0)),
        ],
        out_specs=pl.BlockSpec((1, rows, q_lanes), lambda b, c: (b, 0, c)),
        out_shape=jax.ShapeDtypeStruct((batches, rows, q_lanes * parts), LOW),
        compiler_params=params("arbitrary", "arbitrary"),
        cost_estimate=TINY,
        name="attend",
    )(qkv, qkv, qkv, bias)


def join_kernel(o_ref, x_ref, wo_ref, gain_ref, h1_ref, xn2_ref):
    total = x_ref[0].astype(F32) + dot(o_ref[0], wo_ref[...])
    scale = lax.rsqrt(jnp.mean(total * total, -1, keepdims=True) + EPS)
    h1_ref[0] = total[: h1_ref.shape[1]]
    xn2_ref[0] = (total * scale * gain_ref[...]).astype(LOW)


def join(o, x, wo, gain, own):
    batches, rows, width = x.shape
    batch = lambda *shape: pl.BlockSpec((1,) + shape, lambda b: (b, 0, 0))
    whole = lambda *shape: pl.BlockSpec(shape, lambda b: (0, 0))
    return pl.pallas_call(
        join_kernel,
        grid=(batches,),
        in_specs=[batch(rows, wo.shape[0]), batch(rows, width), whole(*wo.shape), whole(1, width)],
        out_specs=[batch(own, width), batch(rows, width)],
        out_shape=[
            jax.ShapeDtypeStruct((batches, own, width), F32),
            jax.ShapeDtypeStruct((batches, rows, width), LOW),
        ],
        compiler_params=params("arbitrary"),
        cost_estimate=TINY,
        name="join",
    )(o, x, wo, gain)


def expert_hidden(xn_ref, share_ref, wg_ref, wu_ref):
    gate, up = dot(xn_ref[...], wg_ref[0]), dot(xn_ref[...], wu_ref[0])
    share = share_ref[0]
    sigma = jax.nn.sigmoid(gate)
    silu = gate * sigma
    return gate, up, share, sigma, silu


def accumulate(total_ref, part):
    step = pl.program_id(0)

    @pl.when(step == 0)
    def _():
        total_ref[...] = part

    @pl.when(step > 0)
    def _():
        total_ref[...] += part


def hand_out(total_ref, out_refs):
    @pl.when(pl.program_id(0) == pl.num_programs(0) - 1)
    def _():
        batches, own, _ = out_refs[0].shape
        for b in range(batches):
            for j, ref in enumerate(out_refs):
                at = (b * len(out_refs) + j) * own
                ref[b] = total_ref[at : at + own].astype(LOW)


def experts_forward_kernel(place_ref, xn_ref, share_ref, *refs):
    pieces, out_refs = refs[:12], refs[12:-4]
    wg_ref, wu_ref, wd_ref, total_ref = refs[-4:]
    step = pl.program_id(0)
    high = wg_ref.shape[1] // (RING * PAIR * CORES)
    low = wd_ref.shape[1] // (RING * PAIR * CORES)

    def lay(block, x, y, core):
        ring = lax.rem(place_ref[0] + RING - x, RING)
        pair = lax.rem(place_ref[1] + y, PAIR)
        at = (ring * PAIR + pair) * CORES + lax.rem(place_ref[2] + core, CORES)
        rows = pl.ds(pl.multiple_of(at * high, high), high)
        wg_ref[0, rows] = block[0]
        wu_ref[0, rows] = block[1]
        outer = [block[2][k * low : (k + 1) * low] for k in range(high // low)]
        wd_ref[0, pl.ds(pl.multiple_of(at * low, low), low)] = jnp.concatenate(outer, -1)

    @pl.when(step < 2)
    def _():
        for core in range(CORES):
            for ref, xs in zip(pieces[core * 6 : core * 6 + 2], ((0, 1, 3), (2,))):
                for i, x in enumerate(xs):
                    for y in range(PAIR):
                        lay([ref[i, 0, y, k] for k in range(3)], x, y, core)

    @pl.when(step >= 2)
    def _():
        for core in range(CORES):
            for n, ref in enumerate(pieces[core * 6 + 2 : core * 6 + 6]):
                for i, x in enumerate((0, 1, 3) if n % 2 == 0 else (2,)):
                    lay([ref[i, 0, k] for k in range(3)], x, n // 2, core)

    _, up, share, _, silu = expert_hidden(xn_ref, share_ref, wg_ref, wu_ref)
    accumulate(total_ref, dot((silu * up * share).astype(LOW), wd_ref[0]))
    hand_out(total_ref, out_refs)


def experts_forward(place, xn, share, pieces, batches, parts):
    rows, width = xn.shape
    count = share.shape[0]
    high, units = pieces[0].shape[-2:]
    specs = []
    for piece in pieces:
        shape = (piece.shape[0], 1) + piece.shape[2:]
        near = len(shape) == 6
        index = lambda e, p, near=near, n=len(shape) - 2: (0, jnp.minimum(e, 1) if near else jnp.maximum(e - 2, 0)) + (0,) * n
        specs.append(pl.BlockSpec(shape, index))
    block = (batches, rows // batches // parts, width)
    matrix = lambda *shape: pl.BlockSpec((1,) + shape, lambda e, p: (e, 0, 0))
    return pl.pallas_call(
        experts_forward_kernel,
        grid_spec=pltpu.PrefetchScalarGridSpec(
            num_scalar_prefetch=1,
            grid=(count,),
            in_specs=[
                pl.BlockSpec((rows, width), lambda e, p: (0, 0)),
                pl.BlockSpec((1, rows, 1), lambda e, p: (e, 0, 0)),
            ]
            + specs,
            out_specs=[pl.BlockSpec(block, lambda e, p: (0, 0, 0))] * parts
            + [matrix(width, units), matrix(width, units), matrix(units, width)],
            scratch_shapes=[pltpu.VMEM((rows, width), F32)],
        ),
        out_shape=[jax.ShapeDtypeStruct(block, LOW)] * parts
        + [jax.ShapeDtypeStruct((count,) + shape, LOW) for shape in ((width, units), (width, units), (units, width))],
        compiler_params=params("arbitrary", mib=44),
        cost_estimate=TINY,
        name="experts_forward",
    )(place, xn, share, *pieces)


def experts_turn_kernel(xn_ref, share_ref, c_ref, wg_ref, wu_ref, wd_ref, hidden_ref, to_up_ref, to_gate_ref, *refs):
    gate, up, share, sigma, silu = expert_hidden(xn_ref, share_ref, wg_ref, wu_ref)
    shared = silu * share
    hidden_ref[...] = (shared * up).astype(LOW)
    to_up = shared.astype(LOW)
    to_gate = (share * up * sigma * (1.0 + gate * (1.0 - sigma))).astype(LOW)
    to_up_ref[...] = to_up
    to_gate_ref[...] = to_gate
    grads = dot_nt(c_ref[...], wd_ref[0])
    gate_grad = (grads * to_gate.astype(F32)).astype(LOW)
    up_grad = (grads * to_up.astype(F32)).astype(LOW)
    accumulate(refs[-1], dot_nt(gate_grad, wg_ref[0]) + dot_nt(up_grad, wu_ref[0]))
    hand_out(refs[-1], refs[:-1])


def experts_turn(xn, share, c, wg, wu, wd, batches, parts):
    rows, width = xn.shape
    count, _, units = wg.shape
    kept = pl.BlockSpec((rows, units), lambda e: (0, e))
    block = (batches, rows // batches // parts, width)
    return pl.pallas_call(
        experts_turn_kernel,
        grid=(count,),
        in_specs=[
            pl.BlockSpec((rows, width), lambda e: (0, 0)),
            pl.BlockSpec((1, rows, 1), lambda e: (e, 0, 0)),
            pl.BlockSpec((rows, width), lambda e: (0, 0)),
            pl.BlockSpec((1, width, units), lambda e: (e, 0, 0)),
            pl.BlockSpec((1, width, units), lambda e: (e, 0, 0)),
            pl.BlockSpec((1, units, width), lambda e: (e, 0, 0)),
        ],
        out_specs=[kept] * 3 + [pl.BlockSpec(block, lambda e: (0, 0, 0))] * parts,
        out_shape=[jax.ShapeDtypeStruct((rows, units * count), LOW)] * 3 + [jax.ShapeDtypeStruct(block, LOW)] * parts,
        scratch_shapes=[pltpu.VMEM((rows, width), F32)],
        compiler_params=params("arbitrary", mib=36),
        cost_estimate=TINY,
        name="experts_turn",
    )(xn, share, c, wg, wu, wd)


def experts_backward_kernel(c_ref, up_ref, gate_ref, wg_ref, wu_ref, wd_ref, *refs):
    total_ref = refs[-1]
    hidden = dot_nt(c_ref[...], wd_ref[0])
    gate_grad = (hidden * gate_ref[...].astype(F32)).astype(LOW)
    up_grad = (hidden * up_ref[...].astype(F32)).astype(LOW)
    refs[-2][0] = gate_grad
    refs[-2][1] = up_grad
    accumulate(total_ref, dot_nt(gate_grad, wg_ref[0]) + dot_nt(up_grad, wu_ref[0]))
    hand_out(total_ref, refs[:-2])


def experts_backward(c, to_up, to_gate, wg, wu, wd, batches, parts):
    rows, width = c.shape
    count, _, units = wg.shape
    kept = pl.BlockSpec((rows, units), lambda e: (0, e))
    block = (batches, rows // batches // parts, width)
    return pl.pallas_call(
        experts_backward_kernel,
        grid=(count,),
        in_specs=[
            pl.BlockSpec((rows, width), lambda e: (0, 0)),
            kept,
            kept,
            pl.BlockSpec((1, width, units), lambda e: (e, 0, 0)),
            pl.BlockSpec((1, width, units), lambda e: (e, 0, 0)),
            pl.BlockSpec((1, units, width), lambda e: (e, 0, 0)),
        ],
        out_specs=[pl.BlockSpec(block, lambda e: (0, 0, 0))] * parts
        + [pl.BlockSpec((2, rows, units), lambda e: (0, 0, e))],
        out_shape=[jax.ShapeDtypeStruct(block, LOW)] * parts
        + [jax.ShapeDtypeStruct((2, rows, units * count), LOW)],
        scratch_shapes=[pltpu.VMEM((rows, width), F32)],
        compiler_params=params("arbitrary"),
        cost_estimate=TINY,
        name="experts_backward",
    )(c, to_up, to_gate, wg, wu, wd)


def head_grads(queries, key, value, douts, bias):
    probs = softmax_parts(queries, key, bias)
    dprobs = dot_nt(douts, value)
    centre = jnp.sum(probs * dprobs, -1, keepdims=True)
    dscores = (probs * (dprobs - centre) * 0.125).astype(LOW)
    return dot(dscores, key), dot_tn(dscores, queries), dot_tn(probs.astype(LOW), douts)


def stacked_heads(values, pair):
    return jnp.concatenate([head(values, pair * GROUP + j) for j in range(GROUP)], 0)


def chunk_grads(q, k, v, dout, bias):
    rows = q.shape[0]
    bias = jnp.concatenate([bias] * GROUP, 0)
    dqs, dks, dvs = [], [], []
    for pair in range(k.shape[1] // HEAD_SIZE):
        dquery, dkey, dvalue = head_grads(stacked_heads(q, pair), head(k, pair), head(v, pair), stacked_heads(dout, pair), bias)
        dqs += [dquery[j * rows : (j + 1) * rows] for j in range(GROUP)]
        dks.append(dkey)
        dvs.append(dvalue)
    return jnp.concatenate(dqs, -1), jnp.concatenate(dks, -1), jnp.concatenate(dvs, -1).astype(LOW)


def turned_back(grads, cos, sin):
    lanes = grads.shape[-1]
    return (grads * widen_table(cos, lanes) + swap_halves(grads * widen_table(sin, lanes))).astype(LOW)


def attend_backward_kernel(
    z_ref, q_ref, k_ref, v_ref, da_ref, wo_ref, wq_ref, wk_ref, wv_ref, bias_ref, cos_ref, sin_ref, dqkv_ref, dn_ref
):
    dout = dot_nt(da_ref[0], wo_ref[...]).astype(LOW)
    dq, dk, dv = chunk_grads(q_ref[0], k_ref[0], v_ref[0], dout, bias_ref[0])
    dq, dk = turned_back(dq, cos_ref[...], sin_ref[...]), turned_back(dk, cos_ref[...], sin_ref[...])
    dqkv_ref[0] = jnp.concatenate([dq, dk, dv], -1)
    dn = dot_nt(dq, wq_ref[...]) + dot_nt(dk, wk_ref[...]) + dot_nt(dv, wv_ref[...])
    parts, _, own, _ = dn_ref.shape
    for j in range(parts):
        dn_ref[lax.rem(z_ref[0] + parts - j, parts), 0] = dn[j * own : (j + 1) * own].astype(LOW)


def attend_backward(z, qkv, da, wo, wq, wk, wv, bias, cos, sin, parts):
    batches, rows, width = da.shape
    q_lanes, k_lanes = wo.shape[0] // parts, KEY_VALUE_HEADS * HEAD_SIZE // parts
    k_at = wo.shape[0] // k_lanes
    full = lambda *shape: pl.BlockSpec(shape, lambda b, z: (0,) * len(shape))
    batch = lambda *shape: pl.BlockSpec((1,) + shape, lambda b, z: (b, 0, 0))
    columns = lambda lanes: pl.BlockSpec((width, lanes), lambda b, z: (0, z[0]))
    return pl.pallas_call(
        attend_backward_kernel,
        grid_spec=pltpu.PrefetchScalarGridSpec(
            num_scalar_prefetch=1,
            grid=(batches,),
            in_specs=[
                pl.BlockSpec((1, rows, q_lanes), lambda b, z: (b, 0, z[0])),
                pl.BlockSpec((1, rows, k_lanes), lambda b, z: (b, 0, k_at + z[0])),
                pl.BlockSpec((1, rows, k_lanes), lambda b, z: (b, 0, k_at + parts + z[0])),
                batch(rows, width),
                pl.BlockSpec((q_lanes, width), lambda b, z: (z[0], 0)),
                columns(q_lanes),
                columns(k_lanes),
                columns(k_lanes),
                batch(rows, rows),
                full(rows, cos.shape[1]),
                full(rows, cos.shape[1]),
            ],
            out_specs=[
                batch(rows, q_lanes + 2 * k_lanes),
                pl.BlockSpec((parts, 1, rows // parts, width), lambda b, z: (0, b, 0, 0)),
            ],
        ),
        out_shape=[
            jax.ShapeDtypeStruct((batches, rows, q_lanes + 2 * k_lanes), LOW),
            jax.ShapeDtypeStruct((parts, batches, rows // parts, width), LOW),
        ],
        compiler_params=params("arbitrary"),
        cost_estimate=TINY,
        name="attend_backward",
    )(z, qkv, qkv, qkv, da, wo, wq, wk, wv, bias, cos, sin)


def own_backward_kernel(q_ref, k_ref, v_ref, da_ref, wo_ref, bias_ref, cos_ref, sin_ref, dq_ref, *out_refs):
    batches, own, _ = q_ref.shape
    da = jnp.concatenate([da_ref[b] for b in range(batches)], 0)
    dout = dot_nt(da, wo_ref[...]).astype(LOW)
    lanes = k_ref.shape[-1]
    at = pl.multiple_of(pl.program_id(0) * lanes, lanes)
    middle = out_refs[0].shape[-1] // 2
    for b in range(batches):
        dq, dk, dv = chunk_grads(q_ref[b], k_ref[b], v_ref[b], dout[b * own : (b + 1) * own], bias_ref[b])
        dq_ref[b] = turned_back(dq, cos_ref[:own], sin_ref[:own])
        dk = turned_back(dk, cos_ref[...], sin_ref[...])
        for j, ref in enumerate(out_refs):
            ref[b, :, pl.ds(at, lanes)] = dk[j * own : (j + 1) * own]
            ref[b, :, pl.ds(middle + at, lanes)] = dv[j * own : (j + 1) * own]


def own_backward(qkv, da, wo, bias, cos, sin, parts):
    batches, own, width = da.shape
    rows = qkv.shape[1]
    k_lanes = KEY_VALUE_HEADS * HEAD_SIZE // parts
    q_lanes = k_lanes * GROUP
    k_at = parts * GROUP
    full = lambda *shape: pl.BlockSpec(shape, lambda c: (0,) * len(shape))
    block = (batches, own, 2 * k_lanes * parts)
    return pl.pallas_call(
        own_backward_kernel,
        grid=(parts,),
        in_specs=[
            pl.BlockSpec((batches, own, q_lanes), lambda c: (0, 0, c)),
            pl.BlockSpec((batches, rows, k_lanes), lambda c: (0, 0, k_at + c)),
            pl.BlockSpec((batches, rows, k_lanes), lambda c: (0, 0, k_at + parts + c)),
            full(batches, own, width),
            pl.BlockSpec((q_lanes, width), lambda c: (c, 0)),
            full(batches, own, rows),
            full(rows, cos.shape[1]),
            full(rows, cos.shape[1]),
        ],
        out_specs=[pl.BlockSpec((batches, own, q_lanes), lambda c: (0, 0, c))] + [full(*block)] * parts,
        out_shape=[jax.ShapeDtypeStruct((batches, own, q_lanes * parts), LOW)] + [jax.ShapeDtypeStruct(block, LOW)] * parts,
        compiler_params=params("arbitrary"),
        cost_estimate=TINY,
        name="own_backward",
    )(qkv, qkv, qkv, da, wo, bias, cos, sin)


def chip_block(place_ref, x, y, core):
    ring = lax.rem(place_ref[0] + x, RING)
    pair = lax.rem(place_ref[1] + y, PAIR)
    return (ring * PAIR + pair) * CORES + lax.rem(place_ref[2] + core, CORES)


def expert_grad_kernel(cut, place_ref, left_ref, right_ref, mine_ref, other_ref, turned_ref):
    rows = mine_ref.shape[-2] // cut
    lanes = mine_ref.shape[-1]
    step = pl.program_id(1)
    if cut == 1:

        @pl.when((pl.program_id(0) == 0) & (step == 0))
        def _():
            turned_ref[...] = left_ref[...].T

        product = dot(turned_ref[...], right_ref[0]).astype(LOW)
    else:
        product = dot_tn(left_ref[...], right_ref[0]).astype(LOW)
    half = lax.rem(step, 2)

    def place(refs, ring_first):
        for i in range(RING):
            x = lax.rem(i + RING - place_ref[0], RING)
            for j in range(PAIR):
                y = lax.rem(j + PAIR - place_ref[1], PAIR)
                index = (x * 2 + half) * PAIR + y if ring_first else (y * RING + x) * 2 + half
                for core in range(CORES):
                    at = ((i * PAIR + j) * CORES + core) * rows
                    for part in range(cut):
                        value = product[at : at + rows, part * lanes : (part + 1) * lanes]
                        refs[core][0, 0, index, part * rows : (part + 1) * rows] = value

    for core in range(CORES):
        for ring_first in (True, False):

            @pl.when((place_ref[2] == core) & ((step < 2) == ring_first))
            def _(core=core, ring_first=ring_first):
                place((mine_ref, other_ref) if core == 0 else (other_ref, mine_ref), ring_first)


def expert_grad(place, left, right, count, cut):
    number, rows, _ = right.shape
    left_lanes = left.shape[1] // count if cut > 1 else left.shape[1]
    right_lanes = right.shape[2] if cut > 1 else right.shape[2] // count
    owners = RING * PAIR * CORES
    high, lanes = left_lanes // owners, right_lanes // cut
    shape = (2, owners, high * cut, lanes)
    out = pl.BlockSpec((1, 1) + shape[1:], lambda r, e, p: (r, e // 2, 0, 0, 0))
    left_spec = pl.BlockSpec((rows, left_lanes), lambda r, e, p: (0, e if cut > 1 else 0))
    right_spec = pl.BlockSpec((1, rows, right_lanes), lambda r, e, p: (r, 0, 0 if cut > 1 else e))
    return pl.pallas_call(
        functools.partial(expert_grad_kernel, cut),
        grid_spec=pltpu.PrefetchScalarGridSpec(
            num_scalar_prefetch=1,
            grid=(number, count),
            in_specs=[left_spec, right_spec],
            out_specs=[out, out],
            scratch_shapes=[pltpu.VMEM((left_lanes, rows) if cut == 1 else (16, 128), LOW)],
        ),
        out_shape=[jax.ShapeDtypeStruct((number,) + shape, LOW)] * 2,
        compiler_params=params("arbitrary", "arbitrary"),
        name="expert_grad",
    )(place, left, right)


def dense_grad_kernel(
    place_ref, z_ref, mixed_ref, da_ref, xn_ref, dqkv_ref, mine_ref, other_ref, into_ref, out_of_ref
):
    del z_ref
    high = mine_ref.shape[-2]
    lanes, wide = out_of_ref.shape[-1], dqkv_ref.shape[1]
    into = dot_tn(xn_ref[...], dqkv_ref[...]).astype(LOW)
    out_of = dot_tn(mixed_ref[...], da_ref[...]).astype(LOW)
    for chip in range(RING * PAIR):
        for core in range(CORES):
            owner = chip * CORES + core
            for half in range(2):
                at = (owner * 2 + half) * high
                into_ref[owner, half] = into[at : at + high]
                at = (half * CORES + core) * lanes
                out_of_ref[owner, half] = out_of[chip * high : (chip + 1) * high, at : at + lanes]
    for core, ref in enumerate((mine_ref, other_ref)):
        for x in range(RING):
            for y in range(PAIR):
                owner = chip_block(place_ref, x, y, core)
                for half in range(2):
                    ref[0, x * 2 + half, y, :, :wide] = into_ref[owner, half]
                    ref[0, x * 2 + half, y, :, wide:] = out_of_ref[owner, half]


def dense_grad(place, z, mixed, da, xn, dqkv, parts):
    rows, width = xn.shape
    owners = RING * PAIR * CORES
    q_lanes, wide = mixed.shape[1] // parts, dqkv.shape[1]
    high, lanes = width // owners // 2, width // CORES // 2
    shape = (1, 2 * RING, PAIR, high, wide + lanes)
    whole = lambda columns: pl.BlockSpec((rows, columns), lambda i, p, z: (0, 0))
    return pl.pallas_call(
        dense_grad_kernel,
        grid_spec=pltpu.PrefetchScalarGridSpec(
            num_scalar_prefetch=2,
            grid=(1,),
            in_specs=[
                pl.BlockSpec((rows, q_lanes), lambda i, p, z: (0, z[0])),
                whole(width),
                whole(width),
                whole(wide),
            ],
            out_specs=[pl.BlockSpec(shape, lambda i, p, z: (0,) * 5)] * 2,
            scratch_shapes=[pltpu.VMEM((owners, 2, high, wide), LOW), pltpu.VMEM((owners, 2, high, lanes), LOW)],
        ),
        out_shape=[jax.ShapeDtypeStruct(shape, LOW)] * 2,
        compiler_params=params("arbitrary"),
        cost_estimate=TINY,
        name="dense_grad",
    )(place, z, mixed, da, xn, dqkv)


def dense_layout_kernel(by_x, place_ref, z_ref, mine_ref, other_ref, *refs):
    outs = refs[-4:]
    parts = mine_ref.shape[3] if by_x else mine_ref.shape[0]
    wide = mine_ref.shape[-1]
    for core, ref in enumerate((mine_ref, other_ref)):
        to_core = lax.rem(place_ref[2] + core, CORES)
        for y in range(PAIR):
            to_y = lax.rem(place_ref[1] + y, PAIR)
            for k in range(parts):
                at = lax.rem(z_ref[0] + parts - k, parts)
                start = 0
                for out in outs:
                    to_rows = out is outs[3]
                    lanes = out.shape[-1] // (CORES if to_rows else parts)
                    by, begin = divmod(start, wide)
                    index = (0, by, y, k) if by_x else (k, by, y, 0)
                    value = ref[index + (slice(None), slice(begin, begin + lanes))].astype(F32)
                    if to_rows:
                        out[at, 0, to_y, :, pl.ds(pl.multiple_of(to_core * lanes, 128), lanes)] = value
                    else:
                        out[0, to_y, to_core, 0, :, pl.ds(pl.multiple_of(at * lanes, 128), lanes)] = value
                    start += lanes


def dense_layout(place, z, half, mine, other, shapes, before):
    by_x = half == 0
    high, lanes = mine.shape[-2:]
    parts = mine.shape[3] if by_x else mine.shape[0]
    if by_x:
        source = pl.BlockSpec((1, 2, PAIR, parts, high, lanes), lambda x, p, z: (x, 0, 0, 0, 0, 0))
    else:
        source = pl.BlockSpec((parts, 2, PAIR, 1, high, lanes), lambda x, p, z: (0, 0, 0, x, 0, 0))
    ring = lambda x, p: lax.rem(p[0] + RING - x, RING)
    width = shapes[3][1]
    shapes = [(RING, PAIR, CORES, 2, high, shape[1]) for shape in shapes[:3]] + [(parts, RING, PAIR, high, width)]
    out_specs = [
        pl.BlockSpec((1, PAIR, CORES, 1, high, shape[-1]), lambda x, p, z: (ring(x, p), 0, 0, half, 0, 0)) for shape in shapes[:3]
    ] + [pl.BlockSpec((parts, 1, PAIR, high, width // 2), lambda x, p, z: (0, ring(x, p), 0, 0, half))]
    return pl.pallas_call(
        functools.partial(dense_layout_kernel, by_x),
        grid_spec=pltpu.PrefetchScalarGridSpec(
            num_scalar_prefetch=2,
            grid=(RING,),
            in_specs=[source, source] + [pl.BlockSpec(memory_space=pl.ANY)] * len(before),
            out_specs=out_specs,
        ),
        out_shape=[jax.ShapeDtypeStruct(shape, F32) for shape in shapes],
        input_output_aliases={4 + i: i for i in range(len(before))},
        compiler_params=params("arbitrary"),
        cost_estimate=pl.CostEstimate(flops=0, bytes_accessed=24 * mine.size, transcendentals=0),
        name="dense_layout",
    )(place, z, mine, other, *before)


def norm_back(grad_normed, values, gain):
    scale = lax.rsqrt(jnp.mean(values * values, -1, keepdims=True) + EPS)
    scaled = grad_normed * gain
    gain_grad = jnp.sum(grad_normed * values * scale, (0, 1))
    inner = jnp.mean(scaled * values, -1, keepdims=True)
    return (scale * scaled - values * scale * scale * scale * inner, gain_grad)


def local(
    block_input, segments, expert_ids, route_weights, attn_gain, w_query, key_projection_weight,
    value_projection_weight, w_out, ffn_gain, w_gate, w_up, w_down, out_grad,
):
    parts = lax.axis_size("expert")
    section = lax.axis_index("section")
    z = lax.axis_index("expert")
    z_at = z.reshape(1)
    dp = lax.axis_index("dp")
    dp_place = jnp.stack([dp // (PAIR * CORES), dp // CORES % PAIR, dp % CORES])
    batches, own, width = block_input.shape
    rows = parts * own
    wq, wk, wv, wo = w_query[0], key_projection_weight[0], value_projection_weight[0], w_out[0]
    local_experts, units = w_gate.shape[1], w_gate.shape[3]

    outer = w_down[0].reshape(local_experts, -1, width // units, units)
    outer = jnp.swapaxes(outer, 1, 2).reshape(w_gate[0].shape)
    shard = jnp.stack([w_gate[0], w_up[0], outer], 1)
    near, far = shard[:2], shard[2:]
    numbers = jnp.arange(parts * local_experts, dtype=jnp.int32)
    hits = expert_ids[0][..., None] == numbers
    shares = jnp.sum(jnp.where(hits, route_weights[0][..., None], 0.0), 2)
    shares = jnp.concatenate([shares, segments.astype(F32)[..., None]], -1)
    start = spread_group(block_input)
    near_y = moved(near, y=1)
    far_1 = ring_gather_step(far)
    shares = spread_group(shares)
    start, near_y, far_1, shares = hold(start, near_y, far_1, shares)

    start = jnp.concatenate(start, 1)
    shares = jnp.concatenate(shares, 1)
    labels = shares[..., -1]
    shares = shares[..., :-1].reshape(batches * rows, parts, local_experts)
    share = lax.dynamic_index_in_dim(shares, z, 1, keepdims=False).T[..., None]
    block = jnp.arange(parts, dtype=jnp.int32)[:, None]
    place = ((z - block) % parts * own + jnp.arange(own, dtype=jnp.int32)[None, :]).reshape(rows)
    allowed = (place[None, None, :] <= place[None, :, None]) & (labels[:, None, :] == labels[:, :, None])
    bias = jnp.where(allowed, 0.0, -1e30).astype(F32)
    half = HEAD_SIZE // 2
    frequency = 10000.0 ** (-jnp.arange(half, dtype=F32) * 2.0 / HEAD_SIZE)
    angles = place.astype(F32)[:, None] * frequency[None, :]
    cos_half, sin_half = jnp.cos(angles), jnp.sin(angles)
    cos = jnp.concatenate([cos_half] * 4, -1)
    sin = jnp.concatenate([-sin_half, sin_half] * 2, -1)
    cos_all, sin_all = jnp.concatenate([cos] * batches, 0), jnp.concatenate([sin] * batches, 0)

    def attention_in(x):
        qkv, xn = project(x.reshape(batches * rows, width), attn_gain, wq, wk, wv, cos_all, sin_all)
        return qkv.reshape(batches, rows, -1), xn

    def attention_out(qkv, x):
        mixed = attend(qkv, bias, parts)
        h1, xn2 = join(mixed, x, wo, ffn_gain, own)
        return mixed.reshape(batches * rows, -1), h1, xn2.reshape(batches * rows, width)

    near = jnp.stack([near, near_y], 1)
    near_1 = ring_gather_step(near)
    far_2 = ring_gather_next(far_1)
    far_a = jnp.stack([far, *far_1])
    far_ya = moved(far_a, y=1)
    qkv, _ = attention_in(start)
    _, h1, xn2 = attention_out(qkv, start)

    xn2, near_1, far_2, far_ya = hold(xn2, near_1, far_2, far_ya)
    near_a = jnp.stack([near, *near_1])
    near_b = ring_gather_next(near_1)
    far_b = jnp.stack(far_2)[None]
    far_yb = moved(far_b, y=1)
    others = [moved(piece, core=1) for piece in (near_a, far_a, far_b, far_ya)]

    near_b, far_yb, others = hold(near_b, far_yb, others)
    near_b = jnp.stack(near_b)[None]
    others = [others[0], moved(near_b, core=1), *others[1:], moved(far_yb, core=1)]
    pieces = [near_a, near_b, far_a, far_b, far_ya, far_yb, *others]
    *blocks, wg, wu, wd = experts_forward(dp_place, xn2, share, pieces, batches, parts)
    c_second = lax.all_gather(out_grad, "expert")
    c_second = jnp.concatenate([lax.dynamic_index_in_dim(c_second, (z + parts - j) % parts, 0, False) for j in range(parts)], 1)
    result = (h1 + sum_to_owners(blocks)).astype(LOW)
    received = gather_group(to_section(result, 1))

    x = jnp.where(section == 0, start, received)
    qkv, xn = attention_in(x)
    mixed, h1, xn2 = attention_out(qkv, x)
    flat_second = c_second.reshape(batches * rows, width)
    hidden, to_up, to_gate, *blocks = experts_turn(xn2, share, flat_second, wg, wu, wd, batches, parts)

    def after_experts(blocks, c_own):
        norm_part, ffn_grad = norm_back(sum_to_owners(blocks), h1, ffn_gain)
        return c_own.astype(F32) + norm_part, ffn_grad

    def after_attention(after, dn_own):
        norm_part, attn_grad = norm_back(dn_own, x[:, :own].astype(F32), attn_gain)
        return after + norm_part, attn_grad

    outputs = dot(hidden, wd.reshape(local_experts * units, width)).astype(LOW).reshape(batches, parts, own, width)
    outputs = jnp.flip(jnp.moveaxis(outputs, 1, 0), 0)
    outputs = lax.dynamic_slice_in_dim(jnp.concatenate([outputs, outputs], 0), (2 * parts - 1 - z) % parts, parts, 0)
    after, _ = after_experts(blocks, out_grad)
    after, outputs = hold(after, outputs)
    dq, *blocks = own_backward(qkv, after.astype(LOW), wo, bias, cos, sin, parts)
    dn_own = dot_nt(dq.reshape(batches * own, -1), wq)
    dkv = sum_to_owners(blocks).astype(LOW).reshape(batches * own, -1)
    dn_own = dn_own + dot_nt(dkv[:, : wk.shape[1]], wk) + dot_nt(dkv[:, wk.shape[1] :], wv)
    input_grad, _ = after_attention(after, dn_own.reshape(batches, own, width))
    received_own = to_section(input_grad.astype(LOW), 0)

    c_own = jnp.where(section == 1, out_grad, received_own)
    c = jnp.where(section == 1, c_second, gather_group(received_own))
    flat_c = c.reshape(batches * rows, width)
    *blocks, hidden_grads = experts_backward(flat_c, to_up, to_gate, wg, wu, wd, batches, parts)
    after, ffn_grad = after_experts(blocks, c_own)
    both = [
        expert_grad(dp_place, xn2, hidden_grads, local_experts, 1),
        expert_grad(dp_place, hidden, flat_c[None], local_experts, width // units),
    ]
    after, both = hold(after, both)
    both = [(mine, moved(other, core=1)) for mine, other in both]
    da = gather_group(after.astype(LOW))
    by_ring, by_pair = (
        jnp.concatenate([added(mine[:, kind], other[:, kind]).astype(LOW) for mine, other in both], 0) for kind in range(2)
    )
    by_ring = by_ring.reshape((-1, 2 * RING, PAIR) + by_ring.shape[2:])
    by_pair = by_pair.reshape((-1, PAIR, 2 * RING) + by_pair.shape[2:])
    da, by_ring, by_pair = hold(da, by_ring, by_pair)

    ring_1 = ring_step(by_ring)
    pair_1 = [moved(by_pair[:, 1, :RING], y=1), moved(by_pair[:, 1, RING:], y=1)]
    dqkv, dn = attend_backward(z_at, qkv, da, wo, wq, wk, wv, bias, cos, sin, parts)
    mine, other = dense_grad(
        dp_place, z_at, mixed, da.reshape(batches * rows, width), xn, dqkv.reshape(batches * rows, -1), parts
    )
    dn_own = lax.psum_scatter(dn, "expert", scatter_dimension=0, tiled=True)[0].astype(F32)

    mine, other, ring_1, pair_1[0] = hold(mine, other, ring_1, pair_1[0])
    dense = added(mine, moved(other, core=1)).astype(LOW)

    (dense,) = hold(dense)
    dense_1 = ring_step(dense)

    dense_1, dn_own = hold(dense_1, dn_own)
    dense_2 = ring_next(dense, dense_1)
    ring_2 = ring_next(by_ring, ring_1)
    input_grad, attn_grad = after_attention(after, dn_own)
    gains = jnp.stack([attn_grad, ffn_grad])
    gains = gains + exchanged(gains, "expert", 1)

    dense_2, gains, ring_2 = hold(dense_2, gains, ring_2)
    dense = ring_end(dense, dense_1, dense_2)[:, 0]
    dense_3 = moved(dense[:, 1].astype(LOW), y=1)
    gains = gains + exchanged(gains, "expert", 2)
    ring_sums = ring_end(by_ring, ring_1, ring_2)

    dense_3, gains, ring_sums, pair_1 = hold(dense_3, gains, ring_sums, pair_1)
    owned = added(dense[:, 0], dense_3).astype(LOW)
    first, second = owned[0], by_lanes(owned[1])
    first_1 = [shifted(first, k) for k in range(1, parts)]
    second_1 = [moved(second, x=k) for k in range(1, RING)]
    pair_sums = added(by_pair[:, 0], jnp.concatenate(pair_1, 1)).astype(LOW)

    first_1, second_1, pair_sums = hold(first_1, second_1, pair_sums)
    first = jnp.stack([first] + first_1)
    first_2 = moved(first, y=1)
    second = jnp.stack([second] + second_1)
    second_2 = moved(second, y=1)
    pair_2 = ring_step(pair_sums)
    gains = gains + exchanged(gains, "dp", 1)

    first_2, second_2, gains, pair_2 = hold(first_2, second_2, gains, pair_2)
    first = by_lanes(jnp.stack([first, first_2]))
    first_3 = ring_gather_step(first)
    second = jnp.moveaxis(jnp.stack([second, second_2]), 2, 0)
    second_3 = group_gather_step(second)
    ring_away = moved(ring_sums[:, :, 1].astype(LOW), y=1)
    gains = gains + exchanged(gains, "dp", 2)

    first_3, second_3, ring_away, gains = hold(first_3, second_3, ring_away, gains)
    first_4 = ring_gather_next(first_3)
    second_4 = group_gather_next(second_3)
    pair_3 = ring_next(pair_sums, pair_2)
    ring_sums = added(ring_sums[:, :, 0], ring_away)

    first_4, second_4, pair_3, ring_sums = hold(first_4, second_4, pair_3, ring_sums)
    first = ring_stack(first, first_3, first_4)
    first_other = moved(first, core=1)
    pair_sums = ring_end(pair_sums, pair_2, pair_3)
    gains = gains + exchanged(gains, "dp", 4)

    second = ring_stack(second, second_3, second_4)
    second, first_other, gains, pair_sums = hold(second, first_other, gains, pair_sums)
    second_other = moved(second, core=1)
    shapes = (wq.shape, wk.shape, wv.shape, wo.shape)
    laid = dense_layout(dp_place, z_at, 0, first, first_other, shapes, ())
    gains = gains + exchanged(gains, "dp", 8)
    w_gate_grad, w_up_grad, w_down_grad = (jnp.concatenate([ring_sums[:, i], pair_sums[:, i]], 0) for i in range(3))
    w_down_grad = w_down_grad.reshape(local_experts, width // units, -1, units)
    w_down_grad = jnp.swapaxes(w_down_grad, 1, 2).reshape(local_experts, -1, width)

    second_other, laid = hold(second_other, laid)
    laid = dense_layout(dp_place, z_at, 1, second, second_other, shapes, laid)
    w_query_grad, w_key_grad, w_value_grad, w_out_grad = (
        grad.reshape(weight.shape) for grad, weight in zip(laid, (wq, wk, wv, wo))
    )

    outputs, dqkv = hold(outputs, dqkv)
    outputs = lax.psum_scatter(outputs, "expert", scatter_dimension=0, tiled=True)[0]
    layer_outputs = (h1 + outputs.astype(F32)).astype(LOW)
    return (
        layer_outputs[None],
        input_grad[None],
        gains[0:1],
        w_query_grad[None],
        w_key_grad[None],
        w_value_grad[None],
        w_out_grad[None],
        gains[1:2],
        w_gate_grad[None],
        w_up_grad[None],
        w_down_grad[None],
    )


def solution(mesh):
    tokens = P(None, ("dp", "expert"), None)
    layered = P("section", None, ("dp", "expert"), None)
    vector = P("section", None)
    matrix = P("section", None, None)
    expert = P("section", "expert", "dp", None)
    return jax.shard_map(
        local,
        mesh=mesh,
        in_specs=(
            tokens, P(None, ("dp", "expert")), layered, layered, vector, matrix, matrix, matrix, matrix,
            vector, expert, expert, expert, tokens,
        ),
        out_specs=(layered, layered, vector, matrix, matrix, matrix, matrix, vector, expert, expert, expert),
        check_vma=False,
    )
```

```python
import functools

import jax
import jax.numpy as jnp
from jax import lax
from jax.experimental import pallas as pl
from jax.experimental.pallas import tpu as pltpu
from jax.sharding import PartitionSpec as P

QUERY_HEADS = 24
KEY_VALUE_HEADS = 8
HEAD_SIZE = 64
GROUP = QUERY_HEADS // KEY_VALUE_HEADS
EPS = 1e-06
LOW = jnp.bfloat16
F32 = jnp.float32
MIB = 1024 * 1024


def params(*semantics, mib=30):
    return pltpu.CompilerParams(dimension_semantics=semantics, vmem_limit_bytes=mib * MIB)


def dot(left, right):
    return jnp.dot(left, right, preferred_element_type=F32)


def dot_nt(left, right):
    return lax.dot_general(left, right, (((1,), (1,)), ((), ())), preferred_element_type=F32)


def dot_tn(left, right):
    return lax.dot_general(left, right, (((0,), (0,)), ((), ())), preferred_element_type=F32)


def shifted(block, by):
    size = lax.axis_size("expert")
    return lax.ppermute(block, "expert", [(i, (i + by) % size) for i in range(size)])


def spread_group(block):
    return [block] + [shifted(block, j) for j in range(1, lax.axis_size("expert"))]


def gather_group(block):
    return jnp.concatenate(spread_group(block), 1)


def owners_step(blocks):
    size = len(blocks)
    return [blocks[0]] + [shifted(blocks[j], size - j) for j in range(1, size)]


def to_section(block, target):
    return lax.ppermute(block, "section", [(1 - target, target)])


RING, PAIR, CORES = 4, 2, 2


def moved(block, x=0, y=0, core=0):
    route = []
    for i in range(RING):
        for j in range(PAIR):
            for k in range(CORES):
                target = ((i + x) % RING * PAIR + (j + y) % PAIR) * CORES + (k + core) % CORES
                route.append(((i * PAIR + j) * CORES + k, target))
    return lax.ppermute(block, "dp", route)


def added(*terms):
    total = terms[0].astype(F32)
    for term in terms[1:]:
        total = total + term.astype(F32)
    return total


def ring_step(blocks):
    return moved(blocks[:, 3:5], x=1), moved(blocks[:, 5:7], x=-1)


def ring_next(blocks, step):
    from_below, from_above = step
    below = moved(added(blocks[:, 2], from_below[:, 1]).astype(LOW), x=1)
    above = moved(added(blocks[:, 7], from_above[:, 0]).astype(LOW), x=-1)
    return below, above


def ring_end(blocks, step, last):
    first = added(blocks[:, 0], step[1][:, 1], last[0])
    return jnp.stack([first, added(blocks[:, 1], step[0][:, 0], last[1])])


def ring_gather_step(block):
    return moved(block, x=1), moved(block, x=-1)


def ring_gather_next(step):
    return moved(step[0][0], x=1), moved(step[1][1], x=-1)


def group_gather_step(block):
    return shifted(block, 1), shifted(block, 3)


def group_gather_next(step):
    return shifted(step[0][0], 1), shifted(step[1][1], 3)


def ring_stack(block, step, last):
    return jnp.stack([block, step[0], jnp.stack(last), step[1]])


def by_lanes(block):
    lanes = block.shape[-1] // 2
    return jnp.stack([block[..., :lanes], block[..., lanes:]])


def exchanged(values, axis, bit):
    return lax.ppermute(values, axis, [(i, i ^ bit) for i in range(lax.axis_size(axis))])


def hold(*values):
    return lax.optimization_barrier(values)


def once(values, *earlier):
    return hold(values, *earlier)[0]


def swap_halves(values):
    half = HEAD_SIZE // 2
    lanes = values.shape[-1]
    lane = lax.broadcasted_iota(jnp.int32, values.shape, values.ndim - 1)
    ahead = pltpu.roll(values, lanes - half, values.ndim - 1)
    behind = pltpu.roll(values, half, values.ndim - 1)
    return jnp.where(lane % HEAD_SIZE < half, ahead, behind)


def widen_table(table, lanes):
    return jnp.concatenate([table] * (lanes // table.shape[-1]), -1)


def project_kernel(query_steps, x_ref, gain_ref, wq_ref, wk_ref, wv_ref, cos_ref, sin_ref, out_ref, xn_ref):
    step = pl.program_id(0)

    @pl.when(step == 0)
    def _():
        wide = x_ref[...].astype(F32)
        scale = lax.rsqrt(jnp.mean(wide * wide, -1, keepdims=True) + EPS)
        xn_ref[...] = (wide * scale * gain_ref[...]).astype(LOW)

    def turned(weight):
        product = dot(xn_ref[...], weight)
        lanes = product.shape[-1]
        cos, sin = widen_table(cos_ref[...], lanes), widen_table(sin_ref[...], lanes)
        return (product * cos + swap_halves(product) * sin).astype(LOW)

    @pl.when(step < query_steps)
    def _():
        out_ref[...] = turned(wq_ref[...])

    @pl.when(step == query_steps)
    def _():
        out_ref[...] = turned(wk_ref[...])

    @pl.when(step == query_steps + 1)
    def _():
        out_ref[...] = dot(xn_ref[...], wv_ref[...]).astype(LOW)


def project(x, gain, wq, wk, wv, cos, sin):
    rows, width = x.shape
    lanes = wk.shape[1]
    query_steps = wq.shape[1] // lanes
    whole = lambda *shape: pl.BlockSpec(shape, lambda i: (0,) * len(shape))
    return pl.pallas_call(
        functools.partial(project_kernel, query_steps),
        grid=(query_steps + 2,),
        in_specs=[
            whole(rows, width),
            whole(1, width),
            pl.BlockSpec((width, lanes), lambda i: (0, jnp.minimum(i, query_steps - 1))),
            whole(width, lanes),
            whole(width, lanes),
            whole(rows, cos.shape[1]),
            whole(rows, cos.shape[1]),
        ],
        out_specs=[pl.BlockSpec((rows, lanes), lambda i: (0, i)), whole(rows, width)],
        out_shape=[
            jax.ShapeDtypeStruct((rows, lanes * (query_steps + 2)), LOW),
            jax.ShapeDtypeStruct((rows, width), LOW),
        ],
        compiler_params=params("arbitrary"),
        name="project",
    )(x, gain, wq, wk, wv, cos, sin)


def head(values, index):
    return values[:, index * HEAD_SIZE : (index + 1) * HEAD_SIZE]


def softmax_parts(stacked_q, key, bias):
    scores = dot_nt(stacked_q, key) * 0.125 + bias
    raised = jnp.exp(scores - jnp.max(scores, -1, keepdims=True))
    return raised * (1.0 / jnp.sum(raised, -1, keepdims=True))


def attend_kernel(q_ref, k_ref, v_ref, bias_ref, o_ref):
    bias = bias_ref[0]
    q, k, v = q_ref[0] * jnp.asarray(0.125, LOW), k_ref[0], v_ref[0]
    mixed = []
    for pair in range(k.shape[1] // HEAD_SIZE):
        key, value = head(k, pair), head(v, pair)
        for j in range(GROUP):
            scores = dot_nt(head(q, pair * GROUP + j), key) + bias
            raised = jnp.exp(scores - jnp.max(scores, -1, keepdims=True))
            total = jnp.sum(raised, -1, keepdims=True)
            mixed.append(dot(raised.astype(LOW), value) * (1.0 / total))
    o_ref[0] = jnp.concatenate(mixed, -1).astype(LOW)


def attend(qkv, bias, parts):
    batches, rows, lanes = qkv.shape
    k_lanes = KEY_VALUE_HEADS * HEAD_SIZE // parts
    q_lanes = k_lanes * GROUP
    k_at = parts * GROUP
    return pl.pallas_call(
        attend_kernel,
        grid=(batches, parts),
        in_specs=[
            pl.BlockSpec((1, rows, q_lanes), lambda b, c: (b, 0, c)),
            pl.BlockSpec((1, rows, k_lanes), lambda b, c: (b, 0, k_at + c)),
            pl.BlockSpec((1, rows, k_lanes), lambda b, c: (b, 0, k_at + parts + c)),
            pl.BlockSpec((1, rows, rows), lambda b, c: (b, 0, 0)),
        ],
        out_specs=pl.BlockSpec((1, rows, q_lanes), lambda b, c: (b, 0, c)),
        out_shape=jax.ShapeDtypeStruct((batches, rows, q_lanes * parts), LOW),
        compiler_params=params("arbitrary", "arbitrary"),
        name="attend",
    )(qkv, qkv, qkv, bias)


def join_kernel(o_ref, x_ref, wo_ref, gain_ref, h1_ref, xn2_ref):
    total = x_ref[0].astype(F32) + dot(o_ref[0], wo_ref[...])
    scale = lax.rsqrt(jnp.mean(total * total, -1, keepdims=True) + EPS)
    h1_ref[0] = total[: h1_ref.shape[1]]
    xn2_ref[0] = (total * scale * gain_ref[...]).astype(LOW)


def join(o, x, wo, gain, own):
    batches, rows, width = x.shape
    batch = lambda *shape: pl.BlockSpec((1,) + shape, lambda b: (b, 0, 0))
    whole = lambda *shape: pl.BlockSpec(shape, lambda b: (0, 0))
    return pl.pallas_call(
        join_kernel,
        grid=(batches,),
        in_specs=[batch(rows, wo.shape[0]), batch(rows, width), whole(*wo.shape), whole(1, width)],
        out_specs=[batch(own, width), batch(rows, width)],
        out_shape=[
            jax.ShapeDtypeStruct((batches, own, width), F32),
            jax.ShapeDtypeStruct((batches, rows, width), LOW),
        ],
        compiler_params=params("arbitrary"),
        name="join",
    )(o, x, wo, gain)


def expert_hidden(xn_ref, share_ref, wg_ref, wu_ref):
    gate, up = dot(xn_ref[...], wg_ref[0]), dot(xn_ref[...], wu_ref[0])
    share = share_ref[0]
    sigma = jax.nn.sigmoid(gate)
    silu = gate * sigma
    return gate, up, share, sigma, silu


def accumulate(total_ref, part):
    step = pl.program_id(0)

    @pl.when(step == 0)
    def _():
        total_ref[...] = part

    @pl.when(step > 0)
    def _():
        total_ref[...] += part


def hand_out(total_ref, out_refs):
    @pl.when(pl.program_id(0) == pl.num_programs(0) - 1)
    def _():
        batches, own, _ = out_refs[0].shape
        for b in range(batches):
            for j, ref in enumerate(out_refs):
                at = (b * len(out_refs) + j) * own
                ref[b] = total_ref[at : at + own].astype(LOW)


def experts_forward_kernel(place_ref, xn_ref, share_ref, *refs):
    pieces, out_refs = refs[:12], refs[12:-4]
    wg_ref, wu_ref, wd_ref, total_ref = refs[-4:]
    step = pl.program_id(0)
    high = wg_ref.shape[1] // (RING * PAIR * CORES)
    low = wd_ref.shape[1] // (RING * PAIR * CORES)

    def lay(block, x, y, core):
        ring = lax.rem(place_ref[0] + RING - x, RING)
        pair = lax.rem(place_ref[1] + y, PAIR)
        at = (ring * PAIR + pair) * CORES + lax.rem(place_ref[2] + core, CORES)
        rows = pl.ds(pl.multiple_of(at * high, high), high)
        wg_ref[0, rows] = block[0]
        wu_ref[0, rows] = block[1]
        outer = [block[2][k * low : (k + 1) * low] for k in range(high // low)]
        wd_ref[0, pl.ds(pl.multiple_of(at * low, low), low)] = jnp.concatenate(outer, -1)

    @pl.when(step < 2)
    def _():
        for core in range(CORES):
            near_a, near_b = pieces[core * 6 : core * 6 + 2]
            for y in range(PAIR):
                for i, x in enumerate((0, 1, 3)):
                    lay([near_a[i, y, 0, k] for k in range(3)], x, y, core)
                lay([near_b[0, y, k] for k in range(3)], 2, y, core)

    @pl.when(step >= 2)
    def _():
        for core in range(CORES):
            for n, ref in enumerate(pieces[core * 6 + 2 : core * 6 + 6]):
                for i, x in enumerate((0, 1, 3) if n % 2 == 0 else (2,)):
                    lay([ref[(i, 0, k) if n % 2 == 0 else (0, k)] for k in range(3)], x, n // 2, core)

    _, up, share, _, silu = expert_hidden(xn_ref, share_ref, wg_ref, wu_ref)
    accumulate(total_ref, dot((silu * up * share).astype(LOW), wd_ref[0]))
    hand_out(total_ref, out_refs)


def experts_forward(place, xn, share, pieces, batches, own, parts):
    rows, width = xn.shape
    count = share.shape[0]
    high, units = pieces[0].shape[-2:]
    tile = (3, high, units)
    near, far = (lambda e: jnp.minimum(e, 1)), (lambda e: jnp.maximum(e - 2, 0))
    specs = [
        pl.BlockSpec((3, PAIR, 1) + tile, lambda e, p: (0, 0, near(e), 0, 0, 0)),
        pl.BlockSpec((1, PAIR) + tile, lambda e, p: (near(e), 0, 0, 0, 0)),
        pl.BlockSpec((3, 1) + tile, lambda e, p: (0, far(e), 0, 0, 0)),
        pl.BlockSpec((1,) + tile, lambda e, p: (far(e), 0, 0, 0)),
    ]
    specs = (specs + specs[2:]) * CORES
    block = (1, own, width)
    matrix = lambda *shape: pl.BlockSpec((1,) + shape, lambda e, p: (e, 0, 0))
    return pl.pallas_call(
        experts_forward_kernel,
        grid_spec=pltpu.PrefetchScalarGridSpec(
            num_scalar_prefetch=1,
            grid=(count,),
            in_specs=[
                pl.BlockSpec((rows, width), lambda e, p: (0, 0)),
                pl.BlockSpec((1, rows, 1), lambda e, p: (e, 0, 0)),
            ]
            + specs,
            out_specs=[pl.BlockSpec(block, lambda e, p: (0, 0, 0))] * parts * batches
            + [matrix(width, units), matrix(width, units), matrix(units, width)],
            scratch_shapes=[pltpu.VMEM((rows, width), F32)],
        ),
        out_shape=[jax.ShapeDtypeStruct(block, LOW)] * parts * batches
        + [jax.ShapeDtypeStruct((count,) + shape, LOW) for shape in ((width, units), (width, units), (units, width))],
        compiler_params=params("arbitrary", mib=44),
        name="experts_forward",
    )(place, xn, share, *pieces)


def expert_specs(rows, width, units, batch):
    return [
        pl.BlockSpec((1, rows, 1), lambda e: (e, batch, 0)),
        pl.BlockSpec((1, width, units), lambda e: (e, 0, 0)),
        pl.BlockSpec((1, width, units), lambda e: (e, 0, 0)),
        pl.BlockSpec((1, units, width), lambda e: (e, 0, 0)),
    ]


def experts_turn_kernel(xn_ref, c_ref, share_ref, wg_ref, wu_ref, wd_ref, hidden_ref, to_up_ref, to_gate_ref, *refs):
    gate, up, share, sigma, silu = expert_hidden(xn_ref, share_ref, wg_ref, wu_ref)
    shared = silu * share
    hidden_ref[...] = (shared * up).astype(LOW)
    to_up = shared.astype(LOW)
    to_gate = (share * up * sigma * (1.0 + gate * (1.0 - sigma))).astype(LOW)
    to_up_ref[...] = to_up
    to_gate_ref[...] = to_gate
    grads = dot_nt(c_ref[...], wd_ref[0])
    gate_grad = (grads * to_gate.astype(F32)).astype(LOW)
    up_grad = (grads * to_up.astype(F32)).astype(LOW)
    accumulate(refs[-1], dot_nt(gate_grad, wg_ref[0]) + dot_nt(up_grad, wu_ref[0]))
    hand_out(refs[-1], refs[:-1])


def experts_turn(xn, c, share, wg, wu, wd, batch, own, parts):
    rows, width = xn.shape
    count, _, units = wg.shape
    kept = pl.BlockSpec((rows, units), lambda e: (0, e))
    block = (1, own, width)
    return pl.pallas_call(
        experts_turn_kernel,
        grid=(count,),
        in_specs=[
            pl.BlockSpec((rows, width), lambda e: (0, 0)),
            pl.BlockSpec((rows, width), lambda e: (batch, 0)),
        ]
        + expert_specs(rows, width, units, batch),
        out_specs=[kept] * 3 + [pl.BlockSpec(block, lambda e: (0, 0, 0))] * parts,
        out_shape=[jax.ShapeDtypeStruct((rows, units * count), LOW)] * 3 + [jax.ShapeDtypeStruct(block, LOW)] * parts,
        scratch_shapes=[pltpu.VMEM((rows, width), F32)],
        compiler_params=params("arbitrary", mib=56),
        name="experts_turn",
    )(xn, c, share, wg, wu, wd)


def experts_backward_kernel(batches, *refs):
    c_refs, up_refs, gate_refs = (refs[i * batches : (i + 1) * batches] for i in range(3))
    wg_ref, wu_ref, wd_ref, *out_refs = refs[3 * batches : -3]
    kept_ref, total_ref, c_ref = refs[-3:]

    @pl.when(pl.program_id(0) == 0)
    def _():
        c_ref[...] = jnp.concatenate([ref[...] for ref in c_refs], 0)

    hidden = dot_nt(c_ref[...], wd_ref[0])
    gate_grad = (hidden * jnp.concatenate([ref[...] for ref in gate_refs], 0).astype(F32)).astype(LOW)
    up_grad = (hidden * jnp.concatenate([ref[...] for ref in up_refs], 0).astype(F32)).astype(LOW)
    kept_ref[0] = gate_grad
    kept_ref[1] = up_grad
    accumulate(total_ref, dot_nt(gate_grad, wg_ref[0]) + dot_nt(up_grad, wu_ref[0]))
    hand_out(total_ref, out_refs)


def experts_backward(c, to_up, to_gate, wg, wu, wd, own, parts):
    batches = len(c)
    rows, width = c[0].shape
    count, _, units = wg.shape
    kept = pl.BlockSpec((rows, units), lambda e: (0, e))
    block = (batches, own, width)
    return pl.pallas_call(
        functools.partial(experts_backward_kernel, batches),
        grid=(count,),
        in_specs=[pl.BlockSpec((rows, width), lambda e: (0, 0))] * batches
        + [kept] * 2 * batches
        + [
            pl.BlockSpec((1, width, units), lambda e: (e, 0, 0)),
            pl.BlockSpec((1, width, units), lambda e: (e, 0, 0)),
            pl.BlockSpec((1, units, width), lambda e: (e, 0, 0)),
        ],
        out_specs=[pl.BlockSpec(block, lambda e: (0, 0, 0))] * parts
        + [pl.BlockSpec((2, batches * rows, units), lambda e: (0, 0, e))],
        out_shape=[jax.ShapeDtypeStruct(block, LOW)] * parts
        + [jax.ShapeDtypeStruct((2, batches * rows, units * count), LOW)],
        scratch_shapes=[pltpu.VMEM((batches * rows, width), F32), pltpu.VMEM((batches * rows, width), LOW)],
        compiler_params=params("arbitrary", mib=34),
        name="experts_backward",
    )(*c, *to_up, *to_gate, wg, wu, wd)


def head_grads(queries, key, value, douts, bias):
    probs = softmax_parts(queries, key, bias)
    dprobs = dot_nt(douts, value)
    centre = jnp.sum(probs * dprobs, -1, keepdims=True)
    dscores = (probs * (dprobs - centre) * 0.125).astype(LOW)
    return dot(dscores, key), dot_tn(dscores, queries), dot_tn(probs.astype(LOW), douts)


def stacked_heads(values, pair):
    return jnp.concatenate([head(values, pair * GROUP + j) for j in range(GROUP)], 0)


def chunk_grads(q, k, v, dout, bias):
    rows = q.shape[0]
    bias = jnp.concatenate([bias] * GROUP, 0)
    dqs, dks, dvs = [], [], []
    for pair in range(k.shape[1] // HEAD_SIZE):
        dquery, dkey, dvalue = head_grads(stacked_heads(q, pair), head(k, pair), head(v, pair), stacked_heads(dout, pair), bias)
        dqs += [dquery[j * rows : (j + 1) * rows] for j in range(GROUP)]
        dks.append(dkey)
        dvs.append(dvalue)
    return jnp.concatenate(dqs, -1), jnp.concatenate(dks, -1), jnp.concatenate(dvs, -1).astype(LOW)


def turned_back(grads, cos, sin):
    lanes = grads.shape[-1]
    return (grads * widen_table(cos, lanes) + swap_halves(grads * widen_table(sin, lanes))).astype(LOW)


def attend_backward_kernel(batches, parts, z_ref, *refs):
    q_refs, k_refs, v_refs = (refs[i * batches : (i + 1) * batches] for i in range(3))
    da_refs = refs[3 * batches : 3 * batches + parts]
    wo_ref, wq_ref, wk_ref, wv_ref, bias_ref, cos_ref, sin_ref, dqkv_ref, dn_ref = refs[3 * batches + parts :]

    def turn(q_ref, k_ref, v_ref):
        da = jnp.concatenate([ref[0] for ref in da_refs], 0)
        dout = dot_nt(da, wo_ref[...]).astype(LOW)
        dq, dk, dv = chunk_grads(q_ref[0], k_ref[0], v_ref[0], dout, bias_ref[0])
        dq, dk = turned_back(dq, cos_ref[...], sin_ref[...]), turned_back(dk, cos_ref[...], sin_ref[...])
        dqkv_ref[...] = jnp.concatenate([dq, dk, dv], -1)
        dn = dot_nt(dq, wq_ref[...]) + dot_nt(dk, wk_ref[...]) + dot_nt(dv, wv_ref[...])
        own = dn_ref.shape[2]
        for j in range(parts):
            dn_ref[lax.rem(z_ref[0] + parts - j, parts), 0] = dn[j * own : (j + 1) * own].astype(LOW)

    for b in range(batches):

        @pl.when(pl.program_id(0) == b)
        def _(b=b):
            turn(q_refs[b], k_refs[b], v_refs[b])


def attend_backward(z, qkv, da, wo, wq, wk, wv, bias, cos, sin, parts):
    batches, rows = len(qkv), qkv[0].shape[1]
    _, own, width = da[0].shape
    q_lanes, k_lanes = wo.shape[0] // parts, KEY_VALUE_HEADS * HEAD_SIZE // parts
    k_at = wo.shape[0] // k_lanes
    full = lambda *shape: pl.BlockSpec(shape, lambda b, z: (0,) * len(shape))
    batch = lambda *shape: pl.BlockSpec((1,) + shape, lambda b, z: (b, 0, 0))
    columns = lambda lanes: pl.BlockSpec((width, lanes), lambda b, z: (0, z[0]))
    return pl.pallas_call(
        functools.partial(attend_backward_kernel, batches, parts),
        grid_spec=pltpu.PrefetchScalarGridSpec(
            num_scalar_prefetch=1,
            grid=(batches,),
            in_specs=[pl.BlockSpec((1, rows, q_lanes), lambda b, z: (0, 0, z[0]))] * batches
            + [pl.BlockSpec((1, rows, k_lanes), lambda b, z: (0, 0, k_at + z[0]))] * batches
            + [pl.BlockSpec((1, rows, k_lanes), lambda b, z: (0, 0, k_at + parts + z[0]))] * batches
            + [batch(own, width)] * parts
            + [
                pl.BlockSpec((q_lanes, width), lambda b, z: (z[0], 0)),
                columns(q_lanes),
                columns(k_lanes),
                columns(k_lanes),
                batch(rows, rows),
                full(rows, cos.shape[1]),
                full(rows, cos.shape[1]),
            ],
            out_specs=[
                pl.BlockSpec((rows, q_lanes + 2 * k_lanes), lambda b, z: (b, 0)),
                pl.BlockSpec((parts, 1, own, width), lambda b, z: (0, b, 0, 0)),
            ],
        ),
        out_shape=[
            jax.ShapeDtypeStruct((batches * rows, q_lanes + 2 * k_lanes), LOW),
            jax.ShapeDtypeStruct((parts, batches, own, width), LOW),
        ],
        compiler_params=params("arbitrary", mib=56),
        name="attend_backward",
    )(z, *qkv, *qkv, *qkv, *da, wo, wq, wk, wv, bias, cos, sin)


def own_backward_kernel(q_ref, k_ref, v_ref, da_ref, wo_ref, bias_ref, cos_ref, sin_ref, dq_ref, *out_refs):
    batches, own, _ = q_ref.shape
    da = jnp.concatenate([da_ref[b] for b in range(batches)], 0)
    dout = dot_nt(da, wo_ref[...]).astype(LOW)
    lanes = k_ref.shape[-1]
    at = pl.multiple_of(pl.program_id(0) * lanes, lanes)
    middle = out_refs[0].shape[-1] // 2
    for b in range(batches):
        dq, dk, dv = chunk_grads(q_ref[b], k_ref[b], v_ref[b], dout[b * own : (b + 1) * own], bias_ref[b])
        dq_ref[b] = turned_back(dq, cos_ref[:own], sin_ref[:own])
        dk = turned_back(dk, cos_ref[...], sin_ref[...])
        for j, ref in enumerate(out_refs):
            ref[b, :, pl.ds(at, lanes)] = dk[j * own : (j + 1) * own]
            ref[b, :, pl.ds(middle + at, lanes)] = dv[j * own : (j + 1) * own]


def own_backward(qkv, da, wo, bias, cos, sin, parts):
    batches, own, width = da.shape
    rows = qkv.shape[1]
    k_lanes = KEY_VALUE_HEADS * HEAD_SIZE // parts
    q_lanes = k_lanes * GROUP
    k_at = parts * GROUP
    full = lambda *shape: pl.BlockSpec(shape, lambda c: (0,) * len(shape))
    block = (batches, own, 2 * k_lanes * parts)
    return pl.pallas_call(
        own_backward_kernel,
        grid=(parts,),
        in_specs=[
            pl.BlockSpec((batches, own, q_lanes), lambda c: (0, 0, c)),
            pl.BlockSpec((batches, rows, k_lanes), lambda c: (0, 0, k_at + c)),
            pl.BlockSpec((batches, rows, k_lanes), lambda c: (0, 0, k_at + parts + c)),
            full(batches, own, width),
            pl.BlockSpec((q_lanes, width), lambda c: (c, 0)),
            full(batches, own, rows),
            full(rows, cos.shape[1]),
            full(rows, cos.shape[1]),
        ],
        out_specs=[pl.BlockSpec((batches, own, q_lanes), lambda c: (0, 0, c))] + [full(*block)] * parts,
        out_shape=[jax.ShapeDtypeStruct((batches, own, q_lanes * parts), LOW)] + [jax.ShapeDtypeStruct(block, LOW)] * parts,
        compiler_params=params("arbitrary"),
        name="own_backward",
    )(qkv, qkv, qkv, da, wo, bias, cos, sin)


def chip_block(place_ref, x, y, core):
    ring = lax.rem(place_ref[0] + x, RING)
    pair = lax.rem(place_ref[1] + y, PAIR)
    return (ring * PAIR + pair) * CORES + lax.rem(place_ref[2] + core, CORES)


def expert_grad_kernel(cut, batches, place_ref, *refs):
    left_refs, right_refs = refs[:batches], refs[batches:-3]
    mine_ref, other_ref, turned_ref = refs[-3:]
    tokens = left_refs[0].shape[0]
    rows = mine_ref.shape[-2] // cut
    lanes = mine_ref.shape[-1]
    step = pl.program_id(1)
    if cut == 1:

        @pl.when((pl.program_id(0) == 0) & (step == 0))
        def _():
            for i, ref in enumerate(left_refs):
                turned_ref[:, i * tokens : (i + 1) * tokens] = ref[...].T

        product = dot(turned_ref[...], right_refs[0][0]).astype(LOW)
    else:
        products = [dot_tn(left[...], right[0]) for left, right in zip(left_refs, right_refs)]
        product = sum(products[1:], products[0]).astype(LOW)
    half = lax.rem(step, 2)

    def place(refs, ring_first):
        for i in range(RING):
            x = lax.rem(i + RING - place_ref[0], RING)
            for j in range(PAIR):
                y = lax.rem(j + PAIR - place_ref[1], PAIR)
                index = (x * 2 + half) * PAIR + y if ring_first else (y * RING + x) * 2 + half
                for core in range(CORES):
                    at = ((i * PAIR + j) * CORES + core) * rows
                    for part in range(cut):
                        value = product[at : at + rows, part * lanes : (part + 1) * lanes]
                        refs[core][0, 0, index, part * rows : (part + 1) * rows] = value

    for core in range(CORES):
        for ring_first in (True, False):

            @pl.when((place_ref[2] == core) & ((step < 2) == ring_first))
            def _(core=core, ring_first=ring_first):
                place((mine_ref, other_ref) if core == 0 else (other_ref, mine_ref), ring_first)


def expert_grad(place, lefts, rights, count, cut):
    number, right_rows, right_lanes = rights[0].shape
    rows, left_lanes = lefts[0].shape
    if cut > 1:
        left_lanes = left_lanes // count
    else:
        right_lanes = right_lanes // count
    owners = RING * PAIR * CORES
    high, lanes = left_lanes // owners, right_lanes // cut
    shape = (2, owners, high * cut, lanes)
    out = pl.BlockSpec((1, 1) + shape[1:], lambda r, e, p: (r, e // 2, 0, 0, 0))
    left_spec = pl.BlockSpec((rows, left_lanes), lambda r, e, p: (0, e if cut > 1 else 0))
    right_spec = pl.BlockSpec((1, right_rows, right_lanes), lambda r, e, p: (r, 0, 0 if cut > 1 else e))
    batches = len(lefts)
    return pl.pallas_call(
        functools.partial(expert_grad_kernel, cut, batches),
        grid_spec=pltpu.PrefetchScalarGridSpec(
            num_scalar_prefetch=1,
            grid=(number, count),
            in_specs=[left_spec] * batches + [right_spec] * len(rights),
            out_specs=[out, out],
            scratch_shapes=[pltpu.VMEM((left_lanes, rows * batches) if cut == 1 else (16, 128), LOW)],
        ),
        out_shape=[jax.ShapeDtypeStruct((number,) + shape, LOW)] * 2,
        compiler_params=params("arbitrary", "arbitrary"),
        name="expert_grad",
    )(place, *lefts, *rights)


def chip_sum_kernel(
    mine_inner, other_inner, mine_outer, other_outer, keep_ring, to_above, to_below, keep_pair, to_pair, to_pair_next
):
    matrix, kind = pl.program_id(0), pl.program_id(1)
    ring = {index: (keep_ring, at) for at, index in enumerate((0, 1, 2, 7))}
    ring.update({3: (to_above, 0), 4: (to_above, 1), 5: (to_below, 0), 6: (to_below, 1)})

    def add(mine, other, ring_first):
        for index in range(2 * RING * PAIR):
            value = (mine[0, 0, index].astype(F32) + other[0, 0, index].astype(F32)).astype(LOW)
            if ring_first:
                ref, at = ring[index // PAIR]
                ref[0, at, index % PAIR] = value
            elif index < 2 * RING:
                keep_pair[0, index] = value
            else:
                (to_pair if index < 3 * RING else to_pair_next)[0, index % RING] = value

    for inner in (True, False):
        for ring_first in (True, False):

            @pl.when(((matrix < 2) == inner) & ((kind == 0) == ring_first))
            def _(inner=inner, ring_first=ring_first):
                add(*((mine_inner, other_inner) if inner else (mine_outer, other_outer)), ring_first)


def chip_sum(inner, outer):
    tile = inner[0].shape[3:]
    block = (1, 1, 2 * RING * PAIR) + tile
    inner_spec = pl.BlockSpec(block, lambda m, k: (jnp.minimum(m, 1), jnp.where(m < 2, k, 1), 0, 0, 0))
    outer_spec = pl.BlockSpec(block, lambda m, k: (0, jnp.where(m < 2, 0, k), 0, 0, 0))
    shapes = [(4, PAIR), (2, PAIR), (2, PAIR), (2 * RING,), (RING,), (RING,)]
    return pl.pallas_call(
        chip_sum_kernel,
        grid=(3, 2),
        in_specs=[inner_spec, inner_spec, outer_spec, outer_spec],
        out_specs=[pl.BlockSpec((1,) + shape + tile, lambda m, k, n=len(shape) + 2: (m,) + (0,) * n) for shape in shapes],
        out_shape=[jax.ShapeDtypeStruct((3,) + shape + tile, LOW) for shape in shapes],
        compiler_params=params("arbitrary", "arbitrary", mib=56),
        name="chip_sum",
    )(*inner, *outer)


def dense_grad_kernel(batches, parts, place_ref, z_ref, *refs):
    del z_ref
    mixed_refs, xn_refs, da_refs = refs[:batches], refs[batches : 2 * batches], refs[2 * batches : 2 * batches + parts]
    dqkv_ref, mine_ref, other_ref, into_ref, out_of_ref = refs[2 * batches + parts :]
    rows = xn_refs[0].shape[0]
    high = mine_ref.shape[-2]
    lanes, wide = out_of_ref.shape[-1], dqkv_ref.shape[1]
    into = sum(dot_tn(ref[...], dqkv_ref[b * rows : (b + 1) * rows]) for b, ref in enumerate(xn_refs)).astype(LOW)
    da = [jnp.concatenate([ref[b] for ref in da_refs], 0) for b in range(batches)]
    out_of = sum(dot_tn(ref[...], da[b]) for b, ref in enumerate(mixed_refs)).astype(LOW)
    for chip in range(RING * PAIR):
        for core in range(CORES):
            owner = chip * CORES + core
            for half in range(2):
                at = (owner * 2 + half) * high
                into_ref[owner, half] = into[at : at + high]
                at = (half * CORES + core) * lanes
                out_of_ref[owner, half] = out_of[chip * high : (chip + 1) * high, at : at + lanes]
    for core, ref in enumerate((mine_ref, other_ref)):
        for x in range(RING):
            for y in range(PAIR):
                owner = chip_block(place_ref, x, y, core)
                for half in range(2):
                    ref[0, x * 2 + half, y, :, :wide] = into_ref[owner, half]
                    ref[0, x * 2 + half, y, :, wide:] = out_of_ref[owner, half]


def dense_grad(place, z, mixed, da, xn, dqkv, parts):
    batches = len(xn)
    rows, width = xn[0].shape
    owners = RING * PAIR * CORES
    q_lanes, wide = mixed[0].shape[1] // parts, dqkv.shape[1]
    high, lanes = width // owners // 2, width // CORES // 2
    shape = (1, 2 * RING, PAIR, high, wide + lanes)
    whole = lambda *shape: pl.BlockSpec(shape, lambda i, p, z: (0,) * len(shape))
    return pl.pallas_call(
        functools.partial(dense_grad_kernel, batches, parts),
        grid_spec=pltpu.PrefetchScalarGridSpec(
            num_scalar_prefetch=2,
            grid=(1,),
            in_specs=[pl.BlockSpec((rows, q_lanes), lambda i, p, z: (0, z[0]))] * batches
            + [whole(rows, width)] * batches
            + [whole(*da[0].shape)] * parts
            + [whole(*dqkv.shape)],
            out_specs=[pl.BlockSpec(shape, lambda i, p, z: (0,) * 5)] * 2,
            scratch_shapes=[pltpu.VMEM((owners, 2, high, wide), LOW), pltpu.VMEM((owners, 2, high, lanes), LOW)],
        ),
        out_shape=[jax.ShapeDtypeStruct(shape, LOW)] * 2,
        compiler_params=params("arbitrary", mib=56),
        name="dense_grad",
    )(place, z, *mixed, *xn, *da, dqkv)


def dense_layout_kernel(by_x, place_ref, z_ref, mine_ref, other_ref, *refs):
    outs = refs[-4:]
    parts = mine_ref.shape[3] if by_x else mine_ref.shape[0]
    wide = mine_ref.shape[-1]
    for core, ref in enumerate((mine_ref, other_ref)):
        to_core = lax.rem(place_ref[2] + core, CORES)
        for y in range(PAIR):
            to_y = lax.rem(place_ref[1] + y, PAIR)
            for k in range(parts):
                at = lax.rem(z_ref[0] + parts - k, parts)
                start = 0
                for out in outs:
                    to_rows = out is outs[3]
                    lanes = out.shape[-1] // (CORES if to_rows else parts)
                    by, begin = divmod(start, wide)
                    index = (0, by, y, k) if by_x else (k, by, y, 0)
                    value = ref[index + (slice(None), slice(begin, begin + lanes))].astype(F32)
                    if to_rows:
                        out[at, 0, to_y, :, pl.ds(pl.multiple_of(to_core * lanes, 128), lanes)] = value
                    else:
                        out[0, to_y, to_core, 0, :, pl.ds(pl.multiple_of(at * lanes, 128), lanes)] = value
                    start += lanes


def dense_layout(place, z, half, mine, other, shapes, before):
    by_x = half == 0
    high, lanes = mine.shape[-2:]
    parts = mine.shape[3] if by_x else mine.shape[0]
    if by_x:
        source = pl.BlockSpec((1, 2, PAIR, parts, high, lanes), lambda x, p, z: (x, 0, 0, 0, 0, 0))
    else:
        source = pl.BlockSpec((parts, 2, PAIR, 1, high, lanes), lambda x, p, z: (0, 0, 0, x, 0, 0))
    ring = lambda x, p: lax.rem(p[0] + RING - x, RING)
    width = shapes[3][1]
    shapes = [(RING, PAIR, CORES, 2, high, shape[1]) for shape in shapes[:3]] + [(parts, RING, PAIR, high, width)]
    out_specs = [
        pl.BlockSpec((1, PAIR, CORES, 1, high, shape[-1]), lambda x, p, z: (ring(x, p), 0, 0, half, 0, 0)) for shape in shapes[:3]
    ] + [pl.BlockSpec((parts, 1, PAIR, high, width // 2), lambda x, p, z: (0, ring(x, p), 0, 0, half))]
    return pl.pallas_call(
        functools.partial(dense_layout_kernel, by_x),
        grid_spec=pltpu.PrefetchScalarGridSpec(
            num_scalar_prefetch=2,
            grid=(RING,),
            in_specs=[source, source] + [pl.BlockSpec(memory_space=pl.ANY)] * len(before),
            out_specs=out_specs,
        ),
        out_shape=[jax.ShapeDtypeStruct(shape, F32) for shape in shapes],
        input_output_aliases={4 + i: i for i in range(len(before))},
        compiler_params=params("arbitrary"),
        cost_estimate=pl.CostEstimate(flops=0, bytes_accessed=24 * mine.size, transcendentals=0),
        name="dense_layout",
    )(place, z, mine, other, *before)


def norm_back(grad_normed, values, gain):
    scale = lax.rsqrt(jnp.mean(values * values, -1, keepdims=True) + EPS)
    scaled = grad_normed * gain
    gain_grad = jnp.sum(grad_normed * values * scale, (0, 1))
    inner = jnp.mean(scaled * values, -1, keepdims=True)
    return (scale * scaled - values * scale * scale * scale * inner, gain_grad)


def local(
    block_input, segments, expert_ids, route_weights, attn_gain, w_query, key_projection_weight,
    value_projection_weight, w_out, ffn_gain, w_gate, w_up, w_down, out_grad,
):
    parts = lax.axis_size("expert")
    section = lax.axis_index("section")
    z = lax.axis_index("expert")
    z_at = z.reshape(1)
    dp = lax.axis_index("dp")
    dp_place = jnp.stack([dp // (PAIR * CORES), dp // CORES % PAIR, dp % CORES])
    batches, own, width = block_input.shape
    rows = parts * own
    wq, wk, wv, wo = w_query[0], key_projection_weight[0], value_projection_weight[0], w_out[0]
    local_experts, units = w_gate.shape[1], w_gate.shape[3]

    outer = w_down[0].reshape(local_experts, -1, width // units, units)
    outer = jnp.swapaxes(outer, 1, 2).reshape(w_gate[0].shape)
    shard = jnp.stack([w_gate[0], w_up[0], outer], 1)
    near, far = shard[:2], shard[2:]
    numbers = jnp.arange(parts * local_experts, dtype=jnp.int32)
    hits = expert_ids[0][..., None] == numbers
    shares = jnp.sum(jnp.where(hits, route_weights[0][..., None], 0.0), 2)
    shares = jnp.concatenate([shares, segments.astype(F32)[..., None]], -1)
    start = spread_group(block_input)
    near_y = moved(near, y=1)
    far_1 = ring_gather_step(far)
    shares = spread_group(shares)
    start, near_y, far_1, shares = hold(start, near_y, far_1, shares)

    start = jnp.concatenate(start, 1)
    shares = jnp.concatenate(shares, 1)
    labels = shares[..., -1]
    shares = shares[..., :-1].reshape(batches * rows, parts, local_experts)
    share = lax.dynamic_index_in_dim(shares, z, 1, keepdims=False).T[..., None]
    block = jnp.arange(parts, dtype=jnp.int32)[:, None]
    place = ((z - block) % parts * own + jnp.arange(own, dtype=jnp.int32)[None, :]).reshape(rows)
    allowed = (place[None, None, :] <= place[None, :, None]) & (labels[:, None, :] == labels[:, :, None])
    bias = jnp.where(allowed, 0.0, -1e30).astype(F32)
    half = HEAD_SIZE // 2
    frequency = 10000.0 ** (-jnp.arange(half, dtype=F32) * 2.0 / HEAD_SIZE)
    angles = place.astype(F32)[:, None] * frequency[None, :]
    cos_half, sin_half = jnp.cos(angles), jnp.sin(angles)
    cos = jnp.concatenate([cos_half] * 4, -1)
    sin = jnp.concatenate([-sin_half, sin_half] * 2, -1)
    cos_all, sin_all = jnp.concatenate([cos] * batches, 0), jnp.concatenate([sin] * batches, 0)

    def attention_in(x, cos, sin):
        qkv, xn = project(x.reshape(-1, width), attn_gain, wq, wk, wv, cos, sin)
        return qkv.reshape(-1, rows, qkv.shape[1]), xn

    def attention_out(qkv, bias, x):
        mixed = attend(qkv, bias, parts)
        h1, xn2 = join(mixed, x, wo, ffn_gain, own)
        return mixed.reshape(-1, wo.shape[0]), h1, xn2.reshape(-1, width)

    near = jnp.stack([near, near_y])
    near_1 = ring_gather_step(near)
    far_2 = ring_gather_next(far_1)
    far_a = jnp.stack([far, *far_1])
    far_ya = moved(far_a, y=1)
    qkv, _ = attention_in(start, cos_all, sin_all)
    _, h1, xn2 = attention_out(qkv, bias, start)

    xn2, near_1, far_2, far_ya = hold(xn2, near_1, far_2, far_ya)
    near_b = moved(near_1[0][:, 0], x=1), moved(near_1[1][:, 1], x=-1)
    far_b = jnp.stack(far_2)
    far_yb = moved(far_b, y=1)
    near_a = jnp.stack([near, *near_1])
    others = [moved(piece, core=1) for piece in (near_a, far_a)]

    near_b, far_yb, others = hold(near_b, far_yb, others)
    near_b = jnp.stack(near_b)
    pieces = [near_a, near_b, far_a, far_b, far_ya, far_yb]
    pieces += [others[0], moved(near_b, core=1), others[1], *[moved(piece, core=1) for piece in (far_b, far_ya, far_yb)]]
    *blocks, wg, wu, wd = experts_forward(dp_place, xn2, share, pieces, batches, own, parts)
    blocks = [blocks[b * parts : (b + 1) * parts] for b in range(batches)]
    c_second = lax.all_gather(out_grad, "expert")
    c_second = jnp.concatenate([lax.dynamic_index_in_dim(c_second, (z + parts - j) % parts, 0, False) for j in range(parts)], 1)
    flat_second = c_second.reshape(batches * rows, width)
    received = []
    result = None
    for b in range(batches):
        came = owners_step(blocks[b])
        if b > 0:
            came = once(came, result)
        result = (h1[b : b + 1] + added(*came)).astype(LOW)
        received.append(spread_group(to_section(result, 1)))

    biases = [bias[b : b + 1] for b in range(batches)]
    x, qkv, xn, mixed, h1, xn2, hidden, to_up, to_gate, blocks = ([None] * batches for _ in range(10))
    for b in range(batches):
        if b > 0:
            received[b] = once(received[b], hidden[b - 1])
        x[b] = jnp.where(section == 0, start[b : b + 1], jnp.concatenate(received[b], 1))
        qkv[b], xn[b] = attention_in(x[b], cos, sin)
        mixed[b], h1[b], xn2[b] = attention_out(qkv[b], biases[b], x[b])
        hidden[b], to_up[b], to_gate[b], *blocks[b] = experts_turn(xn2[b], flat_second, share, wg, wu, wd, b, own, parts)
    x_own = jnp.concatenate([rows_of[:, :own] for rows_of in x], 0).astype(F32)

    after, dq, kv_came = ([None] * batches for _ in range(3))
    for b in range(batches):
        came = owners_step(blocks[b])
        if b > 0:
            came = once(came, dq[b - 1])
        after[b] = out_grad[b : b + 1].astype(F32) + norm_back(added(*came), h1[b], ffn_gain)[0]
        dq[b], *kv_blocks = own_backward(qkv[b], after[b].astype(LOW), wo, biases[b], cos, sin, parts)
        kv_came[b] = owners_step(kv_blocks)
    kv_came[0] = once(kv_came[0], dq[-1])
    received_own = []
    for b in range(batches):
        if b > 0:
            kv_came[b] = once(kv_came[b], input_grad)
        dkv = added(*kv_came[b]).astype(LOW).reshape(own, -1)
        dn_own = dot_nt(dq[b].reshape(own, -1), wq)
        dn_own = dn_own + dot_nt(dkv[:, : wk.shape[1]], wk) + dot_nt(dkv[:, wk.shape[1] :], wv)
        input_grad = after[b] + norm_back(dn_own[None], x_own[b : b + 1], attn_gain)[0]
        received_own.append(to_section(input_grad.astype(LOW), 0))

    c_own = jnp.where(section == 1, out_grad, jnp.concatenate(received_own, 0))
    c = [jnp.where(section == 1, c_second[b : b + 1], gather_group(received_own[b])).reshape(rows, width) for b in range(batches)]
    *blocks, hidden_grads = experts_backward(c, to_up, to_gate, wg, wu, wd, own, parts)
    norm_part, ffn_grad = norm_back(added(*owners_step(blocks)), jnp.concatenate(h1, 0), ffn_gain)
    after = c_own.astype(F32) + norm_part
    both = [
        expert_grad(dp_place, xn2, [hidden_grads], local_experts, 1),
        expert_grad(dp_place, hidden, [block[None] for block in c], local_experts, width // units),
    ]
    after, both = hold(after, both)
    inner, outer = [(mine, moved(other, core=1)) for mine, other in both]
    da = spread_group(after.astype(LOW))
    keep_ring, to_above, to_below, keep_pair, *to_pair = chip_sum(inner, outer)
    da, to_above, to_below, to_pair = hold(da, to_above, to_below, to_pair)

    ring_1 = moved(to_above, x=1), moved(to_below, x=-1)
    pair_1 = [moved(block, y=1) for block in to_pair]
    dqkv, dn = attend_backward(z_at, qkv, da, wo, wq, wk, wv, bias, cos, sin, parts)
    mine, other = dense_grad(dp_place, z_at, mixed, da, xn, dqkv, parts)
    dn_own = lax.psum_scatter(dn, "expert", scatter_dimension=0, tiled=True)[0].astype(F32)

    mine, other, ring_1, pair_1[0] = hold(mine, other, ring_1, pair_1[0])
    other = moved(other, core=1)
    outputs = jnp.stack([dot(units_of, wd.reshape(local_experts * units, width)).astype(LOW) for units_of in once(hidden, mine)])
    other = once(other, outputs)
    dense = added(mine, other).astype(LOW)

    (dense,) = hold(dense)
    dense_1 = ring_step(dense)
    outputs = outputs.reshape(batches, parts, own, width)
    outputs = jnp.stack([lax.dynamic_index_in_dim(outputs, (z + parts - i) % parts, 1, False) for i in range(parts)])

    dense_1, outputs, dn_own = hold(dense_1, outputs, dn_own)
    outputs = lax.psum_scatter(outputs, "expert", scatter_dimension=0, tiled=True)[0]
    dense_2 = ring_next(dense, dense_1)
    norm_part, attn_grad = norm_back(dn_own, x_own, attn_gain)
    input_grad = after + norm_part
    gains = jnp.stack([attn_grad, ffn_grad])
    gains = gains + exchanged(gains, "expert", 1)
    ring_2 = (
        moved(added(keep_ring[:, 2], ring_1[0][:, 1]).astype(LOW), x=1),
        moved(added(keep_ring[:, 3], ring_1[1][:, 0]).astype(LOW), x=-1),
    )

    dense_2, gains, ring_2 = hold(dense_2, gains, ring_2)
    dense = ring_end(dense, dense_1, dense_2)[:, 0]
    dense_3 = moved(dense[:, 1].astype(LOW), y=1)
    gains = gains + exchanged(gains, "expert", 2)
    ring_sums = jnp.stack(
        [
            added(keep_ring[:, 0], ring_1[1][:, 1], ring_2[0]),
            added(keep_ring[:, 1], ring_1[0][:, 0], ring_2[1]),
        ]
    )

    dense_3, gains, ring_sums = hold(dense_3, gains, ring_sums)
    owned = added(dense[:, 0], dense_3).astype(LOW)
    first, second = owned[0], by_lanes(owned[1])
    first_1 = [shifted(first, k) for k in range(1, parts)]
    second_1 = [moved(second, x=k) for k in range(1, RING)]

    first_1, second_1, pair_1 = hold(first_1, second_1, pair_1)
    pair_sums = added(keep_pair, jnp.concatenate(pair_1, 1)).astype(LOW)
    first = jnp.stack([first] + first_1)
    first_2 = moved(first, y=1)
    second = jnp.stack([second] + second_1)
    second_2 = moved(second, y=1)
    pair_2 = ring_step(pair_sums)
    gains = gains + exchanged(gains, "dp", 1)

    first_2, second_2, gains, pair_2 = hold(first_2, second_2, gains, pair_2)
    first = by_lanes(jnp.stack([first, first_2]))
    first_3 = ring_gather_step(first)
    second = jnp.moveaxis(jnp.stack([second, second_2]), 2, 0)
    second_3 = group_gather_step(second)
    ring_away = moved(ring_sums[:, :, 1].astype(LOW), y=1)
    gains = gains + exchanged(gains, "dp", 2)

    first_3, second_3, ring_away, gains, outputs = hold(first_3, second_3, ring_away, gains, outputs)
    first_4 = ring_gather_next(first_3)
    second_4 = group_gather_next(second_3)
    pair_3 = ring_next(pair_sums, pair_2)
    ring_sums = added(ring_sums[:, :, 0], ring_away)

    first_4, second_4, pair_3, ring_sums = hold(first_4, second_4, pair_3, ring_sums)
    first = ring_stack(first, first_3, first_4)
    first_other = moved(first, core=1)
    pair_sums = ring_end(pair_sums, pair_2, pair_3)
    gains = gains + exchanged(gains, "dp", 4)

    second = ring_stack(second, second_3, second_4)
    second, first_other, gains, pair_sums = hold(second, first_other, gains, pair_sums)
    second_other = moved(second, core=1)
    shapes = (wq.shape, wk.shape, wv.shape, wo.shape)
    laid = dense_layout(dp_place, z_at, 0, first, first_other, shapes, ())
    gains = gains + exchanged(gains, "dp", 8)
    w_gate_grad, w_up_grad, w_down_grad = (jnp.concatenate([ring_sums[:, i], pair_sums[:, i]], 0) for i in range(3))
    w_down_grad = w_down_grad.reshape(local_experts, width // units, -1, units)
    w_down_grad = jnp.swapaxes(w_down_grad, 1, 2).reshape(local_experts, -1, width)

    second_other, laid = hold(second_other, laid)
    laid = dense_layout(dp_place, z_at, 1, second, second_other, shapes, laid)
    w_query_grad, w_key_grad, w_value_grad, w_out_grad = (
        grad.reshape(weight.shape) for grad, weight in zip(laid, (wq, wk, wv, wo))
    )

    layer_outputs = (jnp.concatenate(h1, 0) + outputs.astype(F32)).astype(LOW)
    return (
        layer_outputs[None],
        input_grad[None],
        gains[0:1],
        w_query_grad[None],
        w_key_grad[None],
        w_value_grad[None],
        w_out_grad[None],
        gains[1:2],
        w_gate_grad[None],
        w_up_grad[None],
        w_down_grad[None],
    )


def solution(mesh):
    tokens = P(None, ("dp", "expert"), None)
    layered = P("section", None, ("dp", "expert"), None)
    vector = P("section", None)
    matrix = P("section", None, None)
    expert = P("section", "expert", "dp", None)
    return jax.shard_map(
        local,
        mesh=mesh,
        in_specs=(
            tokens, P(None, ("dp", "expert")), layered, layered, vector, matrix, matrix, matrix, matrix,
            vector, expert, expert, expert, tokens,
        ),
        out_specs=(layered, layered, vector, matrix, matrix, matrix, matrix, vector, expert, expert, expert),
        check_vma=False,
    )
```

```python
import functools

import jax
import jax.numpy as jnp
from jax import lax
from jax.experimental import pallas as pl
from jax.experimental.pallas import tpu as pltpu
from jax.sharding import PartitionSpec as P

QUERY_HEADS = 24
KEY_VALUE_HEADS = 8
HEAD_SIZE = 64
GROUP = QUERY_HEADS // KEY_VALUE_HEADS
EPS = 1e-06
LOW = jnp.bfloat16
F32 = jnp.float32
MIB = 1024 * 1024


def params(*semantics, mib=30):
    return pltpu.CompilerParams(dimension_semantics=semantics, vmem_limit_bytes=mib * MIB)


def dot(left, right):
    return jnp.dot(left, right, preferred_element_type=F32)


def dot_nt(left, right):
    return lax.dot_general(left, right, (((1,), (1,)), ((), ())), preferred_element_type=F32)


def dot_tn(left, right):
    return lax.dot_general(left, right, (((0,), (0,)), ((), ())), preferred_element_type=F32)


def shifted(block, by):
    size = lax.axis_size("expert")
    return lax.ppermute(block, "expert", [(i, (i + by) % size) for i in range(size)])


def spread_group(block):
    return [block] + [shifted(block, j) for j in range(1, lax.axis_size("expert"))]


def gather_group(block):
    return jnp.concatenate(spread_group(block), 1)


def owners_step(blocks):
    size = len(blocks)
    return [blocks[0]] + [shifted(blocks[j], size - j) for j in range(1, size)]


def across(block):
    return lax.ppermute(block, "section", [(0, 1), (1, 0)])


RING, PAIR, CORES = 4, 2, 2


def moved(block, x=0, y=0, core=0):
    route = []
    for i in range(RING):
        for j in range(PAIR):
            for k in range(CORES):
                target = ((i + x) % RING * PAIR + (j + y) % PAIR) * CORES + (k + core) % CORES
                route.append(((i * PAIR + j) * CORES + k, target))
    return lax.ppermute(block, "dp", route)


def added(*terms):
    total = terms[0].astype(F32)
    for term in terms[1:]:
        total = total + term.astype(F32)
    return total


def ring_step(blocks):
    return moved(blocks[3:5], x=1), moved(blocks[5:7], x=-1)


def ring_next(stays, step):
    below = moved(added(stays[0], step[0][1]).astype(LOW), x=1)
    above = moved(added(stays[1], step[1][0]).astype(LOW), x=-1)
    return below, above


def ring_end(stays, step, last):
    return jnp.stack([added(stays[0], step[1][1], last[0]), added(stays[1], step[0][0], last[1])])


def ring_gather_step(block):
    return moved(block, x=1), moved(block, x=-1)


def ring_gather_next(step):
    return moved(step[0][0], x=1), moved(step[1][1], x=-1)


def exchanged(values, axis, bit):
    return lax.ppermute(values, axis, [(i, i ^ bit) for i in range(lax.axis_size(axis))])


def hold(*values):
    return lax.optimization_barrier(values)


def once(values, *earlier):
    return hold(values, *earlier)[0]


def swap_halves(values):
    half = HEAD_SIZE // 2
    lanes = values.shape[-1]
    lane = lax.broadcasted_iota(jnp.int32, values.shape, values.ndim - 1)
    ahead = pltpu.roll(values, lanes - half, values.ndim - 1)
    behind = pltpu.roll(values, half, values.ndim - 1)
    return jnp.where(lane % HEAD_SIZE < half, ahead, behind)


def widen_table(table, lanes):
    return jnp.concatenate([table] * (lanes // table.shape[-1]), -1)


def project_kernel(query_steps, x_ref, gain_ref, wq_ref, wk_ref, wv_ref, cos_ref, sin_ref, out_ref, xn_ref):
    step = pl.program_id(0)

    @pl.when(step == 0)
    def _():
        wide = x_ref[...].astype(F32)
        scale = lax.rsqrt(jnp.mean(wide * wide, -1, keepdims=True) + EPS)
        xn_ref[...] = (wide * scale * gain_ref[...]).astype(LOW)

    def turned(weight):
        product = dot(xn_ref[...], weight)
        lanes = product.shape[-1]
        cos, sin = widen_table(cos_ref[...], lanes), widen_table(sin_ref[...], lanes)
        return (product * cos + swap_halves(product) * sin).astype(LOW)

    @pl.when(step < query_steps)
    def _():
        out_ref[...] = turned(wq_ref[...])

    @pl.when(step == query_steps)
    def _():
        out_ref[...] = turned(wk_ref[...])

    @pl.when(step == query_steps + 1)
    def _():
        out_ref[...] = dot(xn_ref[...], wv_ref[...]).astype(LOW)


def project(x, gain, wq, wk, wv, cos, sin):
    rows, width = x.shape
    lanes = wk.shape[1]
    query_steps = wq.shape[1] // lanes
    whole = lambda *shape: pl.BlockSpec(shape, lambda i: (0,) * len(shape))
    return pl.pallas_call(
        functools.partial(project_kernel, query_steps),
        grid=(query_steps + 2,),
        in_specs=[
            whole(rows, width),
            whole(1, width),
            pl.BlockSpec((width, lanes), lambda i: (0, jnp.minimum(i, query_steps - 1))),
            whole(width, lanes),
            whole(width, lanes),
            whole(rows, cos.shape[1]),
            whole(rows, cos.shape[1]),
        ],
        out_specs=[pl.BlockSpec((rows, lanes), lambda i: (0, i)), whole(rows, width)],
        out_shape=[
            jax.ShapeDtypeStruct((rows, lanes * (query_steps + 2)), LOW),
            jax.ShapeDtypeStruct((rows, width), LOW),
        ],
        compiler_params=params("arbitrary"),
        name="project",
    )(x, gain, wq, wk, wv, cos, sin)


def head(values, index):
    return values[:, index * HEAD_SIZE : (index + 1) * HEAD_SIZE]


def softmax_parts(stacked_q, key, bias):
    scores = dot_nt(stacked_q, key) * 0.125 + bias
    raised = jnp.exp(scores - jnp.max(scores, -1, keepdims=True))
    return raised * (1.0 / jnp.sum(raised, -1, keepdims=True))


def attend_kernel(q_ref, k_ref, v_ref, bias_ref, o_ref):
    bias = bias_ref[0]
    q, k, v = q_ref[0] * jnp.asarray(0.125, LOW), k_ref[0], v_ref[0]
    mixed = []
    for pair in range(k.shape[1] // HEAD_SIZE):
        key, value = head(k, pair), head(v, pair)
        for j in range(GROUP):
            scores = dot_nt(head(q, pair * GROUP + j), key) + bias
            raised = jnp.exp(scores - jnp.max(scores, -1, keepdims=True))
            total = jnp.sum(raised, -1, keepdims=True)
            mixed.append(dot(raised.astype(LOW), value) * (1.0 / total))
    o_ref[0] = jnp.concatenate(mixed, -1).astype(LOW)


def attend(qkv, bias, parts):
    batches, rows, lanes = qkv.shape
    k_lanes = KEY_VALUE_HEADS * HEAD_SIZE // parts
    q_lanes = k_lanes * GROUP
    k_at = parts * GROUP
    return pl.pallas_call(
        attend_kernel,
        grid=(batches, parts),
        in_specs=[
            pl.BlockSpec((1, rows, q_lanes), lambda b, c: (b, 0, c)),
            pl.BlockSpec((1, rows, k_lanes), lambda b, c: (b, 0, k_at + c)),
            pl.BlockSpec((1, rows, k_lanes), lambda b, c: (b, 0, k_at + parts + c)),
            pl.BlockSpec((1, rows, rows), lambda b, c: (b, 0, 0)),
        ],
        out_specs=pl.BlockSpec((1, rows, q_lanes), lambda b, c: (b, 0, c)),
        out_shape=jax.ShapeDtypeStruct((batches, rows, q_lanes * parts), LOW),
        compiler_params=params("arbitrary", "arbitrary"),
        name="attend",
    )(qkv, qkv, qkv, bias)


def join_kernel(o_ref, x_ref, wo_ref, gain_ref, h1_ref, xn2_ref):
    total = x_ref[0].astype(F32) + dot(o_ref[0], wo_ref[...])
    scale = lax.rsqrt(jnp.mean(total * total, -1, keepdims=True) + EPS)
    h1_ref[0] = total[: h1_ref.shape[1]]
    xn2_ref[0] = (total * scale * gain_ref[...]).astype(LOW)


def join(o, x, wo, gain, own):
    batches, rows, width = x.shape
    batch = lambda *shape: pl.BlockSpec((1,) + shape, lambda b: (b, 0, 0))
    whole = lambda *shape: pl.BlockSpec(shape, lambda b: (0, 0))
    return pl.pallas_call(
        join_kernel,
        grid=(batches,),
        in_specs=[batch(rows, wo.shape[0]), batch(rows, width), whole(*wo.shape), whole(1, width)],
        out_specs=[batch(own, width), batch(rows, width)],
        out_shape=[
            jax.ShapeDtypeStruct((batches, own, width), F32),
            jax.ShapeDtypeStruct((batches, rows, width), LOW),
        ],
        compiler_params=params("arbitrary"),
        name="join",
    )(o, x, wo, gain)


def expert_hidden(xn_ref, share_ref, wg_ref, wu_ref):
    gate, up = dot(xn_ref[...], wg_ref[0]), dot(xn_ref[...], wu_ref[0])
    share = share_ref[0]
    sigma = jax.nn.sigmoid(gate)
    silu = gate * sigma
    return gate, up, share, sigma, silu


def accumulate(total_ref, part):
    step = pl.program_id(0)

    @pl.when(step == 0)
    def _():
        total_ref[...] = part

    @pl.when(step > 0)
    def _():
        total_ref[...] += part


def hand_out(total_ref, out_refs):
    @pl.when(pl.program_id(0) == pl.num_programs(0) - 1)
    def _():
        batches, own, _ = out_refs[0].shape
        for b in range(batches):
            for j, ref in enumerate(out_refs):
                at = (b * len(out_refs) + j) * own
                ref[b] = total_ref[at : at + own].astype(LOW)


def experts_forward_kernel(place_ref, xn_ref, share_ref, *refs):
    pieces, out_refs = refs[:12], refs[12:-4]
    wg_ref, wu_ref, wd_ref, total_ref = refs[-4:]
    step = pl.program_id(0)
    high = wg_ref.shape[1] // (RING * PAIR * CORES)
    low = wd_ref.shape[1] // (RING * PAIR * CORES)

    def lay(block, x, y, core):
        ring = lax.rem(place_ref[0] + RING - x, RING)
        pair = lax.rem(place_ref[1] + y, PAIR)
        at = (ring * PAIR + pair) * CORES + lax.rem(place_ref[2] + core, CORES)
        rows = pl.ds(pl.multiple_of(at * high, high), high)
        wg_ref[0, rows] = block[0]
        wu_ref[0, rows] = block[1]
        outer = [block[2][k * low : (k + 1) * low] for k in range(high // low)]
        wd_ref[0, pl.ds(pl.multiple_of(at * low, low), low)] = jnp.concatenate(outer, -1)

    @pl.when(step < 2)
    def _():
        for core in range(CORES):
            near_a, near_b = pieces[core * 6 : core * 6 + 2]
            for y in range(PAIR):
                for i, x in enumerate((0, 1, 3)):
                    lay([near_a[i, y, 0, k] for k in range(3)], x, y, core)
                lay([near_b[0, y, k] for k in range(3)], 2, y, core)

    @pl.when(step >= 2)
    def _():
        for core in range(CORES):
            for n, ref in enumerate(pieces[core * 6 + 2 : core * 6 + 6]):
                for i, x in enumerate((0, 1, 3) if n % 2 == 0 else (2,)):
                    lay([ref[(i, 0, k) if n % 2 == 0 else (0, k)] for k in range(3)], x, n // 2, core)

    _, up, share, _, silu = expert_hidden(xn_ref, share_ref, wg_ref, wu_ref)
    accumulate(total_ref, dot((silu * up * share).astype(LOW), wd_ref[0]))
    hand_out(total_ref, out_refs)


def experts_forward(place, xn, share, pieces, batches, own, parts):
    rows, width = xn.shape
    count = share.shape[0]
    high, units = pieces[0].shape[-2:]
    tile = (3, high, units)
    near, far = (lambda e: jnp.minimum(e, 1)), (lambda e: jnp.maximum(e - 2, 0))
    specs = [
        pl.BlockSpec((3, PAIR, 1) + tile, lambda e, p: (0, 0, near(e), 0, 0, 0)),
        pl.BlockSpec((1, PAIR) + tile, lambda e, p: (near(e), 0, 0, 0, 0)),
        pl.BlockSpec((3, 1) + tile, lambda e, p: (0, far(e), 0, 0, 0)),
        pl.BlockSpec((1,) + tile, lambda e, p: (far(e), 0, 0, 0)),
    ]
    specs = (specs + specs[2:]) * CORES
    block = (1, own, width)
    matrix = lambda *shape: pl.BlockSpec((1,) + shape, lambda e, p: (e, 0, 0))
    return pl.pallas_call(
        experts_forward_kernel,
        grid_spec=pltpu.PrefetchScalarGridSpec(
            num_scalar_prefetch=1,
            grid=(count,),
            in_specs=[
                pl.BlockSpec((rows, width), lambda e, p: (0, 0)),
                pl.BlockSpec((1, rows, 1), lambda e, p: (e, 0, 0)),
            ]
            + specs,
            out_specs=[pl.BlockSpec(block, lambda e, p: (0, 0, 0))] * parts * batches
            + [matrix(width, units), matrix(width, units), matrix(units, width)],
            scratch_shapes=[pltpu.VMEM((rows, width), F32)],
        ),
        out_shape=[jax.ShapeDtypeStruct(block, LOW)] * parts * batches
        + [jax.ShapeDtypeStruct((count,) + shape, LOW) for shape in ((width, units), (width, units), (units, width))],
        compiler_params=params("arbitrary", mib=44),
        name="experts_forward",
    )(place, xn, share, *pieces)


def expert_specs(rows, width, units, batch):
    return [
        pl.BlockSpec((1, rows, 1), lambda e: (e, batch, 0)),
        pl.BlockSpec((1, width, units), lambda e: (e, 0, 0)),
        pl.BlockSpec((1, width, units), lambda e: (e, 0, 0)),
        pl.BlockSpec((1, units, width), lambda e: (e, 0, 0)),
    ]


def experts_turn_kernel(xn_ref, c_ref, share_ref, wg_ref, wu_ref, wd_ref, hidden_ref, to_up_ref, to_gate_ref, *refs):
    gate, up, share, sigma, silu = expert_hidden(xn_ref, share_ref, wg_ref, wu_ref)
    shared = silu * share
    hidden_ref[...] = (shared * up).astype(LOW)
    to_up = shared.astype(LOW)
    to_gate = (share * up * sigma * (1.0 + gate * (1.0 - sigma))).astype(LOW)
    to_up_ref[...] = to_up
    to_gate_ref[...] = to_gate
    grads = dot_nt(c_ref[...], wd_ref[0])
    gate_grad = (grads * to_gate.astype(F32)).astype(LOW)
    up_grad = (grads * to_up.astype(F32)).astype(LOW)
    accumulate(refs[-1], dot_nt(gate_grad, wg_ref[0]) + dot_nt(up_grad, wu_ref[0]))
    hand_out(refs[-1], refs[:-1])


def experts_turn(xn, c, share, wg, wu, wd, batch, own, parts):
    rows, width = xn.shape
    count, _, units = wg.shape
    kept = pl.BlockSpec((rows, units), lambda e: (0, e))
    block = (1, own, width)
    return pl.pallas_call(
        experts_turn_kernel,
        grid=(count,),
        in_specs=[
            pl.BlockSpec((rows, width), lambda e: (0, 0)),
            pl.BlockSpec((rows, width), lambda e: (batch, 0)),
        ]
        + expert_specs(rows, width, units, batch),
        out_specs=[kept] * 3 + [pl.BlockSpec(block, lambda e: (0, 0, 0))] * parts,
        out_shape=[jax.ShapeDtypeStruct((rows, units * count), LOW)] * 3 + [jax.ShapeDtypeStruct(block, LOW)] * parts,
        scratch_shapes=[pltpu.VMEM((rows, width), F32)],
        compiler_params=params("arbitrary", mib=56),
        name="experts_turn",
    )(xn, c, share, wg, wu, wd)


def experts_backward_kernel(batches, *refs):
    c_refs, up_refs, gate_refs = (refs[i * batches : (i + 1) * batches] for i in range(3))
    wg_ref, wu_ref, wd_ref, *out_refs = refs[3 * batches : -3]
    kept_ref, total_ref, c_ref = refs[-3:]

    @pl.when(pl.program_id(0) == 0)
    def _():
        c_ref[...] = jnp.concatenate([ref[...] for ref in c_refs], 0)

    hidden = dot_nt(c_ref[...], wd_ref[0])
    gate_grad = (hidden * jnp.concatenate([ref[...] for ref in gate_refs], 0).astype(F32)).astype(LOW)
    up_grad = (hidden * jnp.concatenate([ref[...] for ref in up_refs], 0).astype(F32)).astype(LOW)
    kept_ref[0] = gate_grad
    kept_ref[1] = up_grad
    accumulate(total_ref, dot_nt(gate_grad, wg_ref[0]) + dot_nt(up_grad, wu_ref[0]))
    hand_out(total_ref, out_refs)


def experts_backward(c, to_up, to_gate, wg, wu, wd, own, parts):
    batches = len(c)
    rows, width = c[0].shape
    count, _, units = wg.shape
    kept = pl.BlockSpec((rows, units), lambda e: (0, e))
    block = (batches, own, width)
    return pl.pallas_call(
        functools.partial(experts_backward_kernel, batches),
        grid=(count,),
        in_specs=[pl.BlockSpec((rows, width), lambda e: (0, 0))] * batches
        + [kept] * 2 * batches
        + [
            pl.BlockSpec((1, width, units), lambda e: (e, 0, 0)),
            pl.BlockSpec((1, width, units), lambda e: (e, 0, 0)),
            pl.BlockSpec((1, units, width), lambda e: (e, 0, 0)),
        ],
        out_specs=[pl.BlockSpec(block, lambda e: (0, 0, 0))] * parts
        + [pl.BlockSpec((2, batches * rows, units), lambda e: (0, 0, e))],
        out_shape=[jax.ShapeDtypeStruct(block, LOW)] * parts
        + [jax.ShapeDtypeStruct((2, batches * rows, units * count), LOW)],
        scratch_shapes=[pltpu.VMEM((batches * rows, width), F32), pltpu.VMEM((batches * rows, width), LOW)],
        compiler_params=params("arbitrary", mib=34),
        name="experts_backward",
    )(*c, *to_up, *to_gate, wg, wu, wd)


def head_grads(queries, key, value, douts, bias):
    probs = softmax_parts(queries, key, bias)
    dprobs = dot_nt(douts, value)
    centre = jnp.sum(probs * dprobs, -1, keepdims=True)
    dscores = (probs * (dprobs - centre) * 0.125).astype(LOW)
    return dot(dscores, key), dot_tn(dscores, queries), dot_tn(probs.astype(LOW), douts)


def stacked_heads(values, pair):
    return jnp.concatenate([head(values, pair * GROUP + j) for j in range(GROUP)], 0)


def chunk_grads(q, k, v, dout, bias):
    rows = q.shape[0]
    bias = jnp.concatenate([bias] * GROUP, 0)
    dqs, dks, dvs = [], [], []
    for pair in range(k.shape[1] // HEAD_SIZE):
        dquery, dkey, dvalue = head_grads(stacked_heads(q, pair), head(k, pair), head(v, pair), stacked_heads(dout, pair), bias)
        dqs += [dquery[j * rows : (j + 1) * rows] for j in range(GROUP)]
        dks.append(dkey)
        dvs.append(dvalue)
    return jnp.concatenate(dqs, -1), jnp.concatenate(dks, -1), jnp.concatenate(dvs, -1).astype(LOW)


def turned_back(grads, cos, sin):
    lanes = grads.shape[-1]
    return (grads * widen_table(cos, lanes) + swap_halves(grads * widen_table(sin, lanes))).astype(LOW)


def attend_backward_kernel(batches, parts, z_ref, *refs):
    q_refs, k_refs, v_refs = (refs[i * batches : (i + 1) * batches] for i in range(3))
    da_refs = refs[3 * batches : 3 * batches + parts]
    wo_ref, wq_ref, wk_ref, wv_ref, bias_ref, cos_ref, sin_ref, dqkv_ref, dn_ref = refs[3 * batches + parts :]

    def turn(q_ref, k_ref, v_ref):
        da = jnp.concatenate([ref[0] for ref in da_refs], 0)
        dout = dot_nt(da, wo_ref[...]).astype(LOW)
        dq, dk, dv = chunk_grads(q_ref[0], k_ref[0], v_ref[0], dout, bias_ref[0])
        dq, dk = turned_back(dq, cos_ref[...], sin_ref[...]), turned_back(dk, cos_ref[...], sin_ref[...])
        dqkv_ref[...] = jnp.concatenate([dq, dk, dv], -1)
        dn = dot_nt(dq, wq_ref[...]) + dot_nt(dk, wk_ref[...]) + dot_nt(dv, wv_ref[...])
        own = dn_ref.shape[2]
        for j in range(parts):
            dn_ref[lax.rem(z_ref[0] + parts - j, parts), 0] = dn[j * own : (j + 1) * own].astype(LOW)

    for b in range(batches):

        @pl.when(pl.program_id(0) == b)
        def _(b=b):
            turn(q_refs[b], k_refs[b], v_refs[b])


def attend_backward(z, qkv, da, wo, wq, wk, wv, bias, cos, sin, parts):
    batches, rows = len(qkv), qkv[0].shape[1]
    _, own, width = da[0].shape
    q_lanes, k_lanes = wo.shape[0] // parts, KEY_VALUE_HEADS * HEAD_SIZE // parts
    k_at = wo.shape[0] // k_lanes
    full = lambda *shape: pl.BlockSpec(shape, lambda b, z: (0,) * len(shape))
    batch = lambda *shape: pl.BlockSpec((1,) + shape, lambda b, z: (b, 0, 0))
    columns = lambda lanes: pl.BlockSpec((width, lanes), lambda b, z: (0, z[0]))
    return pl.pallas_call(
        functools.partial(attend_backward_kernel, batches, parts),
        grid_spec=pltpu.PrefetchScalarGridSpec(
            num_scalar_prefetch=1,
            grid=(batches,),
            in_specs=[pl.BlockSpec((1, rows, q_lanes), lambda b, z: (0, 0, z[0]))] * batches
            + [pl.BlockSpec((1, rows, k_lanes), lambda b, z: (0, 0, k_at + z[0]))] * batches
            + [pl.BlockSpec((1, rows, k_lanes), lambda b, z: (0, 0, k_at + parts + z[0]))] * batches
            + [batch(own, width)] * parts
            + [
                pl.BlockSpec((q_lanes, width), lambda b, z: (z[0], 0)),
                columns(q_lanes),
                columns(k_lanes),
                columns(k_lanes),
                batch(rows, rows),
                full(rows, cos.shape[1]),
                full(rows, cos.shape[1]),
            ],
            out_specs=[
                pl.BlockSpec((rows, q_lanes + 2 * k_lanes), lambda b, z: (b, 0)),
                pl.BlockSpec((parts, 1, own, width), lambda b, z: (0, b, 0, 0)),
            ],
        ),
        out_shape=[
            jax.ShapeDtypeStruct((batches * rows, q_lanes + 2 * k_lanes), LOW),
            jax.ShapeDtypeStruct((parts, batches, own, width), LOW),
        ],
        compiler_params=params("arbitrary", mib=56),
        name="attend_backward",
    )(z, *qkv, *qkv, *qkv, *da, wo, wq, wk, wv, bias, cos, sin)


def own_backward_kernel(q_ref, k_ref, v_ref, da_ref, wo_ref, bias_ref, cos_ref, sin_ref, dq_ref, *out_refs):
    batches, own, _ = q_ref.shape
    da = jnp.concatenate([da_ref[b] for b in range(batches)], 0)
    dout = dot_nt(da, wo_ref[...]).astype(LOW)
    lanes = k_ref.shape[-1]
    at = pl.multiple_of(pl.program_id(0) * lanes, lanes)
    middle = out_refs[0].shape[-1] // 2
    for b in range(batches):
        dq, dk, dv = chunk_grads(q_ref[b], k_ref[b], v_ref[b], dout[b * own : (b + 1) * own], bias_ref[b])
        dq_ref[b] = turned_back(dq, cos_ref[:own], sin_ref[:own])
        dk = turned_back(dk, cos_ref[...], sin_ref[...])
        for j, ref in enumerate(out_refs):
            ref[b, :, pl.ds(at, lanes)] = dk[j * own : (j + 1) * own]
            ref[b, :, pl.ds(middle + at, lanes)] = dv[j * own : (j + 1) * own]


def own_backward(qkv, da, wo, bias, cos, sin, parts):
    batches, own, width = da.shape
    rows = qkv.shape[1]
    k_lanes = KEY_VALUE_HEADS * HEAD_SIZE // parts
    q_lanes = k_lanes * GROUP
    k_at = parts * GROUP
    full = lambda *shape: pl.BlockSpec(shape, lambda c: (0,) * len(shape))
    block = (batches, own, 2 * k_lanes * parts)
    return pl.pallas_call(
        own_backward_kernel,
        grid=(parts,),
        in_specs=[
            pl.BlockSpec((batches, own, q_lanes), lambda c: (0, 0, c)),
            pl.BlockSpec((batches, rows, k_lanes), lambda c: (0, 0, k_at + c)),
            pl.BlockSpec((batches, rows, k_lanes), lambda c: (0, 0, k_at + parts + c)),
            full(batches, own, width),
            pl.BlockSpec((q_lanes, width), lambda c: (c, 0)),
            full(batches, own, rows),
            full(rows, cos.shape[1]),
            full(rows, cos.shape[1]),
        ],
        out_specs=[pl.BlockSpec((batches, own, q_lanes), lambda c: (0, 0, c))] + [full(*block)] * parts,
        out_shape=[jax.ShapeDtypeStruct((batches, own, q_lanes * parts), LOW)] + [jax.ShapeDtypeStruct(block, LOW)] * parts,
        compiler_params=params("arbitrary"),
        name="own_backward",
    )(qkv, qkv, qkv, da, wo, bias, cos, sin)


def chip_block(place_ref, x, y, core):
    ring = lax.rem(place_ref[0] + x, RING)
    pair = lax.rem(place_ref[1] + y, PAIR)
    return (ring * PAIR + pair) * CORES + lax.rem(place_ref[2] + core, CORES)


def expert_grad_kernel(cut, batches, place_ref, *refs):
    left_refs, right_refs = refs[:batches], refs[batches:-3]
    mine_ref, other_ref, turned_ref = refs[-3:]
    tokens = left_refs[0].shape[0]
    rows = mine_ref.shape[-2] // cut
    lanes = mine_ref.shape[-1]
    step = pl.program_id(1)
    if cut == 1:

        @pl.when((pl.program_id(0) == 0) & (step == 0))
        def _():
            for i, ref in enumerate(left_refs):
                turned_ref[:, i * tokens : (i + 1) * tokens] = ref[...].T

        product = dot(turned_ref[...], right_refs[0][0]).astype(LOW)
    else:
        products = [dot_tn(left[...], right[0]) for left, right in zip(left_refs, right_refs)]
        product = sum(products[1:], products[0]).astype(LOW)
    half = lax.rem(step, 2)

    def place(refs, ring_first):
        for i in range(RING):
            x = lax.rem(i + RING - place_ref[0], RING)
            for j in range(PAIR):
                y = lax.rem(j + PAIR - place_ref[1], PAIR)
                index = (x * 2 + half) * PAIR + y if ring_first else (y * RING + x) * 2 + half
                for core in range(CORES):
                    at = ((i * PAIR + j) * CORES + core) * rows
                    for part in range(cut):
                        value = product[at : at + rows, part * lanes : (part + 1) * lanes]
                        refs[core][0, 0, index, part * rows : (part + 1) * rows] = value

    for core in range(CORES):
        for ring_first in (True, False):

            @pl.when((place_ref[2] == core) & ((step < 2) == ring_first))
            def _(core=core, ring_first=ring_first):
                place((mine_ref, other_ref) if core == 0 else (other_ref, mine_ref), ring_first)


def expert_grad(place, lefts, rights, count, cut):
    number, right_rows, right_lanes = rights[0].shape
    rows, left_lanes = lefts[0].shape
    if cut > 1:
        left_lanes = left_lanes // count
    else:
        right_lanes = right_lanes // count
    owners = RING * PAIR * CORES
    high, lanes = left_lanes // owners, right_lanes // cut
    shape = (2, owners, high * cut, lanes)
    out = pl.BlockSpec((1, 1) + shape[1:], lambda r, e, p: (r, e // 2, 0, 0, 0))
    left_spec = pl.BlockSpec((rows, left_lanes), lambda r, e, p: (0, e if cut > 1 else 0))
    right_spec = pl.BlockSpec((1, right_rows, right_lanes), lambda r, e, p: (r, 0, 0 if cut > 1 else e))
    batches = len(lefts)
    return pl.pallas_call(
        functools.partial(expert_grad_kernel, cut, batches),
        grid_spec=pltpu.PrefetchScalarGridSpec(
            num_scalar_prefetch=1,
            grid=(number, count),
            in_specs=[left_spec] * batches + [right_spec] * len(rights),
            out_specs=[out, out],
            scratch_shapes=[pltpu.VMEM((left_lanes, rows * batches) if cut == 1 else (16, 128), LOW)],
        ),
        out_shape=[jax.ShapeDtypeStruct((number,) + shape, LOW)] * 2,
        compiler_params=params("arbitrary", "arbitrary"),
        name="expert_grad",
    )(place, *lefts, *rights)


def chip_sum_kernel(
    mine_inner, other_inner, mine_outer, other_outer, keep_ring, to_above, to_below, keep_pair, to_pair, to_pair_next
):
    matrix, kind = pl.program_id(0), pl.program_id(1)
    ring = {index: (keep_ring, at) for at, index in enumerate((0, 1, 2, 7))}
    ring.update({3: (to_above, 0), 4: (to_above, 1), 5: (to_below, 0), 6: (to_below, 1)})

    def add(mine, other, ring_first):
        for index in range(2 * RING * PAIR):
            value = mine[0, 0, index] + other[0, 0, index]
            if ring_first:
                ref, at = ring[index // PAIR]
                ref[at, index % PAIR, 0] = value
            elif index < 2 * RING:
                keep_pair[index, 0] = value
            else:
                (to_pair if index < 3 * RING else to_pair_next)[index % RING, 0] = value

    for inner in (True, False):
        for ring_first in (True, False):

            @pl.when(((matrix < 2) == inner) & ((kind == 0) == ring_first))
            def _(inner=inner, ring_first=ring_first):
                add(*((mine_inner, other_inner) if inner else (mine_outer, other_outer)), ring_first)


def chip_sum(inner, outer):
    tile = inner[0].shape[3:]
    block = (1, 1, 2 * RING * PAIR) + tile
    inner_spec = pl.BlockSpec(block, lambda m, k: (jnp.minimum(m, 1), jnp.where(m < 2, k, 1), 0, 0, 0))
    outer_spec = pl.BlockSpec(block, lambda m, k: (0, jnp.where(m < 2, 0, k), 0, 0, 0))
    shapes = [(4, PAIR), (2, PAIR), (2, PAIR), (2 * RING,), (RING,), (RING,)]
    return pl.pallas_call(
        chip_sum_kernel,
        grid=(3, 2),
        in_specs=[inner_spec, inner_spec, outer_spec, outer_spec],
        out_specs=[pl.BlockSpec(shape + (1,) + tile, lambda m, k, n=len(shape): (0,) * n + (m, 0, 0)) for shape in shapes],
        out_shape=[jax.ShapeDtypeStruct(shape + (3,) + tile, LOW) for shape in shapes],
        compiler_params=params("arbitrary", "arbitrary", mib=56),
        name="chip_sum",
    )(*inner, *outer)


def dense_grad_kernel(batches, parts, place_ref, z_ref, *refs):
    del z_ref
    mixed_refs, xn_refs, da_refs = refs[:batches], refs[batches : 2 * batches], refs[2 * batches : 2 * batches + parts]
    dqkv_ref, mine_ref, other_ref, into_ref, out_of_ref = refs[2 * batches + parts :]
    rows = xn_refs[0].shape[0]
    high = mine_ref.shape[-2]
    lanes, wide = out_of_ref.shape[-1], dqkv_ref.shape[1]
    into = sum(dot_tn(ref[...], dqkv_ref[b * rows : (b + 1) * rows]) for b, ref in enumerate(xn_refs)).astype(LOW)
    da = [jnp.concatenate([ref[b] for ref in da_refs], 0) for b in range(batches)]
    out_of = sum(dot_tn(ref[...], da[b]) for b, ref in enumerate(mixed_refs)).astype(LOW)
    for chip in range(RING * PAIR):
        for core in range(CORES):
            owner = chip * CORES + core
            for half in range(2):
                at = (owner * 2 + half) * high
                into_ref[owner, half] = into[at : at + high]
                at = (half * CORES + core) * lanes
                out_of_ref[owner, half] = out_of[chip * high : (chip + 1) * high, at : at + lanes]
    for core, ref in enumerate((mine_ref, other_ref)):
        for x in range(RING):
            for y in range(PAIR):
                owner = chip_block(place_ref, x, y, core)
                for half in range(2):
                    ref[x * 2 + half, y, :, :wide] = into_ref[owner, half]
                    ref[x * 2 + half, y, :, wide:] = out_of_ref[owner, half]


def dense_grad(place, z, mixed, da, xn, dqkv, parts):
    batches = len(xn)
    rows, width = xn[0].shape
    owners = RING * PAIR * CORES
    q_lanes, wide = mixed[0].shape[1] // parts, dqkv.shape[1]
    high, lanes = width // owners // 2, width // CORES // 2
    shape = (2 * RING, PAIR, high, wide + lanes)
    whole = lambda *shape: pl.BlockSpec(shape, lambda i, p, z: (0,) * len(shape))
    return pl.pallas_call(
        functools.partial(dense_grad_kernel, batches, parts),
        grid_spec=pltpu.PrefetchScalarGridSpec(
            num_scalar_prefetch=2,
            grid=(1,),
            in_specs=[pl.BlockSpec((rows, q_lanes), lambda i, p, z: (0, z[0]))] * batches
            + [whole(rows, width)] * batches
            + [whole(*da[0].shape)] * parts
            + [whole(*dqkv.shape)],
            out_specs=[pl.BlockSpec(shape, lambda i, p, z: (0,) * 4)] * 2,
            scratch_shapes=[pltpu.VMEM((owners, 2, high, wide), LOW), pltpu.VMEM((owners, 2, high, lanes), LOW)],
        ),
        out_shape=[jax.ShapeDtypeStruct(shape, LOW)] * 2,
        compiler_params=params("arbitrary", mib=56),
        name="dense_grad",
    )(place, z, *mixed, *xn, *da, dqkv)


def dense_layout_kernel(by_x, place_ref, z_ref, mine_ref, other_ref, *refs):
    outs = refs[-4:]
    parts = mine_ref.shape[2] if by_x else mine_ref.shape[0]
    for core, ref in enumerate((mine_ref, other_ref)):
        to_core = lax.rem(place_ref[2] + core, CORES)
        for y in range(PAIR):
            to_y = lax.rem(place_ref[1] + y, PAIR)
            for k in range(parts):
                at = lax.rem(z_ref[0] + parts - k, parts)
                start = 0
                for out in outs:
                    to_rows = out is outs[3]
                    lanes = out.shape[-1] // (CORES if to_rows else parts)
                    index = (0, y, k) if by_x else (k, y, 0)
                    value = ref[index + (slice(None), slice(start, start + lanes))].astype(F32)
                    if to_rows:
                        out[at, 0, to_y, :, pl.ds(pl.multiple_of(to_core * lanes, 128), lanes)] = value
                    else:
                        out[0, to_y, to_core, 0, :, pl.ds(pl.multiple_of(at * lanes, 128), lanes)] = value
                    start += lanes


def dense_layout(place, z, half, mine, other, shapes, before):
    by_x = half == 0
    high, lanes = mine.shape[-2:]
    parts = mine.shape[2] if by_x else mine.shape[0]
    if by_x:
        source = pl.BlockSpec((1, PAIR, parts, high, lanes), lambda x, p, z: (x, 0, 0, 0, 0))
    else:
        source = pl.BlockSpec((parts, PAIR, 1, high, lanes), lambda x, p, z: (0, 0, x, 0, 0))
    ring = lambda x, p: lax.rem(p[0] + RING - x, RING)
    width = shapes[3][1]
    shapes = [(RING, PAIR, CORES, 2, high, shape[1]) for shape in shapes[:3]] + [(parts, RING, PAIR, high, width)]
    out_specs = [
        pl.BlockSpec((1, PAIR, CORES, 1, high, shape[-1]), lambda x, p, z: (ring(x, p), 0, 0, half, 0, 0)) for shape in shapes[:3]
    ] + [pl.BlockSpec((parts, 1, PAIR, high, width // 2), lambda x, p, z: (0, ring(x, p), 0, 0, half))]
    return pl.pallas_call(
        functools.partial(dense_layout_kernel, by_x),
        grid_spec=pltpu.PrefetchScalarGridSpec(
            num_scalar_prefetch=2,
            grid=(RING,),
            in_specs=[source, source] + [pl.BlockSpec(memory_space=pl.ANY)] * len(before),
            out_specs=out_specs,
        ),
        out_shape=[jax.ShapeDtypeStruct(shape, F32) for shape in shapes],
        input_output_aliases={4 + i: i for i in range(len(before))},
        compiler_params=params("arbitrary"),
        cost_estimate=pl.CostEstimate(flops=0, bytes_accessed=24 * mine.size, transcendentals=0),
        name="dense_layout",
    )(place, z, mine, other, *before)


def norm_back(grad_normed, values, gain):
    scale = lax.rsqrt(jnp.mean(values * values, -1, keepdims=True) + EPS)
    scaled = grad_normed * gain
    gain_grad = jnp.sum(grad_normed * values * scale, (0, 1))
    inner = jnp.mean(scaled * values, -1, keepdims=True)
    return (scale * scaled - values * scale * scale * scale * inner, gain_grad)


def local(
    block_input, segments, expert_ids, route_weights, attn_gain, w_query, key_projection_weight,
    value_projection_weight, w_out, ffn_gain, w_gate, w_up, w_down, out_grad,
):
    parts = lax.axis_size("expert")
    section = lax.axis_index("section")
    z = lax.axis_index("expert")
    z_at = z.reshape(1)
    dp = lax.axis_index("dp")
    dp_place = jnp.stack([dp // (PAIR * CORES), dp // CORES % PAIR, dp % CORES])
    batches, own, width = block_input.shape
    rows = parts * own
    wq, wk, wv, wo = w_query[0], key_projection_weight[0], value_projection_weight[0], w_out[0]
    local_experts, units = w_gate.shape[1], w_gate.shape[3]

    outer = w_down[0].reshape(local_experts, -1, width // units, units)
    outer = jnp.swapaxes(outer, 1, 2).reshape(w_gate[0].shape)
    shard = jnp.stack([w_gate[0], w_up[0], outer], 1)
    near, far = shard[:2], shard[2:]
    numbers = jnp.arange(parts * local_experts, dtype=jnp.int32)
    hits = expert_ids[0][..., None] == numbers
    shares = jnp.sum(jnp.where(hits, route_weights[0][..., None], 0.0), 2)
    shares = jnp.concatenate([shares, segments.astype(F32)[..., None]], -1)
    start = spread_group(block_input)
    near_y = moved(near, y=1)
    far_1 = ring_gather_step(far)
    shares = spread_group(shares)
    start, near_y, far_1, shares = hold(start, near_y, far_1, shares)

    start = jnp.concatenate(start, 1)
    shares = jnp.concatenate(shares, 1)
    labels = shares[..., -1]
    shares = shares[..., :-1].reshape(batches * rows, parts, local_experts)
    share = lax.dynamic_index_in_dim(shares, z, 1, keepdims=False).T[..., None]
    block = jnp.arange(parts, dtype=jnp.int32)[:, None]
    place = ((z - block) % parts * own + jnp.arange(own, dtype=jnp.int32)[None, :]).reshape(rows)
    allowed = (place[None, None, :] <= place[None, :, None]) & (labels[:, None, :] == labels[:, :, None])
    bias = jnp.where(allowed, 0.0, -1e30).astype(F32)
    half = HEAD_SIZE // 2
    frequency = 10000.0 ** (-jnp.arange(half, dtype=F32) * 2.0 / HEAD_SIZE)
    angles = place.astype(F32)[:, None] * frequency[None, :]
    cos_half, sin_half = jnp.cos(angles), jnp.sin(angles)
    cos = jnp.concatenate([cos_half] * 4, -1)
    sin = jnp.concatenate([-sin_half, sin_half] * 2, -1)
    cos_all, sin_all = jnp.concatenate([cos] * batches, 0), jnp.concatenate([sin] * batches, 0)

    def attention_in(x, cos, sin):
        qkv, xn = project(x.reshape(-1, width), attn_gain, wq, wk, wv, cos, sin)
        return qkv.reshape(-1, rows, qkv.shape[1]), xn

    def attention_out(qkv, bias, x):
        mixed = attend(qkv, bias, parts)
        h1, xn2 = join(mixed, x, wo, ffn_gain, own)
        return mixed.reshape(-1, wo.shape[0]), h1, xn2.reshape(-1, width)

    near = jnp.stack([near, near_y])
    near_1 = ring_gather_step(near)
    far_2 = ring_gather_next(far_1)
    far_a = jnp.stack([far, *far_1])
    far_ya = moved(far_a, y=1)
    qkv, _ = attention_in(start, cos_all, sin_all)
    _, h1, xn2 = attention_out(qkv, bias, start)

    xn2, near_1, far_2, far_ya = hold(xn2, near_1, far_2, far_ya)
    near_b = moved(near_1[0][:, 0], x=1), moved(near_1[1][:, 1], x=-1)
    far_b = jnp.stack(far_2)
    far_yb = moved(far_b, y=1)
    near_a = jnp.stack([near, *near_1])
    others = [moved(piece, core=1) for piece in (near_a, far_a)]

    near_b, far_yb, others = hold(near_b, far_yb, others)
    near_b = jnp.stack(near_b)
    pieces = [near_a, near_b, far_a, far_b, far_ya, far_yb]
    pieces += [others[0], moved(near_b, core=1), others[1], *[moved(piece, core=1) for piece in (far_b, far_ya, far_yb)]]
    *blocks, wg, wu, wd = experts_forward(dp_place, xn2, share, pieces, batches, own, parts)
    blocks = [blocks[b * parts : (b + 1) * parts] for b in range(batches)]
    c_second = lax.all_gather(out_grad, "expert")
    c_second = jnp.concatenate([lax.dynamic_index_in_dim(c_second, (z + parts - j) % parts, 0, False) for j in range(parts)], 1)
    flat_second = c_second.reshape(batches * rows, width)
    received = []
    result = None
    for b in range(batches):
        came = owners_step(blocks[b])
        if b > 0:
            came = once(came, result)
        result = (h1[b : b + 1] + added(*came)).astype(LOW)
        received.append(spread_group(across(result)))

    biases = [bias[b : b + 1] for b in range(batches)]
    x, qkv, xn, mixed, h1, xn2, hidden, to_up, to_gate, blocks = ([None] * batches for _ in range(10))
    for b in range(batches):
        if b > 0:
            received[b] = once(received[b], hidden[b - 1])
        x[b] = jnp.where(section == 0, start[b : b + 1], jnp.concatenate(received[b], 1))
        qkv[b], xn[b] = attention_in(x[b], cos, sin)
        mixed[b], h1[b], xn2[b] = attention_out(qkv[b], biases[b], x[b])
        hidden[b], to_up[b], to_gate[b], *blocks[b] = experts_turn(xn2[b], flat_second, share, wg, wu, wd, b, own, parts)
    x_own = jnp.concatenate([rows_of[:, :own] for rows_of in x], 0).astype(F32)

    after, dq, kv_came = ([None] * batches for _ in range(3))
    for b in range(batches):
        came = owners_step(blocks[b])
        if b > 0:
            came = once(came, dq[b - 1])
        after[b] = out_grad[b : b + 1].astype(F32) + norm_back(added(*came), h1[b], ffn_gain)[0]
        dq[b], *kv_blocks = own_backward(qkv[b], after[b].astype(LOW), wo, biases[b], cos, sin, parts)
        kv_came[b] = owners_step(kv_blocks)
    kv_came[0] = once(kv_came[0], dq[-1])
    received_own = []
    for b in range(batches):
        if b > 0:
            kv_came[b] = once(kv_came[b], input_grad)
        dkv = added(*kv_came[b]).astype(LOW).reshape(own, -1)
        dn_own = dot_nt(dq[b].reshape(own, -1), wq)
        dn_own = dn_own + dot_nt(dkv[:, : wk.shape[1]], wk) + dot_nt(dkv[:, wk.shape[1] :], wv)
        input_grad = after[b] + norm_back(dn_own[None], x_own[b : b + 1], attn_gain)[0]
        received_own.append(across(input_grad.astype(LOW)))

    c_own = jnp.where(section == 1, out_grad, jnp.concatenate(received_own, 0))
    c = [jnp.where(section == 1, c_second[b : b + 1], gather_group(received_own[b])).reshape(rows, width) for b in range(batches)]
    *blocks, hidden_grads = experts_backward(c, to_up, to_gate, wg, wu, wd, own, parts)
    norm_part, ffn_grad = norm_back(added(*owners_step(blocks)), jnp.concatenate(h1, 0), ffn_gain)
    after = c_own.astype(F32) + norm_part
    both = [
        expert_grad(dp_place, xn2, [hidden_grads], local_experts, 1),
        expert_grad(dp_place, hidden, [block[None] for block in c], local_experts, width // units),
    ]
    after, both = hold(after, both)
    inner, outer = [(mine, moved(other, core=1)) for mine, other in both]
    da = spread_group(after.astype(LOW))
    outputs = [dot(units_of, wd.reshape(local_experts * units, width)).astype(LOW) for units_of in once(hidden, inner[1])]
    outputs = jnp.stack(outputs).reshape(batches, parts, own, width)
    outputs = jnp.stack([lax.dynamic_index_in_dim(outputs, (z + parts - i) % parts, 1, False) for i in range(parts)])
    outer, outputs = hold(outer, outputs)
    keep_ring, to_above, to_below, keep_pair, *to_pair = chip_sum(inner, outer)
    da, to_above, to_below, to_pair = hold(da, to_above, to_below, to_pair)

    ring_1 = moved(to_above, x=1), moved(to_below, x=-1)
    pair_1 = [moved(block, y=1) for block in to_pair]
    dqkv, dn = attend_backward(z_at, qkv, da, wo, wq, wk, wv, bias, cos, sin, parts)
    mine, other = dense_grad(dp_place, z_at, mixed, da, xn, dqkv, parts)
    dn_own = lax.psum_scatter(dn, "expert", scatter_dimension=0, tiled=True)[0].astype(F32)
    mine, other, ring_1, pair_1[0] = hold(mine, other, ring_1, pair_1[0])
    dense = added(mine, moved(other, core=1)).astype(LOW)

    (dense,) = hold(dense)
    dense_1 = ring_step(dense)

    dense_1, outputs, dn_own, ring_1 = hold(dense_1, outputs, dn_own, ring_1)
    outputs = lax.psum_scatter(outputs, "expert", scatter_dimension=0, tiled=True)[0]
    dense_2 = ring_next((dense[2], dense[7]), dense_1)
    norm_part, attn_grad = norm_back(dn_own, x_own, attn_gain)
    input_grad = after + norm_part
    gains = jnp.stack([attn_grad, ffn_grad])
    gains = gains + exchanged(gains, "expert", 1)
    ring_2 = ring_next((keep_ring[2], keep_ring[3]), ring_1)

    dense_2, gains, pair_1 = hold(dense_2, gains, pair_1)
    dense = ring_end(dense, dense_1, dense_2)
    dense_3 = moved(dense[:, 1].astype(LOW), y=1)
    pair_sums = added(keep_pair, jnp.concatenate(pair_1, 0)).astype(LOW)
    pair_2 = ring_step(pair_sums)
    gains = gains + exchanged(gains, "expert", 2)

    dense_3, gains, ring_2, pair_2 = hold(dense_3, gains, ring_2, pair_2)
    ring_sums = ring_end(keep_ring, ring_1, ring_2)
    first, second = (added(dense[half, 0], dense_3[half]).astype(LOW) for half in range(2))
    first_1 = [shifted(first, k) for k in range(1, parts)]
    second_1 = [moved(second, x=k) for k in range(1, RING)]

    first_1, second_1 = hold(first_1, second_1)
    first = jnp.stack([first] + first_1)
    first_2 = moved(first, y=1)
    second = jnp.stack([second] + second_1)
    second_2 = moved(second, y=1)
    pair_3 = ring_next((pair_sums[2], pair_sums[7]), pair_2)
    gains = gains + exchanged(gains, "dp", 1)

    first_2, second_2, gains, pair_3 = hold(first_2, second_2, gains, pair_3)
    first = jnp.stack([first, first_2])
    first_3 = moved(first, x=1), moved(first, x=-1)
    second = jnp.stack([second, second_2])
    second_3 = shifted(second, 1), shifted(second, parts - 1)
    ring_away = moved(ring_sums[:, 1].astype(LOW), y=1)

    first_3, second_3, ring_away, gains = hold(first_3, second_3, ring_away, gains)
    first_4, second_4 = moved(first, x=2), shifted(second, 2)
    gains = gains + exchanged(gains, "dp", 2)
    ring_sums = added(ring_sums[:, 0], ring_away)
    pair_sums = ring_end(pair_sums, pair_2, pair_3)
    w_gate_grad, w_up_grad, w_down_grad = (jnp.concatenate([ring_sums[:, i], pair_sums[:, i]], 0) for i in range(3))
    w_down_grad = w_down_grad.reshape(local_experts, width // units, -1, units)
    w_down_grad = jnp.swapaxes(w_down_grad, 1, 2).reshape(local_experts, -1, width)

    first_4, second_4, w_gate_grad, w_up_grad, w_down_grad, gains, outputs = hold(
        first_4, second_4, w_gate_grad, w_up_grad, w_down_grad, gains, outputs
    )
    first = jnp.stack([first, first_3[0], first_4, first_3[1]])
    first_other = moved(first, core=1)
    gains = gains + exchanged(gains, "dp", 4)

    second = jnp.stack([second, second_3[0], second_4, second_3[1]])
    second, first_other, gains = hold(second, first_other, gains)
    second_other = moved(second, core=1)
    shapes = (wq.shape, wk.shape, wv.shape, wo.shape)
    laid = dense_layout(dp_place, z_at, 0, first, first_other, shapes, ())
    gains = gains + exchanged(gains, "dp", 8)

    second_other, laid = hold(second_other, laid)
    laid = dense_layout(dp_place, z_at, 1, second, second_other, shapes, laid)
    w_query_grad, w_key_grad, w_value_grad, w_out_grad = (
        grad.reshape(weight.shape) for grad, weight in zip(laid, (wq, wk, wv, wo))
    )

    layer_outputs = (jnp.concatenate(h1, 0) + outputs.astype(F32)).astype(LOW)
    return (
        layer_outputs[None],
        input_grad[None],
        gains[0:1],
        w_query_grad[None],
        w_key_grad[None],
        w_value_grad[None],
        w_out_grad[None],
        gains[1:2],
        w_gate_grad[None],
        w_up_grad[None],
        w_down_grad[None],
    )


def solution(mesh):
    tokens = P(None, ("dp", "expert"), None)
    layered = P("section", None, ("dp", "expert"), None)
    vector = P("section", None)
    matrix = P("section", None, None)
    expert = P("section", "expert", "dp", None)
    return jax.shard_map(
        local,
        mesh=mesh,
        in_specs=(
            tokens, P(None, ("dp", "expert")), layered, layered, vector, matrix, matrix, matrix, matrix,
            vector, expert, expert, expert, tokens,
        ),
        out_specs=(layered, layered, vector, matrix, matrix, matrix, matrix, vector, expert, expert, expert),
        check_vma=False,
    )
```

```python
import functools

import jax
import jax.numpy as jnp
from jax import lax
from jax.experimental import pallas as pl
from jax.experimental.pallas import tpu as pltpu
from jax.sharding import PartitionSpec as P

QUERY_HEADS = 24
KEY_VALUE_HEADS = 8
HEAD_SIZE = 64
GROUP = QUERY_HEADS // KEY_VALUE_HEADS
EPS = 1e-06
LOW = jnp.bfloat16
F32 = jnp.float32
MIB = 1024 * 1024


def params(*semantics, mib=30):
    return pltpu.CompilerParams(dimension_semantics=semantics, vmem_limit_bytes=mib * MIB)


def dot(left, right):
    return jnp.dot(left, right, preferred_element_type=F32)


def dot_nt(left, right):
    return lax.dot_general(left, right, (((1,), (1,)), ((), ())), preferred_element_type=F32)


def dot_tn(left, right):
    return lax.dot_general(left, right, (((0,), (0,)), ((), ())), preferred_element_type=F32)


def shifted(block, by):
    size = lax.axis_size("expert")
    return lax.ppermute(block, "expert", [(i, (i + by) % size) for i in range(size)])


def spread_group(block):
    return [block] + [shifted(block, j) for j in range(1, lax.axis_size("expert"))]


def gather_group(block):
    return jnp.concatenate(spread_group(block), 1)


def owners_step(blocks):
    size = len(blocks)
    return [blocks[0]] + [shifted(blocks[j], size - j) for j in range(1, size)]


def across(block):
    return lax.ppermute(block, "section", [(0, 1), (1, 0)])


RING, PAIR, CORES = 4, 2, 2


def moved(block, x=0, y=0, core=0):
    route = []
    for i in range(RING):
        for j in range(PAIR):
            for k in range(CORES):
                target = ((i + x) % RING * PAIR + (j + y) % PAIR) * CORES + (k + core) % CORES
                route.append(((i * PAIR + j) * CORES + k, target))
    return lax.ppermute(block, "dp", route)


def added(*terms):
    total = terms[0].astype(F32)
    for term in terms[1:]:
        total = total + term.astype(F32)
    return total


def ring_step(blocks):
    return moved(blocks[3:5], x=1), moved(blocks[5:7], x=-1)


def ring_next(stays, step):
    below = moved(added(stays[0], step[0][1]).astype(LOW), x=1)
    above = moved(added(stays[1], step[1][0]).astype(LOW), x=-1)
    return below, above


def ring_end(stays, step, last):
    return jnp.stack([added(stays[0], step[1][1], last[0]), added(stays[1], step[0][0], last[1])])


def ring_gather_step(block):
    return moved(block, x=1), moved(block, x=-1)


def ring_gather_next(step):
    return moved(step[0][0], x=1), moved(step[1][1], x=-1)


def exchanged(values, axis, bit):
    return lax.ppermute(values, axis, [(i, i ^ bit) for i in range(lax.axis_size(axis))])


def hold(*values):
    return lax.optimization_barrier(values)


def once(values, *earlier):
    return hold(values, *earlier)[0]


def swap_halves(values):
    half = HEAD_SIZE // 2
    lanes = values.shape[-1]
    lane = lax.broadcasted_iota(jnp.int32, values.shape, values.ndim - 1)
    ahead = pltpu.roll(values, lanes - half, values.ndim - 1)
    behind = pltpu.roll(values, half, values.ndim - 1)
    return jnp.where(lane % HEAD_SIZE < half, ahead, behind)


def widen_table(table, lanes):
    return jnp.concatenate([table] * (lanes // table.shape[-1]), -1)


def project_kernel(query_steps, x_ref, gain_ref, wq_ref, wk_ref, wv_ref, cos_ref, sin_ref, out_ref, xn_ref):
    step = pl.program_id(0)

    @pl.when(step == 0)
    def _():
        wide = x_ref[...].astype(F32)
        scale = lax.rsqrt(jnp.mean(wide * wide, -1, keepdims=True) + EPS)
        xn_ref[...] = (wide * scale * gain_ref[...]).astype(LOW)

    def turned(weight):
        product = dot(xn_ref[...], weight)
        lanes = product.shape[-1]
        cos, sin = widen_table(cos_ref[...], lanes), widen_table(sin_ref[...], lanes)
        return (product * cos + swap_halves(product) * sin).astype(LOW)

    @pl.when(step < query_steps)
    def _():
        out_ref[...] = turned(wq_ref[...])

    @pl.when(step == query_steps)
    def _():
        out_ref[...] = turned(wk_ref[...])

    @pl.when(step == query_steps + 1)
    def _():
        out_ref[...] = dot(xn_ref[...], wv_ref[...]).astype(LOW)


def project(x, gain, wq, wk, wv, cos, sin):
    rows, width = x.shape
    lanes = wk.shape[1]
    query_steps = wq.shape[1] // lanes
    whole = lambda *shape: pl.BlockSpec(shape, lambda i: (0,) * len(shape))
    return pl.pallas_call(
        functools.partial(project_kernel, query_steps),
        grid=(query_steps + 2,),
        in_specs=[
            whole(rows, width),
            whole(1, width),
            pl.BlockSpec((width, lanes), lambda i: (0, jnp.minimum(i, query_steps - 1))),
            whole(width, lanes),
            whole(width, lanes),
            whole(rows, cos.shape[1]),
            whole(rows, cos.shape[1]),
        ],
        out_specs=[pl.BlockSpec((rows, lanes), lambda i: (0, i)), whole(rows, width)],
        out_shape=[
            jax.ShapeDtypeStruct((rows, lanes * (query_steps + 2)), LOW),
            jax.ShapeDtypeStruct((rows, width), LOW),
        ],
        compiler_params=params("arbitrary"),
        name="project",
    )(x, gain, wq, wk, wv, cos, sin)


def head(values, index):
    return values[:, index * HEAD_SIZE : (index + 1) * HEAD_SIZE]


def softmax_parts(stacked_q, key, bias):
    scores = dot_nt(stacked_q, key) * 0.125 + bias
    raised = jnp.exp(scores - jnp.max(scores, -1, keepdims=True))
    return raised * (1.0 / jnp.sum(raised, -1, keepdims=True))


def attend_kernel(q_ref, k_ref, v_ref, bias_ref, o_ref):
    bias = bias_ref[0]
    q, k, v = q_ref[0] * jnp.asarray(0.125, LOW), k_ref[0], v_ref[0]
    mixed = []
    for pair in range(k.shape[1] // HEAD_SIZE):
        key, value = head(k, pair), head(v, pair)
        for j in range(GROUP):
            scores = dot_nt(head(q, pair * GROUP + j), key) + bias
            raised = jnp.exp(scores - jnp.max(scores, -1, keepdims=True))
            total = jnp.sum(raised, -1, keepdims=True)
            mixed.append(dot(raised.astype(LOW), value) * (1.0 / total))
    o_ref[0] = jnp.concatenate(mixed, -1).astype(LOW)


def attend(qkv, bias, parts):
    batches, rows, lanes = qkv.shape
    k_lanes = KEY_VALUE_HEADS * HEAD_SIZE // parts
    q_lanes = k_lanes * GROUP
    k_at = parts * GROUP
    return pl.pallas_call(
        attend_kernel,
        grid=(batches, parts),
        in_specs=[
            pl.BlockSpec((1, rows, q_lanes), lambda b, c: (b, 0, c)),
            pl.BlockSpec((1, rows, k_lanes), lambda b, c: (b, 0, k_at + c)),
            pl.BlockSpec((1, rows, k_lanes), lambda b, c: (b, 0, k_at + parts + c)),
            pl.BlockSpec((1, rows, rows), lambda b, c: (b, 0, 0)),
        ],
        out_specs=pl.BlockSpec((1, rows, q_lanes), lambda b, c: (b, 0, c)),
        out_shape=jax.ShapeDtypeStruct((batches, rows, q_lanes * parts), LOW),
        compiler_params=params("arbitrary", "arbitrary"),
        name="attend",
    )(qkv, qkv, qkv, bias)


def join_kernel(o_ref, x_ref, wo_ref, gain_ref, h1_ref, xn2_ref):
    total = x_ref[0].astype(F32) + dot(o_ref[0], wo_ref[...])
    scale = lax.rsqrt(jnp.mean(total * total, -1, keepdims=True) + EPS)
    h1_ref[0] = total[: h1_ref.shape[1]]
    xn2_ref[0] = (total * scale * gain_ref[...]).astype(LOW)


def join(o, x, wo, gain, own):
    batches, rows, width = x.shape
    batch = lambda *shape: pl.BlockSpec((1,) + shape, lambda b: (b, 0, 0))
    whole = lambda *shape: pl.BlockSpec(shape, lambda b: (0, 0))
    return pl.pallas_call(
        join_kernel,
        grid=(batches,),
        in_specs=[batch(rows, wo.shape[0]), batch(rows, width), whole(*wo.shape), whole(1, width)],
        out_specs=[batch(own, width), batch(rows, width)],
        out_shape=[
            jax.ShapeDtypeStruct((batches, own, width), F32),
            jax.ShapeDtypeStruct((batches, rows, width), LOW),
        ],
        compiler_params=params("arbitrary"),
        name="join",
    )(o, x, wo, gain)


def expert_hidden(xn_ref, share_ref, wg_ref, wu_ref):
    gate, up = dot(xn_ref[...], wg_ref[0]), dot(xn_ref[...], wu_ref[0])
    share = share_ref[0]
    sigma = jax.nn.sigmoid(gate)
    silu = gate * sigma
    return gate, up, share, sigma, silu


def accumulate(total_ref, part):
    step = pl.program_id(0)

    @pl.when(step == 0)
    def _():
        total_ref[...] = part

    @pl.when(step > 0)
    def _():
        total_ref[...] += part


def hand_out(total_ref, out_refs):
    @pl.when(pl.program_id(0) == pl.num_programs(0) - 1)
    def _():
        batches, own, _ = out_refs[0].shape
        for b in range(batches):
            for j, ref in enumerate(out_refs):
                at = (b * len(out_refs) + j) * own
                ref[b] = total_ref[at : at + own].astype(LOW)


def experts_forward_kernel(place_ref, xn_ref, share_ref, *refs):
    pieces, out_refs = refs[:12], refs[12:-4]
    wg_ref, wu_ref, wd_ref, total_ref = refs[-4:]
    step = pl.program_id(0)
    high = wg_ref.shape[1] // (RING * PAIR * CORES)
    low = wd_ref.shape[1] // (RING * PAIR * CORES)

    def lay(block, x, y, core):
        ring = lax.rem(place_ref[0] + RING - x, RING)
        pair = lax.rem(place_ref[1] + y, PAIR)
        at = (ring * PAIR + pair) * CORES + lax.rem(place_ref[2] + core, CORES)
        rows = pl.ds(pl.multiple_of(at * high, high), high)
        wg_ref[0, rows] = block[0]
        wu_ref[0, rows] = block[1]
        outer = [block[2][k * low : (k + 1) * low] for k in range(high // low)]
        wd_ref[0, pl.ds(pl.multiple_of(at * low, low), low)] = jnp.concatenate(outer, -1)

    @pl.when(step < 2)
    def _():
        for core in range(CORES):
            near_a, near_b = pieces[core * 6 : core * 6 + 2]
            for y in range(PAIR):
                for i, x in enumerate((0, 1, 3)):
                    lay([near_a[i, y, 0, k] for k in range(3)], x, y, core)
                lay([near_b[0, y, k] for k in range(3)], 2, y, core)

    @pl.when(step >= 2)
    def _():
        for core in range(CORES):
            for n, ref in enumerate(pieces[core * 6 + 2 : core * 6 + 6]):
                for i, x in enumerate((0, 1, 3) if n % 2 == 0 else (2,)):
                    lay([ref[(i, 0, k) if n % 2 == 0 else (0, k)] for k in range(3)], x, n // 2, core)

    _, up, share, _, silu = expert_hidden(xn_ref, share_ref, wg_ref, wu_ref)
    accumulate(total_ref, dot((silu * up * share).astype(LOW), wd_ref[0]))
    hand_out(total_ref, out_refs)


def experts_forward(place, xn, share, pieces, batches, own, parts):
    rows, width = xn.shape
    count = share.shape[0]
    high, units = pieces[0].shape[-2:]
    tile = (3, high, units)
    near, far = (lambda e: jnp.minimum(e, 1)), (lambda e: jnp.maximum(e - 2, 0))
    specs = [
        pl.BlockSpec((3, PAIR, 1) + tile, lambda e, p: (0, 0, near(e), 0, 0, 0)),
        pl.BlockSpec((1, PAIR) + tile, lambda e, p: (near(e), 0, 0, 0, 0)),
        pl.BlockSpec((3, 1) + tile, lambda e, p: (0, far(e), 0, 0, 0)),
        pl.BlockSpec((1,) + tile, lambda e, p: (far(e), 0, 0, 0)),
    ]
    specs = (specs + specs[2:]) * CORES
    block = (1, own, width)
    matrix = lambda *shape: pl.BlockSpec((1,) + shape, lambda e, p: (e, 0, 0))
    return pl.pallas_call(
        experts_forward_kernel,
        grid_spec=pltpu.PrefetchScalarGridSpec(
            num_scalar_prefetch=1,
            grid=(count,),
            in_specs=[
                pl.BlockSpec((rows, width), lambda e, p: (0, 0)),
                pl.BlockSpec((1, rows, 1), lambda e, p: (e, 0, 0)),
            ]
            + specs,
            out_specs=[pl.BlockSpec(block, lambda e, p: (0, 0, 0))] * parts * batches
            + [matrix(width, units), matrix(width, units), matrix(units, width)],
            scratch_shapes=[pltpu.VMEM((rows, width), F32)],
        ),
        out_shape=[jax.ShapeDtypeStruct(block, LOW)] * parts * batches
        + [jax.ShapeDtypeStruct((count,) + shape, LOW) for shape in ((width, units), (width, units), (units, width))],
        compiler_params=params("arbitrary", mib=44),
        name="experts_forward",
    )(place, xn, share, *pieces)


def expert_specs(rows, width, units, batch):
    return [
        pl.BlockSpec((1, rows, 1), lambda e: (e, batch, 0)),
        pl.BlockSpec((1, width, units), lambda e: (e, 0, 0)),
        pl.BlockSpec((1, width, units), lambda e: (e, 0, 0)),
        pl.BlockSpec((1, units, width), lambda e: (e, 0, 0)),
    ]


def experts_turn_kernel(xn_ref, c_ref, share_ref, wg_ref, wu_ref, wd_ref, hidden_ref, to_up_ref, to_gate_ref, *refs):
    gate, up, share, sigma, silu = expert_hidden(xn_ref, share_ref, wg_ref, wu_ref)
    shared = silu * share
    hidden_ref[...] = (shared * up).astype(LOW)
    to_up = shared.astype(LOW)
    to_gate = (share * up * sigma * (1.0 + gate * (1.0 - sigma))).astype(LOW)
    to_up_ref[...] = to_up
    to_gate_ref[...] = to_gate
    grads = dot_nt(c_ref[...], wd_ref[0])
    gate_grad = (grads * to_gate.astype(F32)).astype(LOW)
    up_grad = (grads * to_up.astype(F32)).astype(LOW)
    accumulate(refs[-1], dot_nt(gate_grad, wg_ref[0]) + dot_nt(up_grad, wu_ref[0]))
    hand_out(refs[-1], refs[:-1])


def experts_turn(xn, c, share, wg, wu, wd, batch, own, parts):
    rows, width = xn.shape
    count, _, units = wg.shape
    kept = pl.BlockSpec((rows, units), lambda e: (0, e))
    block = (1, own, width)
    return pl.pallas_call(
        experts_turn_kernel,
        grid=(count,),
        in_specs=[
            pl.BlockSpec((rows, width), lambda e: (0, 0)),
            pl.BlockSpec((rows, width), lambda e: (batch, 0)),
        ]
        + expert_specs(rows, width, units, batch),
        out_specs=[kept] * 3 + [pl.BlockSpec(block, lambda e: (0, 0, 0))] * parts,
        out_shape=[jax.ShapeDtypeStruct((rows, units * count), LOW)] * 3 + [jax.ShapeDtypeStruct(block, LOW)] * parts,
        scratch_shapes=[pltpu.VMEM((rows, width), F32)],
        compiler_params=params("arbitrary", mib=56),
        name="experts_turn",
    )(xn, c, share, wg, wu, wd)


def experts_backward_kernel(batches, *refs):
    c_refs, up_refs, gate_refs = (refs[i * batches : (i + 1) * batches] for i in range(3))
    wg_ref, wu_ref, wd_ref, *out_refs = refs[3 * batches : -3]
    kept_ref, total_ref, c_ref = refs[-3:]

    @pl.when(pl.program_id(0) == 0)
    def _():
        c_ref[...] = jnp.concatenate([ref[...] for ref in c_refs], 0)

    hidden = dot_nt(c_ref[...], wd_ref[0])
    gate_grad = (hidden * jnp.concatenate([ref[...] for ref in gate_refs], 0).astype(F32)).astype(LOW)
    up_grad = (hidden * jnp.concatenate([ref[...] for ref in up_refs], 0).astype(F32)).astype(LOW)
    kept_ref[0] = gate_grad
    kept_ref[1] = up_grad
    accumulate(total_ref, dot_nt(gate_grad, wg_ref[0]) + dot_nt(up_grad, wu_ref[0]))
    hand_out(total_ref, out_refs)


def experts_backward(c, to_up, to_gate, wg, wu, wd, own, parts):
    batches = len(c)
    rows, width = c[0].shape
    count, _, units = wg.shape
    kept = pl.BlockSpec((rows, units), lambda e: (0, e))
    block = (batches, own, width)
    return pl.pallas_call(
        functools.partial(experts_backward_kernel, batches),
        grid=(count,),
        in_specs=[pl.BlockSpec((rows, width), lambda e: (0, 0))] * batches
        + [kept] * 2 * batches
        + [
            pl.BlockSpec((1, width, units), lambda e: (e, 0, 0)),
            pl.BlockSpec((1, width, units), lambda e: (e, 0, 0)),
            pl.BlockSpec((1, units, width), lambda e: (e, 0, 0)),
        ],
        out_specs=[pl.BlockSpec(block, lambda e: (0, 0, 0))] * parts
        + [pl.BlockSpec((2, batches * rows, units), lambda e: (0, 0, e))],
        out_shape=[jax.ShapeDtypeStruct(block, LOW)] * parts
        + [jax.ShapeDtypeStruct((2, batches * rows, units * count), LOW)],
        scratch_shapes=[pltpu.VMEM((batches * rows, width), F32), pltpu.VMEM((batches * rows, width), LOW)],
        compiler_params=params("arbitrary", mib=34),
        name="experts_backward",
    )(*c, *to_up, *to_gate, wg, wu, wd)


def head_grads(queries, key, value, douts, bias):
    probs = softmax_parts(queries, key, bias)
    dprobs = dot_nt(douts, value)
    centre = jnp.sum(probs * dprobs, -1, keepdims=True)
    dscores = (probs * (dprobs - centre) * 0.125).astype(LOW)
    return dot(dscores, key), dot_tn(dscores, queries), dot_tn(probs.astype(LOW), douts)


def stacked_heads(values, pair):
    return jnp.concatenate([head(values, pair * GROUP + j) for j in range(GROUP)], 0)


def chunk_grads(q, k, v, dout, bias):
    rows = q.shape[0]
    bias = jnp.concatenate([bias] * GROUP, 0)
    dqs, dks, dvs = [], [], []
    for pair in range(k.shape[1] // HEAD_SIZE):
        dquery, dkey, dvalue = head_grads(stacked_heads(q, pair), head(k, pair), head(v, pair), stacked_heads(dout, pair), bias)
        dqs += [dquery[j * rows : (j + 1) * rows] for j in range(GROUP)]
        dks.append(dkey)
        dvs.append(dvalue)
    return jnp.concatenate(dqs, -1), jnp.concatenate(dks, -1), jnp.concatenate(dvs, -1).astype(LOW)


def turned_back(grads, cos, sin):
    lanes = grads.shape[-1]
    return (grads * widen_table(cos, lanes) + swap_halves(grads * widen_table(sin, lanes))).astype(LOW)


def attend_backward_kernel(batches, parts, z_ref, *refs):
    q_refs, k_refs, v_refs = (refs[i * batches : (i + 1) * batches] for i in range(3))
    da_refs = refs[3 * batches : 3 * batches + parts]
    wo_ref, wq_ref, wk_ref, wv_ref, bias_ref, cos_ref, sin_ref, dqkv_ref, dn_ref = refs[3 * batches + parts :]

    def turn(q_ref, k_ref, v_ref):
        da = jnp.concatenate([ref[0] for ref in da_refs], 0)
        dout = dot_nt(da, wo_ref[...]).astype(LOW)
        dq, dk, dv = chunk_grads(q_ref[0], k_ref[0], v_ref[0], dout, bias_ref[0])
        dq, dk = turned_back(dq, cos_ref[...], sin_ref[...]), turned_back(dk, cos_ref[...], sin_ref[...])
        dqkv_ref[...] = jnp.concatenate([dq, dk, dv], -1)
        dn = dot_nt(dq, wq_ref[...]) + dot_nt(dk, wk_ref[...]) + dot_nt(dv, wv_ref[...])
        own = dn_ref.shape[2]
        for j in range(parts):
            dn_ref[lax.rem(z_ref[0] + parts - j, parts), 0] = dn[j * own : (j + 1) * own].astype(LOW)

    for b in range(batches):

        @pl.when(pl.program_id(0) == b)
        def _(b=b):
            turn(q_refs[b], k_refs[b], v_refs[b])


def attend_backward(z, qkv, da, wo, wq, wk, wv, bias, cos, sin, parts):
    batches, rows = len(qkv), qkv[0].shape[1]
    _, own, width = da[0].shape
    q_lanes, k_lanes = wo.shape[0] // parts, KEY_VALUE_HEADS * HEAD_SIZE // parts
    k_at = wo.shape[0] // k_lanes
    full = lambda *shape: pl.BlockSpec(shape, lambda b, z: (0,) * len(shape))
    batch = lambda *shape: pl.BlockSpec((1,) + shape, lambda b, z: (b, 0, 0))
    columns = lambda lanes: pl.BlockSpec((width, lanes), lambda b, z: (0, z[0]))
    return pl.pallas_call(
        functools.partial(attend_backward_kernel, batches, parts),
        grid_spec=pltpu.PrefetchScalarGridSpec(
            num_scalar_prefetch=1,
            grid=(batches,),
            in_specs=[pl.BlockSpec((1, rows, q_lanes), lambda b, z: (0, 0, z[0]))] * batches
            + [pl.BlockSpec((1, rows, k_lanes), lambda b, z: (0, 0, k_at + z[0]))] * batches
            + [pl.BlockSpec((1, rows, k_lanes), lambda b, z: (0, 0, k_at + parts + z[0]))] * batches
            + [batch(own, width)] * parts
            + [
                pl.BlockSpec((q_lanes, width), lambda b, z: (z[0], 0)),
                columns(q_lanes),
                columns(k_lanes),
                columns(k_lanes),
                batch(rows, rows),
                full(rows, cos.shape[1]),
                full(rows, cos.shape[1]),
            ],
            out_specs=[
                pl.BlockSpec((rows, q_lanes + 2 * k_lanes), lambda b, z: (b, 0)),
                pl.BlockSpec((parts, 1, own, width), lambda b, z: (0, b, 0, 0)),
            ],
        ),
        out_shape=[
            jax.ShapeDtypeStruct((batches * rows, q_lanes + 2 * k_lanes), LOW),
            jax.ShapeDtypeStruct((parts, batches, own, width), LOW),
        ],
        compiler_params=params("arbitrary", mib=56),
        name="attend_backward",
    )(z, *qkv, *qkv, *qkv, *da, wo, wq, wk, wv, bias, cos, sin)


def own_backward_kernel(q_ref, k_ref, v_ref, da_ref, wo_ref, bias_ref, cos_ref, sin_ref, dq_ref, *out_refs):
    batches, own, _ = q_ref.shape
    da = jnp.concatenate([da_ref[b] for b in range(batches)], 0)
    dout = dot_nt(da, wo_ref[...]).astype(LOW)
    lanes = k_ref.shape[-1]
    at = pl.multiple_of(pl.program_id(0) * lanes, lanes)
    middle = out_refs[0].shape[-1] // 2
    for b in range(batches):
        dq, dk, dv = chunk_grads(q_ref[b], k_ref[b], v_ref[b], dout[b * own : (b + 1) * own], bias_ref[b])
        dq_ref[b] = turned_back(dq, cos_ref[:own], sin_ref[:own])
        dk = turned_back(dk, cos_ref[...], sin_ref[...])
        for j, ref in enumerate(out_refs):
            ref[b, :, pl.ds(at, lanes)] = dk[j * own : (j + 1) * own]
            ref[b, :, pl.ds(middle + at, lanes)] = dv[j * own : (j + 1) * own]


def own_backward(qkv, da, wo, bias, cos, sin, parts):
    batches, own, width = da.shape
    rows = qkv.shape[1]
    k_lanes = KEY_VALUE_HEADS * HEAD_SIZE // parts
    q_lanes = k_lanes * GROUP
    k_at = parts * GROUP
    full = lambda *shape: pl.BlockSpec(shape, lambda c: (0,) * len(shape))
    block = (batches, own, 2 * k_lanes * parts)
    return pl.pallas_call(
        own_backward_kernel,
        grid=(parts,),
        in_specs=[
            pl.BlockSpec((batches, own, q_lanes), lambda c: (0, 0, c)),
            pl.BlockSpec((batches, rows, k_lanes), lambda c: (0, 0, k_at + c)),
            pl.BlockSpec((batches, rows, k_lanes), lambda c: (0, 0, k_at + parts + c)),
            full(batches, own, width),
            pl.BlockSpec((q_lanes, width), lambda c: (c, 0)),
            full(batches, own, rows),
            full(rows, cos.shape[1]),
            full(rows, cos.shape[1]),
        ],
        out_specs=[pl.BlockSpec((batches, own, q_lanes), lambda c: (0, 0, c))] + [full(*block)] * parts,
        out_shape=[jax.ShapeDtypeStruct((batches, own, q_lanes * parts), LOW)] + [jax.ShapeDtypeStruct(block, LOW)] * parts,
        compiler_params=params("arbitrary"),
        name="own_backward",
    )(qkv, qkv, qkv, da, wo, bias, cos, sin)


def chip_block(place_ref, x, y, core):
    ring = lax.rem(place_ref[0] + x, RING)
    pair = lax.rem(place_ref[1] + y, PAIR)
    return (ring * PAIR + pair) * CORES + lax.rem(place_ref[2] + core, CORES)


def expert_grad_kernel(cut, batches, place_ref, *refs):
    left_refs, right_refs = refs[:batches], refs[batches:-3]
    mine_ref, other_ref, turned_ref = refs[-3:]
    tokens = left_refs[0].shape[0]
    rows = mine_ref.shape[-2] // cut
    lanes = mine_ref.shape[-1]
    step = pl.program_id(1)
    if cut == 1:

        @pl.when((pl.program_id(0) == 0) & (step == 0))
        def _():
            for i, ref in enumerate(left_refs):
                turned_ref[:, i * tokens : (i + 1) * tokens] = ref[...].T

        product = dot(turned_ref[...], right_refs[0][0]).astype(LOW)
    else:
        products = [dot_tn(left[...], right[0]) for left, right in zip(left_refs, right_refs)]
        product = sum(products[1:], products[0]).astype(LOW)
    half = lax.rem(step, 2)

    def place(refs, ring_first):
        for i in range(RING):
            x = lax.rem(i + RING - place_ref[0], RING)
            for j in range(PAIR):
                y = lax.rem(j + PAIR - place_ref[1], PAIR)
                index = (x * 2 + half) * PAIR + y if ring_first else (y * RING + x) * 2 + half
                for core in range(CORES):
                    at = ((i * PAIR + j) * CORES + core) * rows
                    for part in range(cut):
                        value = product[at : at + rows, part * lanes : (part + 1) * lanes]
                        refs[core][0, 0, index, part * rows : (part + 1) * rows] = value

    for core in range(CORES):
        for ring_first in (True, False):

            @pl.when((place_ref[2] == core) & ((step < 2) == ring_first))
            def _(core=core, ring_first=ring_first):
                place((mine_ref, other_ref) if core == 0 else (other_ref, mine_ref), ring_first)


def expert_grad(place, lefts, rights, count, cut):
    number, right_rows, right_lanes = rights[0].shape
    rows, left_lanes = lefts[0].shape
    if cut > 1:
        left_lanes = left_lanes // count
    else:
        right_lanes = right_lanes // count
    owners = RING * PAIR * CORES
    high, lanes = left_lanes // owners, right_lanes // cut
    shape = (2, owners, high * cut, lanes)
    out = pl.BlockSpec((1, 1) + shape[1:], lambda r, e, p: (r, e // 2, 0, 0, 0))
    left_spec = pl.BlockSpec((rows, left_lanes), lambda r, e, p: (0, e if cut > 1 else 0))
    right_spec = pl.BlockSpec((1, right_rows, right_lanes), lambda r, e, p: (r, 0, 0 if cut > 1 else e))
    batches = len(lefts)
    return pl.pallas_call(
        functools.partial(expert_grad_kernel, cut, batches),
        grid_spec=pltpu.PrefetchScalarGridSpec(
            num_scalar_prefetch=1,
            grid=(number, count),
            in_specs=[left_spec] * batches + [right_spec] * len(rights),
            out_specs=[out, out],
            scratch_shapes=[pltpu.VMEM((left_lanes, rows * batches) if cut == 1 else (16, 128), LOW)],
        ),
        out_shape=[jax.ShapeDtypeStruct((number,) + shape, LOW)] * 2,
        compiler_params=params("arbitrary", "arbitrary"),
        name="expert_grad",
    )(place, *lefts, *rights)


def chip_sum_kernel(ring_first, mine_inner, other_inner, mine_outer, other_outer, *refs):
    matrix = pl.program_id(0)
    keep, *away = refs
    places = [(keep, 0), (keep, 1), (keep, 2), (away[0], 0), (away[0], 1), (away[1], 0), (away[1], 1), (keep, 3)]

    def add(mine, other):
        for index in range(2 * RING * PAIR):
            value = mine[0, 0, index] + other[0, 0, index]
            if ring_first:
                ref, at = places[index // PAIR]
                ref[at, index % PAIR, 0] = value
            elif index < 2 * RING:
                keep[index, 0] = value
            else:
                away[index // RING - 2][index % RING, 0] = value

    @pl.when(matrix < 2)
    def _():
        add(mine_inner, other_inner)

    @pl.when(matrix == 2)
    def _():
        add(mine_outer, other_outer)


def chip_sum(inner, outer, ring_first):
    tile = inner[0].shape[3:]
    kind = 0 if ring_first else 1
    block = (1, 1, 2 * RING * PAIR) + tile
    inner_spec = pl.BlockSpec(block, lambda m: (jnp.minimum(m, 1), kind, 0, 0, 0))
    outer_spec = pl.BlockSpec(block, lambda m: (0, kind, 0, 0, 0))
    shapes = [(4, PAIR), (2, PAIR), (2, PAIR)] if ring_first else [(2 * RING,), (RING,), (RING,)]
    return pl.pallas_call(
        functools.partial(chip_sum_kernel, ring_first),
        grid=(3,),
        in_specs=[inner_spec, inner_spec, outer_spec, outer_spec],
        out_specs=[pl.BlockSpec(shape + (1,) + tile, lambda m, n=len(shape): (0,) * n + (m, 0, 0)) for shape in shapes],
        out_shape=[jax.ShapeDtypeStruct(shape + (3,) + tile, LOW) for shape in shapes],
        compiler_params=params("arbitrary", mib=56),
        name="chip_sum",
    )(*inner, *outer)


def dense_grad_kernel(batches, parts, place_ref, z_ref, *refs):
    del z_ref
    mixed_refs, xn_refs, da_refs = refs[:batches], refs[batches : 2 * batches], refs[2 * batches : 2 * batches + parts]
    dqkv_ref, mine_ref, other_ref, into_ref, out_of_ref = refs[2 * batches + parts :]
    rows = xn_refs[0].shape[0]
    high = mine_ref.shape[-2]
    lanes, wide = out_of_ref.shape[-1], dqkv_ref.shape[1]
    into = sum(dot_tn(ref[...], dqkv_ref[b * rows : (b + 1) * rows]) for b, ref in enumerate(xn_refs)).astype(LOW)
    da = [jnp.concatenate([ref[b] for ref in da_refs], 0) for b in range(batches)]
    out_of = sum(dot_tn(ref[...], da[b]) for b, ref in enumerate(mixed_refs)).astype(LOW)
    for chip in range(RING * PAIR):
        for core in range(CORES):
            owner = chip * CORES + core
            for half in range(2):
                at = (owner * 2 + half) * high
                into_ref[owner, half] = into[at : at + high]
                at = (half * CORES + core) * lanes
                out_of_ref[owner, half] = out_of[chip * high : (chip + 1) * high, at : at + lanes]
    for core, ref in enumerate((mine_ref, other_ref)):
        for x in range(RING):
            for y in range(PAIR):
                owner = chip_block(place_ref, x, y, core)
                for half in range(2):
                    ref[x * 2 + half, y, :, :wide] = into_ref[owner, half]
                    ref[x * 2 + half, y, :, wide:] = out_of_ref[owner, half]


def dense_grad(place, z, mixed, da, xn, dqkv, parts):
    batches = len(xn)
    rows, width = xn[0].shape
    owners = RING * PAIR * CORES
    q_lanes, wide = mixed[0].shape[1] // parts, dqkv.shape[1]
    high, lanes = width // owners // 2, width // CORES // 2
    shape = (2 * RING, PAIR, high, wide + lanes)
    whole = lambda *shape: pl.BlockSpec(shape, lambda i, p, z: (0,) * len(shape))
    return pl.pallas_call(
        functools.partial(dense_grad_kernel, batches, parts),
        grid_spec=pltpu.PrefetchScalarGridSpec(
            num_scalar_prefetch=2,
            grid=(1,),
            in_specs=[pl.BlockSpec((rows, q_lanes), lambda i, p, z: (0, z[0]))] * batches
            + [whole(rows, width)] * batches
            + [whole(*da[0].shape)] * parts
            + [whole(*dqkv.shape)],
            out_specs=[pl.BlockSpec(shape, lambda i, p, z: (0,) * 4)] * 2,
            scratch_shapes=[pltpu.VMEM((owners, 2, high, wide), LOW), pltpu.VMEM((owners, 2, high, lanes), LOW)],
        ),
        out_shape=[jax.ShapeDtypeStruct(shape, LOW)] * 2,
        compiler_params=params("arbitrary", mib=56),
        name="dense_grad",
    )(place, z, *mixed, *xn, *da, dqkv)


def dense_layout_kernel(by_x, place_ref, z_ref, mine_ref, other_ref, *refs):
    outs = refs[-4:]
    parts = mine_ref.shape[2] if by_x else mine_ref.shape[0]
    for core, ref in enumerate((mine_ref, other_ref)):
        to_core = lax.rem(place_ref[2] + core, CORES)
        for y in range(PAIR):
            to_y = lax.rem(place_ref[1] + y, PAIR)
            for k in range(parts):
                at = lax.rem(z_ref[0] + parts - k, parts)
                start = 0
                for out in outs:
                    to_rows = out is outs[3]
                    lanes = out.shape[-1] // (CORES if to_rows else parts)
                    index = (0, y, k) if by_x else (k, y, 0)
                    value = ref[index + (slice(None), slice(start, start + lanes))].astype(F32)
                    if to_rows:
                        out[at, 0, to_y, :, pl.ds(pl.multiple_of(to_core * lanes, 128), lanes)] = value
                    else:
                        out[0, to_y, to_core, 0, :, pl.ds(pl.multiple_of(at * lanes, 128), lanes)] = value
                    start += lanes


def dense_layout(place, z, half, mine, other, shapes, before):
    by_x = half == 0
    high, lanes = mine.shape[-2:]
    parts = mine.shape[2] if by_x else mine.shape[0]
    if by_x:
        source = pl.BlockSpec((1, PAIR, parts, high, lanes), lambda x, p, z: (x, 0, 0, 0, 0))
    else:
        source = pl.BlockSpec((parts, PAIR, 1, high, lanes), lambda x, p, z: (0, 0, x, 0, 0))
    ring = lambda x, p: lax.rem(p[0] + RING - x, RING)
    width = shapes[3][1]
    shapes = [(RING, PAIR, CORES, 2, high, shape[1]) for shape in shapes[:3]] + [(parts, RING, PAIR, high, width)]
    out_specs = [
        pl.BlockSpec((1, PAIR, CORES, 1, high, shape[-1]), lambda x, p, z: (ring(x, p), 0, 0, half, 0, 0)) for shape in shapes[:3]
    ] + [pl.BlockSpec((parts, 1, PAIR, high, width // 2), lambda x, p, z: (0, ring(x, p), 0, 0, half))]
    return pl.pallas_call(
        functools.partial(dense_layout_kernel, by_x),
        grid_spec=pltpu.PrefetchScalarGridSpec(
            num_scalar_prefetch=2,
            grid=(RING,),
            in_specs=[source, source] + [pl.BlockSpec(memory_space=pl.ANY)] * len(before),
            out_specs=out_specs,
        ),
        out_shape=[jax.ShapeDtypeStruct(shape, F32) for shape in shapes],
        input_output_aliases={4 + i: i for i in range(len(before))},
        compiler_params=params("arbitrary"),
        cost_estimate=pl.CostEstimate(flops=0, bytes_accessed=24 * mine.size, transcendentals=0),
        name="dense_layout",
    )(place, z, mine, other, *before)


def norm_back(grad_normed, values, gain):
    scale = lax.rsqrt(jnp.mean(values * values, -1, keepdims=True) + EPS)
    scaled = grad_normed * gain
    gain_grad = jnp.sum(grad_normed * values * scale, (0, 1))
    inner = jnp.mean(scaled * values, -1, keepdims=True)
    return (scale * scaled - values * scale * scale * scale * inner, gain_grad)


def local(
    block_input, segments, expert_ids, route_weights, attn_gain, w_query, key_projection_weight,
    value_projection_weight, w_out, ffn_gain, w_gate, w_up, w_down, out_grad,
):
    parts = lax.axis_size("expert")
    section = lax.axis_index("section")
    z = lax.axis_index("expert")
    z_at = z.reshape(1)
    dp = lax.axis_index("dp")
    dp_place = jnp.stack([dp // (PAIR * CORES), dp // CORES % PAIR, dp % CORES])
    batches, own, width = block_input.shape
    rows = parts * own
    wq, wk, wv, wo = w_query[0], key_projection_weight[0], value_projection_weight[0], w_out[0]
    local_experts, units = w_gate.shape[1], w_gate.shape[3]

    outer = w_down[0].reshape(local_experts, -1, width // units, units)
    outer = jnp.swapaxes(outer, 1, 2).reshape(w_gate[0].shape)
    shard = jnp.stack([w_gate[0], w_up[0], outer], 1)
    near, far = shard[:2], shard[2:]
    numbers = jnp.arange(parts * local_experts, dtype=jnp.int32)
    hits = expert_ids[0][..., None] == numbers
    shares = jnp.sum(jnp.where(hits, route_weights[0][..., None], 0.0), 2)
    shares = jnp.concatenate([shares, segments.astype(F32)[..., None]], -1)
    start = spread_group(block_input)
    near_y = moved(near, y=1)
    far_1 = ring_gather_step(far)
    shares = spread_group(shares)
    start, near_y, far_1, shares = hold(start, near_y, far_1, shares)

    start = jnp.concatenate(start, 1)
    shares = jnp.concatenate(shares, 1)
    labels = shares[..., -1]
    shares = shares[..., :-1].reshape(batches * rows, parts, local_experts)
    share = lax.dynamic_index_in_dim(shares, z, 1, keepdims=False).T[..., None]
    block = jnp.arange(parts, dtype=jnp.int32)[:, None]
    place = ((z - block) % parts * own + jnp.arange(own, dtype=jnp.int32)[None, :]).reshape(rows)
    allowed = (place[None, None, :] <= place[None, :, None]) & (labels[:, None, :] == labels[:, :, None])
    bias = jnp.where(allowed, 0.0, -1e30).astype(F32)
    half = HEAD_SIZE // 2
    frequency = 10000.0 ** (-jnp.arange(half, dtype=F32) * 2.0 / HEAD_SIZE)
    angles = place.astype(F32)[:, None] * frequency[None, :]
    cos_half, sin_half = jnp.cos(angles), jnp.sin(angles)
    cos = jnp.concatenate([cos_half] * 4, -1)
    sin = jnp.concatenate([-sin_half, sin_half] * 2, -1)
    cos_all, sin_all = jnp.concatenate([cos] * batches, 0), jnp.concatenate([sin] * batches, 0)

    def attention_in(x, cos, sin):
        qkv, xn = project(x.reshape(-1, width), attn_gain, wq, wk, wv, cos, sin)
        return qkv.reshape(-1, rows, qkv.shape[1]), xn

    def attention_out(qkv, bias, x):
        mixed = attend(qkv, bias, parts)
        h1, xn2 = join(mixed, x, wo, ffn_gain, own)
        return mixed.reshape(-1, wo.shape[0]), h1, xn2.reshape(-1, width)

    near = jnp.stack([near, near_y])
    near_1 = ring_gather_step(near)
    far_2 = ring_gather_next(far_1)
    far_a = jnp.stack([far, *far_1])
    far_ya = moved(far_a, y=1)
    qkv, _ = attention_in(start, cos_all, sin_all)
    _, h1, xn2 = attention_out(qkv, bias, start)

    xn2, near_1, far_2, far_ya = hold(xn2, near_1, far_2, far_ya)
    near_b = moved(near_1[0][:, 0], x=1), moved(near_1[1][:, 1], x=-1)
    far_b = jnp.stack(far_2)
    far_yb = moved(far_b, y=1)
    near_a = jnp.stack([near, *near_1])
    others = [moved(piece, core=1) for piece in (near_a, far_a)]

    near_b, far_yb, others = hold(near_b, far_yb, others)
    near_b = jnp.stack(near_b)
    pieces = [near_a, near_b, far_a, far_b, far_ya, far_yb]
    pieces += [others[0], moved(near_b, core=1), others[1], *[moved(piece, core=1) for piece in (far_b, far_ya, far_yb)]]
    *blocks, wg, wu, wd = experts_forward(dp_place, xn2, share, pieces, batches, own, parts)
    blocks = [blocks[b * parts : (b + 1) * parts] for b in range(batches)]
    c_second = lax.all_gather(out_grad, "expert")
    c_second = jnp.concatenate([lax.dynamic_index_in_dim(c_second, (z + parts - j) % parts, 0, False) for j in range(parts)], 1)
    flat_second = c_second.reshape(batches * rows, width)
    received = []
    result = None
    for b in range(batches):
        came = owners_step(blocks[b])
        if b > 0:
            came = once(came, result)
        result = (h1[b : b + 1] + added(*came)).astype(LOW)
        received.append(spread_group(across(result)))

    biases = [bias[b : b + 1] for b in range(batches)]
    x, qkv, xn, mixed, h1, xn2, hidden, to_up, to_gate, blocks = ([None] * batches for _ in range(10))
    for b in range(batches):
        if b > 0:
            received[b] = once(received[b], hidden[b - 1])
        x[b] = jnp.where(section == 0, start[b : b + 1], jnp.concatenate(received[b], 1))
        qkv[b], xn[b] = attention_in(x[b], cos, sin)
        mixed[b], h1[b], xn2[b] = attention_out(qkv[b], biases[b], x[b])
        hidden[b], to_up[b], to_gate[b], *blocks[b] = experts_turn(xn2[b], flat_second, share, wg, wu, wd, b, own, parts)
    x_own = jnp.concatenate([rows_of[:, :own] for rows_of in x], 0).astype(F32)

    after, dq, kv_came = ([None] * batches for _ in range(3))
    for b in range(batches):
        came = owners_step(blocks[b])
        if b > 0:
            came = once(came, dq[b - 1])
        after[b] = out_grad[b : b + 1].astype(F32) + norm_back(added(*came), h1[b], ffn_gain)[0]
        dq[b], *kv_blocks = own_backward(qkv[b], after[b].astype(LOW), wo, biases[b], cos, sin, parts)
        kv_came[b] = owners_step(kv_blocks)
    kv_came[0] = once(kv_came[0], dq[-1])
    received_own = []
    for b in range(batches):
        if b > 0:
            kv_came[b] = once(kv_came[b], input_grad)
        dkv = added(*kv_came[b]).astype(LOW).reshape(own, -1)
        dn_own = dot_nt(dq[b].reshape(own, -1), wq)
        dn_own = dn_own + dot_nt(dkv[:, : wk.shape[1]], wk) + dot_nt(dkv[:, wk.shape[1] :], wv)
        input_grad = after[b] + norm_back(dn_own[None], x_own[b : b + 1], attn_gain)[0]
        received_own.append(across(input_grad.astype(LOW)))

    c_own = jnp.where(section == 1, out_grad, jnp.concatenate(received_own, 0))
    c = [jnp.where(section == 1, c_second[b : b + 1], gather_group(received_own[b])).reshape(rows, width) for b in range(batches)]
    *blocks, hidden_grads = experts_backward(c, to_up, to_gate, wg, wu, wd, own, parts)
    norm_part, ffn_grad = norm_back(added(*owners_step(blocks)), jnp.concatenate(h1, 0), ffn_gain)
    after = c_own.astype(F32) + norm_part
    both = [
        expert_grad(dp_place, xn2, [hidden_grads], local_experts, 1),
        expert_grad(dp_place, hidden, [block[None] for block in c], local_experts, width // units),
    ]
    after, both = hold(after, both)
    inner, outer = [(mine, moved(other, core=1)) for mine, other in both]
    da = spread_group(after.astype(LOW))
    outputs = [dot(units_of, wd.reshape(local_experts * units, width)).astype(LOW) for units_of in once(hidden, inner[1])]
    outputs = jnp.stack(outputs).reshape(batches, parts, own, width)
    outputs = jnp.stack([lax.dynamic_index_in_dim(outputs, (z + parts - i) % parts, 1, False) for i in range(parts)])
    outer, outputs = hold(outer, outputs)
    keep_ring, to_above, to_below = chip_sum(inner, outer, True)
    keep_pair, *to_pair = chip_sum(once(inner, to_above), outer, False)
    da, to_pair = hold(da, to_pair)

    ring_1 = moved(to_above, x=1), moved(to_below, x=-1)
    pair_1 = [moved(block, y=1) for block in to_pair]
    dqkv, dn = attend_backward(z_at, qkv, da, wo, wq, wk, wv, bias, cos, sin, parts)
    mine, other = dense_grad(dp_place, z_at, mixed, da, xn, dqkv, parts)
    dn_own = lax.psum_scatter(dn, "expert", scatter_dimension=0, tiled=True)[0].astype(F32)
    mine, other, ring_1, pair_1[0] = hold(mine, other, ring_1, pair_1[0])
    dense = added(mine, moved(other, core=1)).astype(LOW)

    (dense,) = hold(dense)
    dense_1 = ring_step(dense)

    dense_1, outputs, dn_own, ring_1 = hold(dense_1, outputs, dn_own, ring_1)
    outputs = lax.psum_scatter(outputs, "expert", scatter_dimension=0, tiled=True)[0]
    dense_2 = ring_next((dense[2], dense[7]), dense_1)
    norm_part, attn_grad = norm_back(dn_own, x_own, attn_gain)
    input_grad = after + norm_part
    gains = jnp.stack([attn_grad, ffn_grad])
    gains = gains + exchanged(gains, "expert", 1)
    ring_2 = ring_next((keep_ring[2], keep_ring[3]), ring_1)

    dense_2, gains, pair_1 = hold(dense_2, gains, pair_1)
    dense = ring_end(dense, dense_1, dense_2)
    dense_3 = moved(dense[:, 1].astype(LOW), y=1)
    pair_sums = added(keep_pair, jnp.concatenate(pair_1, 0)).astype(LOW)
    pair_2 = ring_step(pair_sums)
    gains = gains + exchanged(gains, "expert", 2)

    dense_3, gains, ring_2, pair_2 = hold(dense_3, gains, ring_2, pair_2)
    ring_sums = ring_end(keep_ring, ring_1, ring_2)
    first, second = (added(dense[half, 0], dense_3[half]).astype(LOW) for half in range(2))
    first_1 = [shifted(first, k) for k in range(1, parts)]
    second_1 = [moved(second, x=k) for k in range(1, RING)]

    first_1, second_1 = hold(first_1, second_1)
    first = jnp.stack([first] + first_1)
    first_2 = moved(first, y=1)
    second = jnp.stack([second] + second_1)
    second_2 = moved(second, y=1)
    pair_3 = ring_next((pair_sums[2], pair_sums[7]), pair_2)
    gains = gains + exchanged(gains, "dp", 1)

    first_2, second_2, gains, pair_3 = hold(first_2, second_2, gains, pair_3)
    first = jnp.stack([first, first_2])
    first_3 = moved(first, x=1), moved(first, x=-1)
    second = jnp.stack([second, second_2])
    second_3 = shifted(second, 1), shifted(second, parts - 1)
    ring_away = moved(ring_sums[:, 1].astype(LOW), y=1)

    first_3, second_3, ring_away, gains = hold(first_3, second_3, ring_away, gains)
    first_4, second_4 = moved(first, x=2), shifted(second, 2)
    gains = gains + exchanged(gains, "dp", 2)
    ring_sums = added(ring_sums[:, 0], ring_away)
    pair_sums = ring_end(pair_sums, pair_2, pair_3)
    w_gate_grad, w_up_grad, w_down_grad = (jnp.concatenate([ring_sums[:, i], pair_sums[:, i]], 0) for i in range(3))
    w_down_grad = w_down_grad.reshape(local_experts, width // units, -1, units)
    w_down_grad = jnp.swapaxes(w_down_grad, 1, 2).reshape(local_experts, -1, width)

    first_4, second_4, w_gate_grad, w_up_grad, w_down_grad, gains, outputs = hold(
        first_4, second_4, w_gate_grad, w_up_grad, w_down_grad, gains, outputs
    )
    first = jnp.stack([first, first_3[0], first_4, first_3[1]])
    first_other = moved(first, core=1)
    gains = gains + exchanged(gains, "dp", 4)

    second = jnp.stack([second, second_3[0], second_4, second_3[1]])
    second, first_other, gains = hold(second, first_other, gains)
    second_other = moved(second, core=1)
    shapes = (wq.shape, wk.shape, wv.shape, wo.shape)
    laid = dense_layout(dp_place, z_at, 0, first, first_other, shapes, ())
    gains = gains + exchanged(gains, "dp", 8)

    second_other, laid = hold(second_other, laid)
    laid = dense_layout(dp_place, z_at, 1, second, second_other, shapes, laid)
    w_query_grad, w_key_grad, w_value_grad, w_out_grad = (
        grad.reshape(weight.shape) for grad, weight in zip(laid, (wq, wk, wv, wo))
    )

    layer_outputs = (jnp.concatenate(h1, 0) + outputs.astype(F32)).astype(LOW)
    return (
        layer_outputs[None],
        input_grad[None],
        gains[0:1],
        w_query_grad[None],
        w_key_grad[None],
        w_value_grad[None],
        w_out_grad[None],
        gains[1:2],
        w_gate_grad[None],
        w_up_grad[None],
        w_down_grad[None],
    )


def solution(mesh):
    tokens = P(None, ("dp", "expert"), None)
    layered = P("section", None, ("dp", "expert"), None)
    vector = P("section", None)
    matrix = P("section", None, None)
    expert = P("section", "expert", "dp", None)
    return jax.shard_map(
        local,
        mesh=mesh,
        in_specs=(
            tokens, P(None, ("dp", "expert")), layered, layered, vector, matrix, matrix, matrix, matrix,
            vector, expert, expert, expert, tokens,
        ),
        out_specs=(layered, layered, vector, matrix, matrix, matrix, matrix, vector, expert, expert, expert),
        check_vma=False,
    )
```
